32 devices in a mesh: tile: 8 (over z, core), scan: 4 (over y, x).
Axes of the slice: x: 2, y: 2, z: 4, core: 2. Of those that a mesh axis runs over, the one named last changes fastest.
Arguments:
- consensus: float32 [8, 2, 256, 256], P('tile'), may hold values from -4 to 4
- duals: float32 [4, 8, 2, 256, 256], P('scan', 'tile'), may hold values from -3 to 3
- probes: float32 [4, 2, 256, 256], P('scan'), may hold values from -4 to 4
- amplitudes: bfloat16 [4, 8, 4, 256, 256], P('scan', 'tile'), may hold values from 0.19921875 to 2
- offsets: int32 [4, 8, 4, 2], P('scan', 'tile'), may hold values from 0 to 128
- counts: int32 [4, 8], P('scan', 'tile'), may hold values from 1 to 4, as said below
Outputs:
- consensus_new: float32 [8, 2, 256, 256], P('tile')
- duals_new: float32 [4, 8, 2, 256, 256], P('scan', 'tile')
- probes_new: float32 [4, 2, 256, 256], P('scan')
The draws below stay inside these ranges and needn't reach their ends.
Inputs may be any that keep to these rules, and one draw needn't show every extreme that they name: counts: some group has 4 scan positions in some tile; slots at or past the count are unused. offsets: first the row, then the column.
All inputs are finite; a program needn't handle non-finite values.
Results may differ from the reference program's by a relative error of at most 0.015.
Values may be sent and summed in bfloat16 or wider, within the bound.
No kernel may reach another device: no remote copies, remote signals or barrier semaphores. Data moves between devices by JAX's collectives and lax.ppermute only.
A program may use at most 64 MiB of HBM per device.

```python
import math
import jax
import jax.numpy as jnp
from jax import lax

PS = 256
TS = 256
OVER = 128
TGW = 4
SLOTS = 4
INNER = 2
GROUPS = 4
TILES = 8


def draw_counts(key, part):
    levels = jax.random.randint(key, (GROUPS, TILES), 0, 4)
    result = jnp.where(levels == 0, SLOTS, 1).astype(jnp.int32)
    return result.at[0, 0].set(SLOTS)


def with_ends(entries, rng, smallest, largest):
    place = [jax.random.randint(jax.random.fold_in(rng, axis), (), 0, length) for axis, length in enumerate(entries.shape)]
    widest = entries.shape.index(max(entries.shape))
    neighbour = place[:widest] + [(place[widest] + 1) % entries.shape[widest]] + place[widest + 1:]
    return entries.at[tuple(place)].set(smallest).at[tuple(neighbour)].set(largest)


def level_of(stream_key, shape, split, low, high):
    def one(position, parts):
        heights = jax.random.uniform(jax.random.fold_in(jax.random.fold_in(stream_key, 6), position), (parts,), jnp.float32, low / len(split), high / len(split))
        return jnp.repeat(jnp.exp(heights), shape[position] // parts).reshape((-1,) + (1,) * (len(shape) - position - 1))

    gain = one(*split[0])
    for cut in split[1:]:
        gain = gain * one(*cut)
    return gain


def gaussian(key, dims, scale, bound, split=(), held_as=jnp.bfloat16):
    loudness = level_of(key, dims, split, -0.22, 0.18) if split else 1.0
    values = jax.random.normal(key, dims, jnp.float32) * scale * loudness
    return jnp.minimum(jnp.maximum(values, -bound), bound).astype(held_as)


def setup_inputs(seed: int = 0) -> dict:
    key_of = jax.random.split(jax.random.key(seed), 7)
    consensus = gaussian(key_of[0], (TILES, 2, TS, TS), 0.6, 4.0, ((0, 8),), jnp.float32)
    duals = gaussian(key_of[1], (GROUPS, TILES, 2, TS, TS), 0.3, 3.0, ((0, 4), (1, 8)), jnp.float32)
    probes = gaussian(key_of[2], (GROUPS, 2, PS, PS), 0.7, 4.0, ((0, 4),), jnp.float32)
    amplitudes = jnp.clip(0.19921875 + 1.8007812 * jax.random.uniform(key_of[3], (GROUPS, TILES, SLOTS, PS, PS), jnp.float32) ** level_of(key_of[3], (GROUPS, TILES, SLOTS, PS, PS), ((0, 4), (1, 8)), -0.2, 0.2), 0.19921875, 2.0).astype(jnp.bfloat16)
    offsets = with_ends(jax.random.randint(key_of[4], (GROUPS, TILES, SLOTS, 2), 0, TS - PS + OVER + 1), jax.random.fold_in(key_of[4], 1), 0, TS - PS + OVER).astype(jnp.int32)
    counts = draw_counts(jax.random.fold_in(key_of[6], 71), 0)
    return {"consensus": consensus, "duals": duals, "probes": probes, "amplitudes": amplitudes, "offsets": offsets, "counts": counts}


penalty = 0.5
smoothing = 0.05
probe_step = 3.0

def dft_tables(length):
    indices = jnp.arange(length, dtype=jnp.int32)
    phase_index = indices[:, None] * indices[None, :] % length
    angles = phase_index.astype(jnp.float32) * (2.0 * math.pi / length)
    norm_scale = 1.0 / math.sqrt(length)
    real_part = (jnp.cos(angles) * norm_scale).astype(jnp.bfloat16)
    imag_part = (-jnp.sin(angles) * norm_scale).astype(jnp.bfloat16)
    return (real_part, imag_part)

def forward_wave(wave_real, wave_imag, stacked, spread, length):
    section_one = jnp.dot(stacked, jnp.concatenate([wave_real, wave_imag], 1), preferred_element_type=jnp.float32)
    inner_real = (section_one[:length, :length] - section_one[length:, length:]).astype(jnp.bfloat16)
    inner_imag = (section_one[:length, length:] + section_one[length:, :length]).astype(jnp.bfloat16)
    section_two = jnp.dot(jnp.concatenate([inner_real, inner_imag], 0), spread, preferred_element_type=jnp.float32)
    return (section_two[:length, :length] - section_two[length:, length:], section_two[:length, length:] + section_two[length:, :length])

def inverse_wave(wave_real, wave_imag, stacked, spread, length):
    section_one = jnp.dot(stacked, jnp.concatenate([wave_real, wave_imag], 1), preferred_element_type=jnp.float32)
    inner_real = (section_one[:length, :length] + section_one[length:, length:]).astype(jnp.bfloat16)
    inner_imag = (section_one[:length, length:] - section_one[length:, :length]).astype(jnp.bfloat16)
    section_two = jnp.dot(jnp.concatenate([inner_real, inner_imag], 0), spread, preferred_element_type=jnp.float32)
    return (section_two[:length, :length] + section_two[length:, length:], section_two[length:, :length] - section_two[:length, length:])

def patch_terms(window, probe_field, measured, stacked, spread):
    length = window.shape[1]
    object_real = window[0].astype(jnp.float32)
    object_imag = window[1].astype(jnp.float32)
    probe_real = probe_field[0]
    probe_imag = probe_field[1]
    exit_real = (probe_real * object_real - probe_imag * object_imag).astype(jnp.bfloat16)
    exit_imag = (probe_real * object_imag + probe_imag * object_real).astype(jnp.bfloat16)
    wave_real, wave_imag = forward_wave(exit_real, exit_imag, stacked, spread, length)
    modulus = jnp.sqrt(wave_real * wave_real + wave_imag * wave_imag + smoothing)
    factor = measured.astype(jnp.float32) / modulus - 1.0
    resid_real = (wave_real * factor).astype(jnp.bfloat16)
    resid_imag = (wave_imag * factor).astype(jnp.bfloat16)
    back_real, back_imag = inverse_wave(resid_real, resid_imag, stacked, spread, length)
    object_terms = jnp.stack([probe_real * back_real + probe_imag * back_imag, probe_real * back_imag - probe_imag * back_real, probe_real * probe_real + probe_imag * probe_imag])
    probe_terms = jnp.stack([object_real * back_real + object_imag * back_imag, object_real * back_imag - object_imag * back_real, object_real * object_real + object_imag * object_imag])
    return (object_terms, probe_terms)

def to_grid(blocks):
    tile_rows = TILES // TGW
    channels = blocks.shape[1]
    return blocks.reshape(tile_rows, TGW, channels, TS, TS).transpose(2, 0, 3, 1, 4).reshape(channels, tile_rows * TS, TGW * TS)

def to_tiles(grid):
    tile_rows = TILES // TGW
    channels = grid.shape[0]
    return grid.reshape(channels, tile_rows, TS, TGW, TS).transpose(1, 3, 0, 2, 4).reshape(tile_rows * TGW, channels, TS, TS)

def reference(consensus, duals, probes, amplitudes, offsets, counts):
    tile_rows = TILES // TGW
    height = tile_rows * TS
    width = TGW * TS
    span = TS + OVER
    real_part, imag_part = dft_tables(PS)
    stacked = jnp.concatenate([real_part, imag_part], 0)
    spread = jnp.concatenate([real_part, imag_part], 1)
    tile_ids = jnp.arange(TILES, dtype=jnp.int32)
    row_base = (tile_ids // TGW * TS).astype(jnp.int32)
    col_base = (tile_ids % TGW * TS).astype(jnp.int32)
    zero_index = jnp.zeros((), jnp.int32)
    grid_consensus = to_grid(consensus)

    def solve_group(operands):
        dual_tiles, probe_field, measured, corners, slot_counts = operands
        grid_dual = to_grid(dual_tiles)
        estimate = grid_consensus
        probe_sum = jnp.zeros((3, PS, PS), jnp.float32)
        for sweep_index in range(INNER):
            padded = jnp.pad(estimate.astype(jnp.bfloat16), ((0, 0), (0, OVER), (0, OVER)))

            def visit_tile(carried, tile_index):
                totals, probe_acc = carried
                row_start = row_base[tile_index]
                col_start = col_base[tile_index]
                extended = lax.dynamic_slice(padded, (zero_index, row_start, col_start), (2, span, span))

                def visit_slot(slot_index, inner_state):
                    local_totals, local_probe = inner_state
                    top_row = corners[tile_index, slot_index, 0].astype(jnp.int32)
                    left_col = corners[tile_index, slot_index, 1].astype(jnp.int32)
                    window = lax.dynamic_slice(extended, (zero_index, top_row, left_col), (2, PS, PS))
                    object_terms, probe_terms = patch_terms(window, probe_field, measured[tile_index, slot_index], stacked, spread)
                    region = lax.dynamic_slice(local_totals, (zero_index, top_row, left_col), (3, PS, PS))
                    local_totals = lax.dynamic_update_slice(local_totals, region + object_terms, (zero_index, top_row, left_col))
                    return (local_totals, local_probe + probe_terms)
                start_totals = jnp.zeros((3, span, span), jnp.float32)
                local_totals, probe_acc = lax.fori_loop(0, slot_counts[tile_index], visit_slot, (start_totals, probe_acc))
                region = lax.dynamic_slice(totals, (zero_index, row_start, col_start), (3, span, span))
                totals = lax.dynamic_update_slice(totals, region + local_totals, (zero_index, row_start, col_start))
                return ((totals, probe_acc), None)
            totals = jnp.zeros((3, height + OVER, width + OVER), jnp.float32)
            (totals, probe_sum), unused = lax.scan(visit_tile, (totals, probe_sum), tile_ids)
            returned = totals[:, :height, :width]
            estimate = estimate + (returned[0:2] + penalty * (grid_consensus - grid_dual - estimate)) / (returned[2] + penalty)
        probe_new = probe_field + probe_step * probe_sum[0:2] / jnp.sqrt(probe_sum[2] + 1.0)
        return (estimate, probe_new)
    estimates, probes_new = lax.map(solve_group, (duals, probes, amplitudes, offsets, counts))
    grid_duals = lax.map(to_grid, duals)
    average = lax.optimization_barrier(jnp.sum(estimates + grid_duals, axis=0)) / GROUPS
    magnitude = jnp.sqrt(average[0] * average[0] + average[1] * average[1])
    settled = average / jnp.maximum(magnitude, 1.0)[None]
    duals_grid_new = grid_duals + estimates - settled[None]
    return (to_tiles(settled), lax.map(to_tiles, duals_grid_new), probes_new)
```

```python
import functools
import math

import jax
import jax.numpy as jnp
import ml_dtypes
import numpy as np
from jax import lax
from jax.experimental import pallas as pl
from jax.experimental.pallas import tpu as pltpu
from jax.sharding import PartitionSpec as P

PS = 256
TS = 256
OVER = 128
TGW = 4
SLOTS = 4
SPAN = TS + OVER
L = 128
CH = 32
META = 16

penalty = 0.5
smoothing = 0.05
probe_step = 3.0

f32 = jnp.float32
bf16 = jnp.bfloat16


def dft_tables():
    indices = np.arange(PS, dtype=np.int32)
    phase_index = indices[:, None] * indices[None, :] % PS
    angles = phase_index.astype(np.float32) * np.float32(2.0 * math.pi / PS)
    scale = np.float32(1.0 / math.sqrt(PS))
    re = (np.cos(angles) * scale).astype(ml_dtypes.bfloat16)
    im = (-np.sin(angles) * scale).astype(ml_dtypes.bfloat16)
    fwd = np.block([[re, -im], [im, re]])
    bwd = np.block([[re, im], [-im, re]])
    return jnp.asarray(fwd), jnp.asarray(bwd)


def shifted(value, rows, cols):
    n = lax.axis_size("tile")
    pairs = []
    for i in range(n):
        r, c = divmod(i, TGW)
        if 0 <= r + rows < n // TGW and 0 <= c + cols < TGW:
            pairs.append((i, i + rows * TGW + cols))
    return lax.ppermute(value, "tile", pairs)


def swapped(value, axis, bit):
    n = lax.axis_size(axis)
    return lax.ppermute(value, axis, [(i, i ^ bit) for i in range(n)])


def is_power(n):
    return n & (n - 1) == 0


def scan_sum(value):
    n = lax.axis_size("scan")
    if not is_power(n):
        return lax.psum(value, "scan").astype(f32)
    bits = [1 << k for k in range(n.bit_length() - 1)]
    half = value.shape[1] // 2
    parts = [value[:, :half], value[:, half:]]
    for k in range(len(bits)):
        for p in range(2):
            bit = bits[(k + p) % len(bits)]
            held = parts[p].astype(bf16)
            parts[p] = held.astype(f32) + swapped(held, "scan", bit).astype(f32)
    return jnp.concatenate(parts, 1)


def probe_update(total):
    return probe_step * total[0:2] / jnp.sqrt(total[2] + 1.0)


def probe_change(sums):
    n = lax.axis_size("tile")
    if not is_power(n) or n > PS // 16:
        return probe_update(lax.psum(sums, "tile"))
    index = lax.axis_index("tile")
    bits = [1 << k for k in range(n.bit_length() - 1)]
    for bit in bits:
        upper = (index // bit) % 2
        halves = sums.reshape(3, 2, sums.shape[1] // 2, PS)
        keep = lax.dynamic_index_in_dim(halves, upper, 1, keepdims=False)
        send = lax.dynamic_index_in_dim(halves, 1 - upper, 1, keepdims=False)
        sums = keep + swapped(send.astype(bf16), "tile", bit).astype(f32)
    change = probe_update(sums).astype(bf16)
    for bit in bits[::-1]:
        upper = (index // bit) % 2
        other = swapped(change, "tile", bit)
        change = jnp.where(
            upper == 1,
            jnp.concatenate([other, change], 1),
            jnp.concatenate([change, other], 1),
        )
    return change.astype(f32)


def lane_pull(blocks, c):
    lane = lax.broadcasted_iota(jnp.int32, blocks[0].shape, 1)
    keep = lane < L - c
    r = [pltpu.roll(v, (L - c) % L, 1) for v in blocks]
    return jnp.concatenate([jnp.where(keep, r[0], r[1]), jnp.where(keep, r[1], r[2])], 1)


def lane_push(blocks, c):
    lane = lax.broadcasted_iota(jnp.int32, blocks[0].shape, 1)
    past = lane >= c
    r = [pltpu.roll(v, c % L, 1) for v in blocks]
    z = jnp.zeros_like(r[0])
    return [jnp.where(past, r[0], z), jnp.where(past, r[1], r[0]), jnp.where(past, z, r[1])]


def visit_slot(s, r, c, ext, probe, amps, fwd, bwd, acc, pnum, win, X, Y, W):
    N = PS
    for k in range(0, N, CH):
        rows = slice(k, k + CH)
        w = [lane_pull([ext[ch, j, pl.ds(r + k, CH), :] for j in range(3)], c) for ch in range(2)]
        pr, pi = probe[0, rows, :], probe[1, rows, :]
        win[0, rows, :] = w[0]
        win[1, rows, :] = w[1]
        X[rows, :] = (pr * w[0] - pi * w[1]).astype(bf16)
        X[N + k : N + k + CH, :] = (pr * w[1] + pi * w[0]).astype(bf16)
        pnum[2, rows, :] += w[0] * w[0] + w[1] * w[1]
    t = jnp.dot(fwd[...], X[...], preferred_element_type=f32)
    Y[:, :N] = t[:N].astype(bf16)
    Y[:, N:] = t[N:].astype(bf16)
    W[...] = jnp.dot(Y[...], bwd[...], preferred_element_type=f32)
    for k in range(0, N, CH):
        wr, wi = W[k : k + CH, :N], W[k : k + CH, N:]
        f = amps[s, k : k + CH, :].astype(f32) * lax.rsqrt(wr * wr + wi * wi + smoothing) - 1.0
        X[k : k + CH, :] = (wr * f).astype(bf16)
        X[N + k : N + k + CH, :] = (wi * f).astype(bf16)
    t = jnp.dot(bwd[...], X[...], preferred_element_type=f32)
    Y[:, :N] = t[:N].astype(bf16)
    Y[:, N:] = t[N:].astype(bf16)
    W[...] = jnp.dot(Y[...], fwd[...], preferred_element_type=f32)
    for k in range(0, N, CH):
        rows = slice(k, k + CH)
        br, bi = W[rows, :N], W[rows, N:]
        pr, pi = probe[0, rows, :], probe[1, rows, :]
        wr, wi = win[0, rows, :], win[1, rows, :]
        pnum[0, rows, :] += wr * br + wi * bi
        pnum[1, rows, :] += wr * bi - wi * br
        for ch, v in enumerate((pr * br + pi * bi, pr * bi - pi * br)):
            for j, u in enumerate(lane_push([v[:, :L], v[:, L:]], c)):
                acc[ch, j, pl.ds(r + k, CH), :] += u


def first_pass(
    meta, own, dual, right, below, diag, probe, amps, fwd, bwd,
    acc, pnum, to_right, to_left, ext, win, X, Y, W,
):
    for j in range(2):
        cols = slice(j * L, (j + 1) * L)
        ext[:, j, :TS, :] = own[:, :, cols].astype(bf16).astype(f32)
        ext[:, j, TS:, :] = below[:, :, cols].astype(f32)
        acc[:, j, :TS, :] = -penalty * dual[:, :, cols]
        acc[:, j, TS:, :] = jnp.zeros((2, OVER, L), f32)
    ext[:, 2, :TS, :] = right[...].astype(f32)
    ext[:, 2, TS:, :] = diag[...].astype(f32)
    acc[:, 2] = jnp.zeros((2, SPAN, L), f32)
    pnum[...] = jnp.zeros_like(pnum)

    @pl.loop(0, meta[2 * SLOTS])
    def _(s):
        visit_slot(
            s, meta[2 * s], meta[2 * s + 1], ext, probe, amps, fwd, bwd, acc, pnum, win, X, Y, W
        )

    to_right[...] = acc[:, 2].astype(bf16)
    to_left[...] = acc[:, 0].astype(bf16)


def between(acc, from_left, from_right, to_below, to_above):
    for rows, out in ((slice(TS, SPAN), to_below), (slice(0, OVER), to_above)):
        out[:, 0] = (acc[:, 0, rows, :] + from_left[:, rows, :].astype(f32)).astype(bf16)
        out[:, 1] = acc[:, 1, rows, :].astype(bf16)
        out[:, 2] = (acc[:, 2, rows, :] + from_right[:, rows, :].astype(f32)).astype(bf16)


def weigh(metas, probe, weight, p2, buf):
    buf[...] = jnp.zeros_like(buf)
    for j in range(2):
        cols = slice(j * L, (j + 1) * L)
        p2[j] = probe[0, :, cols] * probe[0, :, cols] + probe[1, :, cols] * probe[1, :, cols]
    for dr in (-1, 0, 1):
        for dc in (-1, 0, 1):
            place = (dr + 1) * 3 + dc + 1
            first, rows = {-1: (OVER, OVER), 0: (0, PS), 1: (0, OVER)}[dr]
            base = {-1: 0, 0: OVER, 1: OVER + TS}[dr]

            @pl.loop(0, metas[place, 2 * SLOTS])
            def _(s, place=place, dc=dc, first=first, rows=rows, base=base):
                r, c = metas[place, 2 * s], metas[place, 2 * s + 1]
                for k in range(0, rows, 64):
                    at = pl.ds(base + r + k, 64)
                    v = [p2[j, first + k : first + k + 64, :] for j in range(2)]
                    lane = lax.broadcasted_iota(jnp.int32, v[0].shape, 1)
                    if dc == 0:
                        for j, u in enumerate(lane_push(v, c)):
                            buf[j, at, :] += u
                    elif dc < 0:
                        buf[0, at, :] += jnp.where(lane < c, pltpu.roll(v[1], c % L, 1), 0.0)
                    else:
                        buf[2, at, :] += jnp.where(lane >= c, pltpu.roll(v[0], c % L, 1), 0.0)

    weight[...] = buf[:, OVER : OVER + SPAN, :]


def second_pass(
    meta, own, dual, right, below, diag, acc1, from_left, from_right, from_above, from_below,
    weight, pnum1, probe, amps, fwd, bwd,
    partial, to_right, to_below, to_diag, pnum, ext, acc, win, X, Y, W,
):
    has_right = meta[2 * SLOTS + 1].astype(f32)
    has_below = meta[2 * SLOTS + 2].astype(f32)
    for ch in range(2):
        for j in range(3):
            cols = slice(j * L, (j + 1) * L)
            for k in range(0, SPAN, 64):
                rows = slice(k, k + 64)
                total = acc1[ch, j, rows, :]
                if j == 0:
                    total = total + from_left[ch, rows, :].astype(f32)
                if j == 2:
                    total = total + from_right[ch, rows, :].astype(f32)
                if k < OVER:
                    total = total + from_above[ch, j, rows, :].astype(f32)
                if k >= TS:
                    total = total + from_below[ch, j, k - TS : k - TS + 64, :].astype(f32)
                step = total / (weight[j, rows, :] + penalty)
                if j < 2 and k < TS:
                    est = own[ch, rows, cols] + step
                    partial[ch, rows, cols] = est
                else:
                    if k < TS:
                        est = right[ch, rows, :].astype(f32) + step
                    elif j < 2:
                        est = below[ch, k - TS : k - TS + 64, cols].astype(f32) + step
                    else:
                        est = diag[ch, k - TS : k - TS + 64, :].astype(f32) + step
                    if j == 2:
                        est = est * has_right
                    if k >= TS:
                        est = est * has_below
                ext[ch, j, rows, :] = est.astype(bf16).astype(f32)
    acc[...] = jnp.zeros_like(acc)
    pnum[...] = pnum1[...]

    @pl.loop(0, meta[2 * SLOTS])
    def _(s):
        visit_slot(
            s, meta[2 * s], meta[2 * s + 1], ext, probe, amps, fwd, bwd, acc, pnum, win, X, Y, W
        )

    for j in range(2):
        cols = slice(j * L, (j + 1) * L)
        to_below[:, :, cols] = acc[:, j, TS:, :].astype(bf16)
        for ch in range(2):
            for k in range(0, TS, 64):
                rows = slice(k, k + 64)
                est = partial[ch, rows, cols]
                pull = penalty * (own[ch, rows, cols] - dual[ch, rows, cols] - est)
                partial[ch, rows, cols] = est + (acc[ch, j, rows, :] + pull) / (
                    weight[j, rows, :] + penalty
                )
    to_right[...] = acc[:, 2, :TS, :].astype(bf16)
    to_diag[...] = acc[:, 2, TS:, :].astype(bf16)


def finish_estimate(partial, dual, weight, from_left, from_above, from_diag, combined, rounded):
    for ch in range(2):
        for j in range(2):
            cols = slice(j * L, (j + 1) * L)
            for k in range(0, TS, 64):
                rows = slice(k, k + 64)
                total = partial[ch, rows, cols] + dual[ch, rows, cols]
                came = None
                if j == 0:
                    came = from_left[ch, rows, :].astype(f32)
                if k < OVER:
                    above = from_above[ch, rows, cols].astype(f32)
                    came = above if came is None else came + above
                    if j == 0:
                        came = came + from_diag[ch, rows, :].astype(f32)
                if came is not None:
                    total = total + came / (weight[j, rows, :] + penalty)
                combined[ch, rows, cols] = total
                rounded[ch, rows, cols] = total.astype(bf16)


def settle(groups, summed, combined, settled, dual_new):
    for k in range(0, TS, CH):
        rows = slice(k, k + CH)
        re = summed[0, rows, :] * (1.0 / groups)
        im = summed[1, rows, :] * (1.0 / groups)
        over = 1.0 / jnp.maximum(jnp.sqrt(re * re + im * im), 1.0)
        re, im = re * over, im * over
        settled[0, rows, :] = re
        settled[1, rows, :] = im
        dual_new[0, rows, :] = combined[0, rows, :] - re
        dual_new[1, rows, :] = combined[1, rows, :] - im


V = pl.BlockSpec(memory_space=pltpu.VMEM)
S = pl.BlockSpec(memory_space=pltpu.SMEM)


def call(body, name, outs, scratch=(), scalars=0):
    def run(*operands):
        return pl.pallas_call(
            body,
            in_specs=[S] * scalars + [V] * (len(operands) - scalars),
            out_specs=[V] * len(outs),
            out_shape=[jax.ShapeDtypeStruct(shape, dtype) for shape, dtype in outs],
            scratch_shapes=[pltpu.VMEM(shape, dtype) for shape, dtype in scratch],
            compiler_params=pltpu.CompilerParams(vmem_limit_bytes=24 * 2**20),
            name=name,
        )(*operands)

    return run


WORK = [
    ((2, PS, PS), f32),
    ((2 * PS, PS), bf16),
    ((PS, 2 * PS), bf16),
    ((PS, 2 * PS), f32),
]
WIDE = ((2, 3, SPAN, L), f32)


def shards(consensus, duals, probes, amplitudes, offsets, counts):
    fwd, bwd = dft_tables()
    n = lax.axis_size("tile")
    index = lax.axis_index("tile")
    own = consensus[0]
    dual = duals[0, 0]
    probe = probes[0]
    amps = amplitudes[0, 0]

    rounded = own.astype(bf16)
    right = shifted(rounded[:, :, :OVER], 0, -1)
    below = shifted(rounded[:, :OVER, :], -1, 0)
    diag = shifted(rounded[:, :OVER, :OVER], -1, -1)

    edges = jnp.stack([index % TGW < TGW - 1, index // TGW < n // TGW - 1]).astype(jnp.int32)
    meta = jnp.concatenate(
        [
            offsets[0, 0].reshape(2 * SLOTS),
            counts[0],
            edges,
            jnp.zeros((META - 2 * SLOTS - 3,), jnp.int32),
        ]
    )
    beside = jnp.stack([shifted(meta, 0, 1), meta, shifted(meta, 0, -1)])
    metas = jnp.concatenate([shifted(beside, 1, 0), beside, shifted(beside, -1, 0)])
    (weight,) = call(
        weigh, "weigh", [((3, SPAN, L), f32)],
        [((2, PS, L), f32), ((3, SPAN + 2 * OVER, L), f32)], 1,
    )(metas, probe)

    acc, pnum, to_right, to_left = call(
        first_pass, "first_pass",
        [WIDE, ((3, PS, PS), f32), ((2, SPAN, L), bf16), ((2, SPAN, L), bf16)],
        [WIDE] + WORK, 1,
    )(meta, own, dual, right, below, diag, probe, amps, fwd, bwd)
    from_left = shifted(to_right, 0, 1)
    from_right = shifted(to_left, 0, -1)
    to_below, to_above = call(
        between, "between", [((2, 3, OVER, L), bf16)] * 2
    )(acc, from_left, from_right)
    from_above = shifted(to_below, 1, 0)
    from_below = shifted(to_above, -1, 0)

    partial, to_right, to_below, to_diag, pnum = call(
        second_pass, "second_pass",
        [((2, TS, TS), f32), ((2, TS, OVER), bf16), ((2, OVER, TS), bf16), ((2, OVER, OVER), bf16),
         ((3, PS, PS), f32)],
        [WIDE, WIDE] + WORK, 1,
    )(meta, own, dual, right, below, diag, acc, from_left, from_right, from_above, from_below,
      weight, pnum, probe, amps, fwd, bwd)
    from_left = shifted(to_right, 0, 1)
    from_above = shifted(to_below, 1, 0)
    from_diag = shifted(to_diag, 1, 1)
    combined, rounded = call(
        finish_estimate, "finish_estimate", [((2, TS, TS), f32), ((2, TS, TS), bf16)]
    )(partial, dual, weight, from_left, from_above, from_diag)
    summed = scan_sum(rounded)
    settled, dual_new = call(
        functools.partial(settle, lax.axis_size("scan")), "settle", [((2, TS, TS), f32)] * 2
    )(summed, combined)
    probe_new = probe + probe_change(pnum)
    return (settled[None], dual_new[None, None], probe_new[None])


def solution(mesh):
    placed = (
        P("tile", None, None, None),
        P("scan", "tile", None, None, None),
        P("scan", None, None, None),
        P("scan", "tile", None, None, None),
        P("scan", "tile", None, None),
        P("scan", "tile"),
    )
    return jax.shard_map(
        shards,
        mesh=mesh,
        in_specs=placed,
        out_specs=(
            P("tile", None, None, None),
            P("scan", "tile", None, None, None),
            P("scan", None, None, None),
        ),
        check_vma=False,
    )
```

```python
import functools
import math

import jax
import jax.numpy as jnp
import ml_dtypes
import numpy as np
from jax import lax
from jax.experimental import pallas as pl
from jax.experimental.pallas import tpu as pltpu
from jax.sharding import PartitionSpec as P

PS = 256
TS = 256
OVER = 128
TGW = 4
SLOTS = 4
SPAN = TS + OVER
L = 128
CH = 32
META = 16
COUNT = 2 * SLOTS
HAS_LEFT, HAS_RIGHT, HAS_ABOVE, HAS_BELOW, ODD, BIT1 = range(6)

penalty = 0.5
smoothing = 0.05
probe_step = 3.0

f32 = jnp.float32
bf16 = jnp.bfloat16


def dft_tables():
    indices = np.arange(PS, dtype=np.int32)
    phase_index = indices[:, None] * indices[None, :] % PS
    angles = phase_index.astype(np.float32) * np.float32(2.0 * math.pi / PS)
    scale = np.float32(1.0 / math.sqrt(PS))
    re = (np.cos(angles) * scale).astype(ml_dtypes.bfloat16)
    im = (-np.sin(angles) * scale).astype(ml_dtypes.bfloat16)
    fwd = np.block([[re, -im], [im, re]])
    bwd = np.block([[re, im], [-im, re]])
    return jnp.asarray(fwd), jnp.asarray(bwd)


def shifted(value, rows, cols):
    height = lax.axis_size("tile") // TGW
    pairs = []
    for i in range(height * TGW):
        r, c = divmod(i, TGW)
        pairs.append((i, (r + rows) % height * TGW + (c + cols) % TGW))
    return lax.ppermute(value, "tile", pairs)


def swapped(value, axis, bit):
    n = lax.axis_size(axis)
    return lax.ppermute(value, axis, [(i, i ^ bit) for i in range(n)])


def is_power(n):
    return n & (n - 1) == 0


def inner_swapped(value):
    n = lax.axis_size("tile")
    return lax.ppermute(value, "tile", [(i, i ^ 3 if i % TGW in (1, 2) else i) for i in range(n)])


def scan_sums(parts, sums):
    n = lax.axis_size("scan")
    change = None
    if not is_power(n):
        return [v for part in parts for v in (lax.psum(part, "scan"), jnp.zeros_like(part))], change
    bits = [1 << k for k in range(n.bit_length() - 1)]
    for k in range(len(bits)):
        came = [swapped(parts[p], "scan", bits[(k + p) % len(bits)]) for p in range(2)]
        pairs = [parts[0], came[0], parts[1], came[1]]
        if k < len(bits) - 1:
            outs = [(parts[0].shape, bf16)] * 2
            if sums is not None and k == 0:
                last = swapped(sums, "tile", 4)
                outs = outs + [((2,) + sums.shape[1:], bf16)]
                *parts, change = call(mix_and_update, "mix_and_update", outs)(*pairs, sums, last)
            else:
                parts = call(mix, f"mix{k}", outs)(*pairs)
    return pairs, change


def doubled(index, change, bit):
    other = swapped(change, "tile", bit)
    return jnp.where(
        (index // bit) % 2 == 1,
        jnp.concatenate([other, change], 1),
        jnp.concatenate([change, other], 1),
    )


def lane_pull(blocks, c):
    lane = lax.broadcasted_iota(jnp.int32, blocks[0].shape, 1)
    keep = lane < L - c
    r = [pltpu.roll(v, (L - c) % L, 1) for v in blocks]
    return jnp.concatenate([jnp.where(keep, r[0], r[1]), jnp.where(keep, r[1], r[2])], 1)


def lane_push(blocks, c):
    lane = lax.broadcasted_iota(jnp.int32, blocks[0].shape, 1)
    past = lane >= c
    r = [pltpu.roll(v, c % L, 1) for v in blocks]
    z = jnp.zeros_like(r[0])
    return [jnp.where(past, r[0], z), jnp.where(past, r[1], r[0]), jnp.where(past, z, r[1])]


def visit_pair(p, meta, ext, probe, amps, fwd, bwd, acc, pnum, win, X, Y, W):
    N = PS
    used = jnp.where(2 * p + 1 < meta[COUNT], 1.0, 0.0).astype(f32)
    corners = [(meta[4 * p + 2 * i], meta[4 * p + 2 * i + 1]) for i in range(2)]

    def leave(i):
        r, c = corners[i]
        for k in range(0, N, CH):
            rows = slice(k, k + CH)
            w = [
                lane_pull([ext[ch, j, pl.ds(r + k, CH), :] for j in range(3)], c) for ch in range(2)
            ]
            if i == 1:
                w = [v * used for v in w]
            pr, pi = probe[0, rows, :], probe[1, rows, :]
            win[i, 0, rows, :] = w[0]
            win[i, 1, rows, :] = w[1]
            X[i, rows, :] = (pr * w[0] - pi * w[1]).astype(bf16)
            X[i, N + k : N + k + CH, :] = (pr * w[1] + pi * w[0]).astype(bf16)
            pnum[2, rows, :] += w[0] * w[0] + w[1] * w[1]

    def columns(i, table):
        t = jnp.dot(table[...], X[i], preferred_element_type=f32)
        Y[i, :, :N] = t[:N].astype(bf16)
        Y[i, :, N:] = t[N:].astype(bf16)

    def rows_of(i, table):
        W[i] = jnp.dot(Y[i], table[...], preferred_element_type=f32)

    def compare(i):
        for k in range(0, N, CH):
            wr, wi = W[i, k : k + CH, :N], W[i, k : k + CH, N:]
            a = amps[2 * p + i, k : k + CH, :].astype(f32)
            f = a * lax.rsqrt(wr * wr + wi * wi + smoothing) - 1.0
            X[i, k : k + CH, :] = (wr * f).astype(bf16)
            X[i, N + k : N + k + CH, :] = (wi * f).astype(bf16)

    def gather(i):
        r, c = corners[i]
        for k in range(0, N, CH):
            rows = slice(k, k + CH)
            br, bi = W[i, rows, :N], W[i, rows, N:]
            pr, pi = probe[0, rows, :], probe[1, rows, :]
            wr, wi = win[i, 0, rows, :], win[i, 1, rows, :]
            pnum[0, rows, :] += wr * br + wi * bi
            pnum[1, rows, :] += wr * bi - wi * br
            for ch, v in enumerate((pr * br + pi * bi, pr * bi - pi * br)):
                for j, u in enumerate(lane_push([v[:, :L], v[:, L:]], c)):
                    acc[ch, j, pl.ds(r + k, CH), :] += u

    leave(0)
    columns(0, fwd)
    leave(1)
    rows_of(0, bwd)
    columns(1, fwd)
    compare(0)
    rows_of(1, bwd)
    columns(0, bwd)
    compare(1)
    rows_of(0, fwd)
    columns(1, bwd)
    gather(0)
    rows_of(1, fwd)
    gather(1)


def fetch(pairs, sems):
    copies = [pltpu.make_async_copy(src, dst, sems.at[i]) for i, (src, dst) in enumerate(pairs)]
    for copy in copies:
        copy.start()
    return copies


def stage(own_h, dual_h, probe_h, ext, acc, probe, sems, own, dual):
    copies = fetch([(own_h, own), (dual_h, dual), (probe_h, probe)], sems)
    acc[:, 2] = jnp.zeros((2, SPAN, L), f32)
    copies[0].wait()
    for j in range(2):
        cols = slice(j * L, (j + 1) * L)
        acc[:, j, TS:, :] = jnp.zeros((2, OVER, L), f32)
        ext[:, j, :TS, :] = own[:, :, cols].astype(bf16).astype(f32)
    copies[1].wait()
    for j in range(2):
        cols = slice(j * L, (j + 1) * L)
        acc[:, j, :TS, :] = -penalty * dual[:, :, cols]
    copies[2].wait()


def first_pass(
    two, meta, flags, right, below, diag, ext0, acc0, probe, fwd_h, bwd_h, amps_h, *rest,
):
    ext, acc, pnum, side, inner, *mids, fwd, bwd, amps, sems, win, X, Y, W = rest[3:]
    copies = fetch([(fwd_h, fwd), (bwd_h, bwd), (amps_h, amps)], sems)
    has_right = flags[HAS_RIGHT : HAS_RIGHT + 1, :]
    has_below = flags[HAS_BELOW : HAS_BELOW + 1, :]
    ext[:, 2, :TS, :] = right[...].astype(f32) * has_right
    ext[:, 2, TS:, :] = diag[...].astype(f32) * (has_right * has_below)
    for j in range(2):
        cols = slice(j * L, (j + 1) * L)
        ext[:, j, TS:, :] = below[:, :, cols].astype(f32) * has_below
    pnum[...] = jnp.zeros_like(pnum)
    for copy in copies:
        copy.wait()

    @pl.loop(0, (meta[COUNT] + 1) // 2)
    def _(p):
        visit_pair(p, meta, ext, probe, amps, fwd, bwd, acc, pnum, win, X, Y, W)

    odd = flags[ODD : ODD + 1, :] > 0.0
    for ch in range(2):
        side[ch] = jnp.where(odd, acc[ch, 0], acc[ch, 2]).astype(bf16)
        inner[ch] = jnp.where(odd, acc[ch, 2], acc[ch, 0]).astype(bf16)
        for rim, mid in zip(rims_of(two, flags, lambda rows: acc[ch, 1, rows, :]), mids):
            mid[ch] = rim.astype(bf16)


def rims_of(two, flags, get):
    down, up = get(slice(TS, SPAN)), get(slice(0, OVER))
    return [jnp.where(flags[HAS_BELOW : HAS_BELOW + 1, :] > 0.0, down, up)] if two else [down, up]


def from_sides(flags, side, inner):
    odd = flags[ODD : ODD + 1, :] > 0.0
    valid = flags[HAS_LEFT : HAS_LEFT + 1, :] * flags[HAS_RIGHT : HAS_RIGHT + 1, :]
    side, inner = side.astype(f32), inner.astype(f32) * valid
    return jnp.where(odd, side, inner), jnp.where(odd, inner, side)


def between(two, flags, acc, side, inner, *rest):
    outs = rest[-1:] if two else rest[-2:]
    for ch in range(2):
        for at in range(2):

            def total(rows):
                came = from_sides(flags, side[ch, rows, :], inner[ch, rows, :])[at]
                return acc[ch, 2 * at, rows, :] + came

            for rim, out in zip(rims_of(two, flags, total), outs):
                out[ch, at] = rim.astype(bf16)


def weigh(two, *rest):
    metas = rest[:3]
    flags, *sources = rest[-18:-11]
    weight, *targets, sems, p2, buf, there = rest[-11:]
    copies = fetch([(flags, there)] + list(zip(sources, targets)), sems)
    probe = targets[2]
    buf[...] = jnp.zeros_like(buf)
    copies[3].wait()
    for j in range(2):
        cols = slice(j * L, (j + 1) * L)
        p2[j] = probe[0, :, cols] * probe[0, :, cols] + probe[1, :, cols] * probe[1, :, cols]
    copies[0].wait()
    for dr in (-1, 0, 1):
        for dc in (-1, 0, 1):
            meta, at_row = metas[{0: 0, -1: 1, 1: 2}[dc]], {0: 0, -1: 1, 1: 1 if two else 2}[dr]
            first, rows = {-1: (OVER, OVER), 0: (0, PS), 1: (0, OVER)}[dr]
            base = {-1: 0, 0: OVER, 1: OVER + TS}[dr]
            count = meta[at_row, COUNT]
            for flag, at, step in (
                (HAS_ABOVE, -1, dr), (HAS_BELOW, 1, dr), (HAS_LEFT, -1, dc), (HAS_RIGHT, 1, dc)
            ):
                if step == at:
                    count = jnp.where(there[flag, 0] > 0.0, count, 0)

            @pl.loop(0, count)
            def _(s, meta=meta, at_row=at_row, dc=dc, first=first, rows=rows, base=base):
                r, c = meta[at_row, 2 * s], meta[at_row, 2 * s + 1]
                for k in range(0, rows, 64):
                    at = pl.ds(base + r + k, 64)
                    v = [p2[j, first + k : first + k + 64, :] for j in range(2)]
                    lane = lax.broadcasted_iota(jnp.int32, v[0].shape, 1)
                    if dc == 0:
                        for j, u in enumerate(lane_push(v, c)):
                            buf[j, at, :] += u
                    elif dc < 0:
                        buf[0, at, :] += jnp.where(lane < c, pltpu.roll(v[1], c % L, 1), 0.0)
                    else:
                        buf[2, at, :] += jnp.where(lane >= c, pltpu.roll(v[0], c % L, 1), 0.0)

    weight[...] = buf[:, OVER : OVER + SPAN, :]
    for k, copy in enumerate(copies):
        if k not in (0, 3):
            copy.wait()


def second_pass(
    meta, flags, right, below, diag, acc1, side, inner, mid_above, mid_below, from_above, from_below,
    weight, pnum1, own, dual, probe, amps, fwd, bwd,
    base, shrink, to_right, to_below, to_diag, pnum, to_swap,
    partial, ext, acc, win, X, Y, W,
):
    has_right = flags[HAS_RIGHT : HAS_RIGHT + 1, :]
    has_below = flags[HAS_BELOW : HAS_BELOW + 1, :]
    has_above = flags[HAS_ABOVE : HAS_ABOVE + 1, :]
    acc[...] = jnp.zeros_like(acc)
    pnum[...] = pnum1[...]
    for ch in range(2):
        for j in range(3):
            cols = slice(j * L, (j + 1) * L)
            for k in range(0, SPAN, 64):
                rows = slice(k, k + 64)
                total = acc1[ch, j, rows, :]
                if j != 1:
                    total = total + from_sides(flags, side[ch, rows, :], inner[ch, rows, :])[j // 2]
                if k < OVER:
                    came = mid_above[ch, rows, :] if j == 1 else from_above[ch, j // 2, rows, :]
                    total = total + came.astype(f32) * has_above
                if k >= TS:
                    rim = slice(k - TS, k - TS + 64)
                    came = mid_below[ch, rim, :] if j == 1 else from_below[ch, j // 2, rim, :]
                    total = total + came.astype(f32)
                step = total / (weight[j, rows, :] + penalty)
                if j < 2 and k < TS:
                    est = own[ch, rows, cols] + step
                    partial[ch, rows, cols] = est
                else:
                    if k < TS:
                        est = right[ch, rows, :].astype(f32) + step
                    elif j < 2:
                        est = below[ch, k - TS : k - TS + 64, cols].astype(f32) + step
                    else:
                        est = diag[ch, k - TS : k - TS + 64, :].astype(f32) + step
                    if j == 2:
                        est = est * has_right
                    if k >= TS:
                        est = est * has_below
                ext[ch, j, rows, :] = est.astype(bf16).astype(f32)

    @pl.loop(0, (meta[COUNT] + 1) // 2)
    def _(p):
        visit_pair(p, meta, ext, probe, amps, fwd, bwd, acc, pnum, win, X, Y, W)

    to_diag[...] = acc[:, 2, TS:, :].astype(bf16)
    to_right[...] = acc[:, 2, :TS, :].astype(bf16)
    odd = flags[ODD : ODD + 1, :1] > 0.0
    for ch in range(3):
        lo, hi = pnum[ch, : PS // 2, :], pnum[ch, PS // 2 :, :]
        to_swap[ch] = jnp.where(odd, lo, hi).astype(bf16)
    for j in range(2):
        cols = slice(j * L, (j + 1) * L)
        to_below[:, :, cols] = acc[:, j, TS:, :].astype(bf16)
        for k in range(0, TS, 64):
            rows = slice(k, k + 64)
            over = 1.0 / (weight[j, rows, :] + penalty)
            shrink[j, rows, :] = over
            for ch in range(2):
                est = partial[ch, rows, cols]
                held = dual[ch, rows, cols]
                pull = penalty * (own[ch, rows, cols] - held - est)
                base[ch, rows, cols] = est + held + (acc[ch, j, rows, :] + pull) * over


def halve(k, flags, sums, came, *rest):
    outs = rest[-1:] if k == 1 else rest[-2:]
    total = []
    for ch in range(3):
        kept = sums[ch]
        if k == 0:
            lo, hi = kept[: PS // 2], kept[PS // 2 :]
            kept = jnp.where(flags[ODD : ODD + 1, :1] > 0.0, hi, lo)
        total.append(kept + came[ch].astype(f32))
    if k == 1:
        for ch in range(3):
            outs[0][ch] = total[ch].astype(bf16)
        return
    up = flags[BIT1 : BIT1 + 1, :1] > 0.0
    half = came.shape[1] // 2
    for ch in range(3):
        lo, hi = total[ch][:half], total[ch][half:]
        outs[0][ch] = jnp.where(up, hi, lo)
        outs[1][ch] = jnp.where(up, lo, hi).astype(bf16)


def finish_estimate(flags, base, shrink, from_left, from_above, from_diag, *rest):
    combined, parts = rest[-3], rest[-2:]
    has_left = flags[HAS_LEFT : HAS_LEFT + 1, :]
    has_above = flags[HAS_ABOVE : HAS_ABOVE + 1, :]
    for ch in range(2):
        for j in range(2):
            cols = slice(j * L, (j + 1) * L)
            for k in range(0, TS, 64):
                rows = slice(k, k + 64)
                total = base[ch, rows, cols]
                came = None
                if j == 0:
                    came = from_left[ch, rows, :].astype(f32) * has_left
                if k < OVER:
                    above = from_above[ch, rows, cols].astype(f32) * has_above
                    came = above if came is None else came + above
                    if j == 0:
                        came = came + from_diag[ch, rows, :].astype(f32) * (has_left * has_above)
                if came is not None:
                    total = total + came * shrink[j, rows, :]
                combined[ch, rows, cols] = total
                part = slice(k % (TS // 2), k % (TS // 2) + 64)
                parts[k // (TS // 2)][ch, part, cols] = total.astype(bf16)


def mixed(first, first_came, second, second_came, outs):
    for out, part, came in ((outs[0], first, first_came), (outs[1], second, second_came)):
        for ch in range(2):
            out[ch] = (part[ch].astype(f32) + came[ch].astype(f32)).astype(bf16)


def mix(*refs):
    mixed(*refs[:4], refs[-2:])


def mix_and_update(first, first_came, second, second_came, held, came, *outs):
    mixed(first, first_came, second, second_came, outs)
    total = [held[ch].astype(f32) + came[ch].astype(f32) for ch in range(3)]
    over = probe_step * lax.rsqrt(total[2] + 1.0)
    for ch in range(2):
        outs[2][ch] = (total[ch] * over).astype(bf16)


def settle(groups, first, first_came, second, second_came, combined, *rest):
    settled, dual_new = rest[-2:]
    for k in range(0, TS, CH):
        rows = slice(k, k + CH)
        part, came = (first, first_came) if k < TS // 2 else (second, second_came)
        at = slice(k % (TS // 2), k % (TS // 2) + CH)
        re, im = [
            (part[ch, at, :].astype(f32) + came[ch, at, :].astype(f32)) * (1.0 / groups)
            for ch in range(2)
        ]
        over = 1.0 / jnp.maximum(jnp.sqrt(re * re + im * im), 1.0)
        re, im = re * over, im * over
        settled[0, rows, :] = re
        settled[1, rows, :] = im
        dual_new[0, rows, :] = combined[0, rows, :] - re
        dual_new[1, rows, :] = combined[1, rows, :] - im


V = pl.BlockSpec(memory_space=pltpu.VMEM)
S = pl.BlockSpec(memory_space=pltpu.SMEM)
H = pl.BlockSpec(memory_space=pltpu.HBM)


def pinned(value):
    return pltpu.with_memory_space_constraint(value, pltpu.VMEM)


def call(body, name, outs, scratch=(), scalars=0, far=0, copies=0, aliases=None, held=False, flops=0):
    def run(*operands):
        near = len(operands) - scalars - far
        spaces = [None] * (scalars + near) + [pltpu.HBM] * far
        operands = [
            v if space is None else pltpu.with_memory_space_constraint(v, space)
            for v, space in zip(operands, spaces)
        ]
        return pl.pallas_call(
            body,
            in_specs=[S] * scalars + [V] * near + [H] * far,
            out_specs=[V] * len(outs),
            out_shape=[
                pltpu.VMEM(shape, dtype) if held else jax.ShapeDtypeStruct(shape, dtype)
                for shape, dtype in outs
            ],
            scratch_shapes=[
                pltpu.SemaphoreType.DMA((copies,)) if one is None else pltpu.VMEM(*one)
                if isinstance(one, tuple) else one
                for one in scratch
            ],
            input_output_aliases=aliases or {},
            cost_estimate=pl.CostEstimate(
                flops=flops or sum(math.prod(shape) for shape, _ in outs),
                bytes_accessed=sum(v.size * v.dtype.itemsize for v in operands[scalars + near :]),
                transcendentals=0,
            ),
            compiler_params=pltpu.CompilerParams(vmem_limit_bytes=24 * 2**20),
            name=name,
        )(*operands)

    return run


PLANES = ((2, PS, PS), f32)
PASS = SLOTS * 4 * 8 * PS**3
WORK = [
    ((2, 2, PS, PS), f32),
    ((2, 2 * PS, PS), bf16),
    ((2, PS, 2 * PS), bf16),
    ((2, PS, 2 * PS), f32),
]
TABLE = ((2 * PS, 2 * PS), bf16)
WIDE = ((2, 3, SPAN, L), f32)
SUMS = ((3, PS, PS), f32)


def shards(consensus, duals, probes, amplitudes, offsets, counts):
    fwd, bwd = dft_tables()
    n = lax.axis_size("tile")
    index = lax.axis_index("tile")
    own = consensus[0]
    dual = duals[0, 0]
    probe = probes[0]
    amps = amplitudes[0, 0]
    measured = ((SLOTS, PS, PS), bf16)

    rounded = own.astype(bf16)
    below = shifted(rounded[:, :OVER, :], -1, 0)
    diag = shifted(rounded[:, :OVER, :OVER], -1, -1)
    right = shifted(rounded[:, :, :OVER], 0, -1)

    height = n // TGW
    two = height == 2
    row, col = index // TGW, index % TGW
    flags = [col > 0, col < TGW - 1, row > 0, row < height - 1]
    flags = flags + [(index // bit) % 2 == 1 for bit in (1, 2)] + [col < 0] * 2
    flags = jnp.broadcast_to(jnp.stack(flags).astype(f32)[:, None], (8, L))
    meta = jnp.concatenate(
        [offsets[0, 0].reshape(COUNT), counts[0], jnp.zeros((META - COUNT - 1,), jnp.int32)]
    )
    column = [meta, shifted(meta, 1, 0)] if two else [meta, shifted(meta, 1, 0), shifted(meta, -1, 0)]
    column = jnp.stack(column)
    metas = [column, shifted(column, 0, 1), shifted(column, 0, -1)]

    inputs = (own, dual, probe, amps, fwd, bwd)
    staged = call(
        stage, "stage", [WIDE, WIDE, PLANES], [None, PLANES, PLANES], 0, 3, 3, held=True
    )(own, dual, probe)
    staged = [pinned(v) for v in staged]
    rim = ((2, OVER, L), bf16)
    ext, acc, pnum, side, inner, *mids = call(
        functools.partial(first_pass, two), "first_pass",
        [WIDE, WIDE, SUMS, ((2, SPAN, L), bf16), ((2, SPAN, L), bf16)] + [rim] * (1 if two else 2),
        [TABLE, TABLE, measured, None] + WORK, 1, 6, 3, aliases={5: 0, 6: 1}, flops=PASS,
    )(meta, flags, right, below, diag, *staged, fwd, bwd, amps, *metas)
    side = swapped(side, "tile", 1)
    inner = inner_swapped(inner)

    def down_and_up(rims):
        down = shifted(rims[0], 1, 0)
        return down, down if two else shifted(rims[1], -1, 0)

    mid_above, mid_below = down_and_up(mids)
    rims = call(
        functools.partial(between, two), "between", [((2, 2, OVER, L), bf16)] * (1 if two else 2)
    )(flags, acc, side, inner, pnum, right, below, diag, mid_above, mid_below)
    from_above, from_below = down_and_up(rims)
    weight, *inputs = call(
        functools.partial(weigh, two), "weigh",
        [((3, SPAN, L), f32), PLANES, PLANES, PLANES, measured, TABLE, TABLE],
        [None, ((2, PS, L), f32), ((3, SPAN + 2 * OVER, L), f32), pltpu.SMEM((8, L), f32)],
        len(metas), 7, 7, held=True,
    )(*metas, rims[0], acc, side, inner, pnum, right, below, diag, mid_above, mid_below, flags, *inputs)
    weight, *inputs = [pinned(v) for v in (weight, *inputs)]

    base, shrink, to_right, to_below, to_diag, pnum, to_swap = call(
        second_pass, "second_pass",
        [PLANES, ((2, TS, L), f32), ((2, TS, OVER), bf16), ((2, OVER, TS), bf16),
         ((2, OVER, OVER), bf16), SUMS, ((3, PS // 2, PS), bf16)],
        [PLANES, WIDE, WIDE] + WORK, 1, flops=PASS,
    )(meta, flags, right, below, diag, acc, side, inner, mid_above, mid_below, from_above,
      from_below, weight, pnum, *inputs)
    from_above = shifted(to_below, 1, 0)
    from_diag = shifted(to_diag, 1, 1)
    from_left = shifted(to_right, 0, 1)

    def halved(k, sums, send, *after):
        came = swapped(send, "tile", 1 << k)
        rows = came.shape[1]
        outs = [((3, rows // 2, PS), f32), ((3, rows // 2, PS), bf16)]
        if k == 1:
            outs = [((3, rows, PS), bf16)]
        return call(functools.partial(halve, k), f"halve{k}", outs)(flags, sums, came, *after)

    eight = n == 8 and lax.axis_size("scan") in (4, 8)
    first = halved(0, pnum, to_swap, base, shrink) if eight else []
    combined, *parts = call(
        finish_estimate, "finish_estimate", [PLANES] + [((2, TS // 2, TS), bf16)] * 2
    )(flags, base, shrink, from_left, from_above, from_diag, *first)
    sums = halved(1, *first, parts[0])[0] if eight else None
    pairs, change = scan_sums(parts, sums)
    settled, dual_new = call(
        functools.partial(settle, lax.axis_size("scan")), "settle", [PLANES] * 2
    )(*pairs, combined)
    if eight:
        change = doubled(index, doubled(index, change, 2), 1).astype(f32)
    else:
        total = lax.psum(pnum, "tile")
        change = probe_step * total[0:2] / jnp.sqrt(total[2] + 1.0)
    probe_new = probe + change
    return (settled[None], dual_new[None, None], probe_new[None])


def solution(mesh):
    placed = (
        P("tile", None, None, None),
        P("scan", "tile", None, None, None),
        P("scan", None, None, None),
        P("scan", "tile", None, None, None),
        P("scan", "tile", None, None),
        P("scan", "tile"),
    )
    return jax.shard_map(
        shards,
        mesh=mesh,
        in_specs=placed,
        out_specs=(
            P("tile", None, None, None),
            P("scan", "tile", None, None, None),
            P("scan", None, None, None),
        ),
        check_vma=False,
    )
```

```python
import functools
import math

import jax
import jax.numpy as jnp
import ml_dtypes
import numpy as np
from jax import lax
from jax.experimental import pallas as pl
from jax.experimental.pallas import tpu as pltpu
from jax.sharding import PartitionSpec as P

PS = 256
TS = 256
OVER = 128
TGW = 4
SLOTS = 4
SPAN = TS + OVER
L = 128
CH = 32
META = 16
COUNT = 2 * SLOTS
HAS_LEFT, HAS_RIGHT, HAS_ABOVE, HAS_BELOW, ODD = range(5)

penalty = 0.5
smoothing = 0.05
probe_step = 3.0

f32 = jnp.float32
bf16 = jnp.bfloat16


def dft_tables():
    indices = np.arange(PS, dtype=np.int32)
    phase_index = indices[:, None] * indices[None, :] % PS
    angles = phase_index.astype(np.float32) * np.float32(2.0 * math.pi / PS)
    scale = np.float32(1.0 / math.sqrt(PS))
    re = (np.cos(angles) * scale).astype(ml_dtypes.bfloat16)
    im = (-np.sin(angles) * scale).astype(ml_dtypes.bfloat16)
    fwd = np.block([[re, -im], [im, re]])
    bwd = np.block([[re, im], [-im, re]])
    return jnp.asarray(fwd), jnp.asarray(bwd)


def shifted(value, rows, cols):
    height = lax.axis_size("tile") // TGW
    pairs = []
    for i in range(height * TGW):
        r, c = divmod(i, TGW)
        pairs.append((i, (r + rows) % height * TGW + (c + cols) % TGW))
    return lax.ppermute(value, "tile", pairs)


def swapped(value, axis, bit):
    n = lax.axis_size(axis)
    return lax.ppermute(value, axis, [(i, i ^ bit) for i in range(n)])


def is_power(n):
    return n & (n - 1) == 0


def inner_swapped(value):
    n = lax.axis_size("tile")
    return lax.ppermute(value, "tile", [(i, i ^ 3 if i % TGW in (1, 2) else i) for i in range(n)])


def scan_sums(parts):
    n = lax.axis_size("scan")
    if not is_power(n):
        return [v for part in parts for v in (lax.psum(part, "scan"), jnp.zeros_like(part))]
    bits = [1 << k for k in range(n.bit_length() - 1)]
    for k in range(len(bits)):
        came = [swapped(parts[p], "scan", bits[(k + p) % len(bits)]) for p in range(2)]
        pairs = [parts[0], came[0], parts[1], came[1]]
        if k < len(bits) - 1:
            outs = [(parts[0].shape, bf16)] * 2
            parts = call(mix, f"mix{k}", outs)(*pairs)
    return pairs


def doubled(index, change, bit):
    other = swapped(change, "tile", bit)
    return jnp.where(
        (index // bit) % 2 == 1,
        jnp.concatenate([other, change], 1),
        jnp.concatenate([change, other], 1),
    )


def lane_pull(blocks, c):
    lane = lax.broadcasted_iota(jnp.int32, blocks[0].shape, 1)
    keep = lane < L - c
    r = [pltpu.roll(v, (L - c) % L, 1) for v in blocks]
    return jnp.concatenate([jnp.where(keep, r[0], r[1]), jnp.where(keep, r[1], r[2])], 1)


def lane_push(blocks, c):
    lane = lax.broadcasted_iota(jnp.int32, blocks[0].shape, 1)
    past = lane >= c
    r = [pltpu.roll(v, c % L, 1) for v in blocks]
    z = jnp.zeros_like(r[0])
    return [jnp.where(past, r[0], z), jnp.where(past, r[1], r[0]), jnp.where(past, z, r[1])]


def visit_pair(p, meta, ext, probe, amps, fwd, bwd, acc, pnum, win, X, Y, W):
    N = PS
    used = jnp.where(2 * p + 1 < meta[COUNT], 1.0, 0.0).astype(f32)
    corners = [(meta[4 * p + 2 * i], meta[4 * p + 2 * i + 1]) for i in range(2)]

    def leave(i):
        r, c = corners[i]
        for k in range(0, N, CH):
            rows = slice(k, k + CH)
            w = [
                lane_pull([ext[ch, j, pl.ds(r + k, CH), :] for j in range(3)], c) for ch in range(2)
            ]
            if i == 1:
                w = [v * used for v in w]
            pr, pi = probe[0, rows, :], probe[1, rows, :]
            win[i, 0, rows, :] = w[0]
            win[i, 1, rows, :] = w[1]
            X[i, rows, :] = (pr * w[0] - pi * w[1]).astype(bf16)
            X[i, N + k : N + k + CH, :] = (pr * w[1] + pi * w[0]).astype(bf16)
            pnum[2, rows, :] += w[0] * w[0] + w[1] * w[1]

    def columns(i, table):
        t = jnp.dot(table[...], X[i], preferred_element_type=f32)
        Y[i, :, :N] = t[:N].astype(bf16)
        Y[i, :, N:] = t[N:].astype(bf16)

    def rows_of(i, table):
        W[i] = jnp.dot(Y[i], table[...], preferred_element_type=f32)

    def compare(i):
        for k in range(0, N, CH):
            wr, wi = W[i, k : k + CH, :N], W[i, k : k + CH, N:]
            a = amps[2 * p + i, k : k + CH, :].astype(f32)
            f = a * lax.rsqrt(wr * wr + wi * wi + smoothing) - 1.0
            X[i, k : k + CH, :] = (wr * f).astype(bf16)
            X[i, N + k : N + k + CH, :] = (wi * f).astype(bf16)

    def gather(i):
        r, c = corners[i]
        for k in range(0, N, CH):
            rows = slice(k, k + CH)
            br, bi = W[i, rows, :N], W[i, rows, N:]
            pr, pi = probe[0, rows, :], probe[1, rows, :]
            wr, wi = win[i, 0, rows, :], win[i, 1, rows, :]
            pnum[0, rows, :] += wr * br + wi * bi
            pnum[1, rows, :] += wr * bi - wi * br
            for ch, v in enumerate((pr * br + pi * bi, pr * bi - pi * br)):
                for j, u in enumerate(lane_push([v[:, :L], v[:, L:]], c)):
                    acc[ch, j, pl.ds(r + k, CH), :] += u

    leave(0)
    columns(0, fwd)
    leave(1)
    rows_of(0, bwd)
    columns(1, fwd)
    compare(0)
    rows_of(1, bwd)
    columns(0, bwd)
    compare(1)
    rows_of(0, fwd)
    columns(1, bwd)
    gather(0)
    rows_of(1, fwd)
    gather(1)


def fetch(pairs, sems):
    copies = [pltpu.make_async_copy(src, dst, sems.at[i]) for i, (src, dst) in enumerate(pairs)]
    for copy in copies:
        copy.start()
    return copies


def stage(own_h, dual_h, probe_h, ext, acc, probe, sems, own, dual):
    copies = fetch([(own_h, own), (dual_h, dual), (probe_h, probe)], sems)
    acc[:, 2] = jnp.zeros((2, SPAN, L), f32)
    copies[0].wait()
    for j in range(2):
        cols = slice(j * L, (j + 1) * L)
        acc[:, j, TS:, :] = jnp.zeros((2, OVER, L), f32)
        ext[:, j, :TS, :] = own[:, :, cols].astype(bf16).astype(f32)
    copies[1].wait()
    for j in range(2):
        cols = slice(j * L, (j + 1) * L)
        acc[:, j, :TS, :] = -penalty * dual[:, :, cols]
    copies[2].wait()


def first_pass(
    two, meta, flags, right, below0, below1, diag, ext0, acc0, probe, fwd_h, bwd_h, amps_h, *rest,
):
    ext, acc, pnum, side, inner, *mids, fwd, bwd, amps, sems, win, X, Y, W = rest[3:]
    copies = fetch([(fwd_h, fwd), (bwd_h, bwd), (amps_h, amps)], sems)
    has_right = flags[HAS_RIGHT : HAS_RIGHT + 1, :]
    has_below = flags[HAS_BELOW : HAS_BELOW + 1, :]
    ext[:, 2, :TS, :] = right[...].astype(f32) * has_right
    ext[:, 2, TS:, :] = diag[...].astype(f32) * (has_right * has_below)
    for j in range(2):
        ext[:, j, TS:, :] = (below0, below1)[j][...].astype(f32) * has_below
    pnum[...] = jnp.zeros_like(pnum)
    for copy in copies:
        copy.wait()

    @pl.loop(0, (meta[COUNT] + 1) // 2)
    def _(p):
        visit_pair(p, meta, ext, probe, amps, fwd, bwd, acc, pnum, win, X, Y, W)

    odd = flags[ODD : ODD + 1, :] > 0.0
    for ch in range(2):
        side[ch] = jnp.where(odd, acc[ch, 0], acc[ch, 2]).astype(bf16)
        inner[ch] = jnp.where(odd, acc[ch, 2], acc[ch, 0]).astype(bf16)
        for rim, mid in zip(rims_of(two, flags, lambda rows: acc[ch, 1, rows, :]), mids):
            mid[ch] = rim.astype(bf16)


def rims_of(two, flags, get):
    down, up = get(slice(TS, SPAN)), get(slice(0, OVER))
    return [jnp.where(flags[HAS_BELOW : HAS_BELOW + 1, :] > 0.0, down, up)] if two else [down, up]


def from_sides(flags, side, inner):
    odd = flags[ODD : ODD + 1, :] > 0.0
    valid = flags[HAS_LEFT : HAS_LEFT + 1, :] * flags[HAS_RIGHT : HAS_RIGHT + 1, :]
    side, inner = side.astype(f32), inner.astype(f32) * valid
    return jnp.where(odd, side, inner), jnp.where(odd, inner, side)


def between(two, flags, acc, side, inner, *rest):
    outs = rest[-1:] if two else rest[-2:]
    for ch in range(2):
        for at in range(2):

            def total(rows):
                came = from_sides(flags, side[ch, rows, :], inner[ch, rows, :])[at]
                return acc[ch, 2 * at, rows, :] + came

            for rim, out in zip(rims_of(two, flags, total), outs):
                out[ch, at] = rim.astype(bf16)


def weigh(two, *rest):
    metas = rest[:3]
    flags, *sources = rest[-18:-11]
    weight, *targets, sems, p2, buf, there = rest[-11:]
    copies = fetch([(flags, there)] + list(zip(sources, targets)), sems)
    probe = targets[2]
    buf[...] = jnp.zeros_like(buf)
    copies[3].wait()
    for j in range(2):
        cols = slice(j * L, (j + 1) * L)
        p2[j] = probe[0, :, cols] * probe[0, :, cols] + probe[1, :, cols] * probe[1, :, cols]
    copies[0].wait()
    for dr in (-1, 0, 1):
        for dc in (-1, 0, 1):
            meta, at_row = metas[{0: 0, -1: 1, 1: 2}[dc]], {0: 0, -1: 1, 1: 1 if two else 2}[dr]
            first, rows = {-1: (OVER, OVER), 0: (0, PS), 1: (0, OVER)}[dr]
            base = {-1: 0, 0: OVER, 1: OVER + TS}[dr]
            count = meta[at_row, COUNT]
            for flag, at, step in (
                (HAS_ABOVE, -1, dr), (HAS_BELOW, 1, dr), (HAS_LEFT, -1, dc), (HAS_RIGHT, 1, dc)
            ):
                if step == at:
                    count = jnp.where(there[flag, 0] > 0.0, count, 0)

            @pl.loop(0, count)
            def _(s, meta=meta, at_row=at_row, dc=dc, first=first, rows=rows, base=base):
                r, c = meta[at_row, 2 * s], meta[at_row, 2 * s + 1]
                for k in range(0, rows, 64):
                    at = pl.ds(base + r + k, 64)
                    v = [p2[j, first + k : first + k + 64, :] for j in range(2)]
                    lane = lax.broadcasted_iota(jnp.int32, v[0].shape, 1)
                    if dc == 0:
                        for j, u in enumerate(lane_push(v, c)):
                            buf[j, at, :] += u
                    elif dc < 0:
                        buf[0, at, :] += jnp.where(lane < c, pltpu.roll(v[1], c % L, 1), 0.0)
                    else:
                        buf[2, at, :] += jnp.where(lane >= c, pltpu.roll(v[0], c % L, 1), 0.0)

    weight[...] = buf[:, OVER : OVER + SPAN, :]
    for k, copy in enumerate(copies):
        if k not in (0, 3):
            copy.wait()


def second_pass(
    meta, flags, right, below0, below1, diag, acc1, side, inner, mid_above, mid_below, from_above, from_below,
    weight, pnum1, own, dual, probe, amps, fwd, bwd,
    base, shrink, to_right, lower, to_below, pnum, to_swap,
    partial, ext, acc, win, X, Y, W,
):
    has_right = flags[HAS_RIGHT : HAS_RIGHT + 1, :]
    has_below = flags[HAS_BELOW : HAS_BELOW + 1, :]
    has_above = flags[HAS_ABOVE : HAS_ABOVE + 1, :]
    acc[...] = jnp.zeros_like(acc)
    pnum[...] = pnum1[...]
    for ch in range(2):
        for j in range(3):
            cols = slice(j * L, (j + 1) * L)
            for k in range(0, SPAN, 64):
                rows = slice(k, k + 64)
                total = acc1[ch, j, rows, :]
                if j != 1:
                    total = total + from_sides(flags, side[ch, rows, :], inner[ch, rows, :])[j // 2]
                if k < OVER:
                    came = mid_above[ch, rows, :] if j == 1 else from_above[ch, j // 2, rows, :]
                    total = total + came.astype(f32) * has_above
                if k >= TS:
                    rim = slice(k - TS, k - TS + 64)
                    came = mid_below[ch, rim, :] if j == 1 else from_below[ch, j // 2, rim, :]
                    total = total + came.astype(f32)
                step = total / (weight[j, rows, :] + penalty)
                if j < 2 and k < TS:
                    est = own[ch, rows, cols] + step
                    partial[ch, rows, cols] = est
                else:
                    if k < TS:
                        est = right[ch, rows, :].astype(f32) + step
                    elif j < 2:
                        est = (below0, below1)[j][ch, k - TS : k - TS + 64, :].astype(f32) + step
                    else:
                        est = diag[ch, k - TS : k - TS + 64, :].astype(f32) + step
                    if j == 2:
                        est = est * has_right
                    if k >= TS:
                        est = est * has_below
                ext[ch, j, rows, :] = est.astype(bf16).astype(f32)

    @pl.loop(0, (meta[COUNT] + 1) // 2)
    def _(p):
        visit_pair(p, meta, ext, probe, amps, fwd, bwd, acc, pnum, win, X, Y, W)

    to_right[...] = acc[:, 2].astype(bf16)
    to_below[...] = acc[:, 1, TS:, :].astype(bf16)
    lower[...] = acc[:, 0, TS:, :]
    odd = flags[ODD : ODD + 1, :1] > 0.0
    for ch in range(3):
        lo, hi = pnum[ch, : PS // 2, :], pnum[ch, PS // 2 :, :]
        to_swap[ch] = jnp.where(odd, lo, hi).astype(bf16)
    for j in range(2):
        cols = slice(j * L, (j + 1) * L)
        for k in range(0, TS, 64):
            rows = slice(k, k + 64)
            over = 1.0 / (weight[j, rows, :] + penalty)
            shrink[j, rows, :] = over
            for ch in range(2):
                est = partial[ch, rows, cols]
                held = dual[ch, rows, cols]
                pull = penalty * (own[ch, rows, cols] - held - est)
                base[ch, rows, cols] = est + held + (acc[ch, j, rows, :] + pull) * over


def halve(flags, sums, came, *rest):
    odd = flags[ODD : ODD + 1, :1] > 0.0
    for ch in range(3):
        lo, hi = sums[ch, : PS // 2, :], sums[ch, PS // 2 :, :]
        rest[-1][ch] = (jnp.where(odd, hi, lo) + came[ch].astype(f32)).astype(bf16)


def add(held, came, *rest):
    for ch in range(3):
        rest[-1][ch] = (held[ch].astype(f32) + came[ch].astype(f32)).astype(bf16)


def add_rim(flags, rim, from_left, *rest):
    has_left = flags[HAS_LEFT : HAS_LEFT + 1, :]
    for ch in range(2):
        rest[-1][ch] = (rim[ch] + from_left[ch, TS:, :].astype(f32) * has_left).astype(bf16)


def finish_estimate(flags, base, shrink, from_left, above0, above1, *rest):
    combined, parts = rest[-3], rest[-2:]
    has_left = flags[HAS_LEFT : HAS_LEFT + 1, :]
    has_above = flags[HAS_ABOVE : HAS_ABOVE + 1, :]
    for ch in range(2):
        for j in range(2):
            cols = slice(j * L, (j + 1) * L)
            for k in range(0, TS, 64):
                rows = slice(k, k + 64)
                total = base[ch, rows, cols]
                came = None
                if j == 0:
                    came = from_left[ch, rows, :].astype(f32) * has_left
                if k < OVER:
                    above = (above0, above1)[j][ch, rows, :].astype(f32) * has_above
                    came = above if came is None else came + above
                if came is not None:
                    total = total + came * shrink[j, rows, :]
                combined[ch, rows, cols] = total
                part = slice(k % (TS // 2), k % (TS // 2) + 64)
                parts[k // (TS // 2)][ch, part, cols] = total.astype(bf16)


def mixed(first, first_came, second, second_came, outs):
    for out, part, came in ((outs[0], first, first_came), (outs[1], second, second_came)):
        for ch in range(2):
            out[ch] = (part[ch].astype(f32) + came[ch].astype(f32)).astype(bf16)


def mix(*refs):
    mixed(*refs[:4], refs[-2:])


def update(held, came, *rest):
    total = [held[ch].astype(f32) + came[ch].astype(f32) for ch in range(3)]
    over = probe_step * lax.rsqrt(total[2] + 1.0)
    for ch in range(2):
        rest[-1][ch] = (total[ch] * over).astype(bf16)


def settle(groups, first, first_came, second, second_came, combined, *rest):
    settled, dual_new = rest[-2:]
    for k in range(0, TS, CH):
        rows = slice(k, k + CH)
        part, came = (first, first_came) if k < TS // 2 else (second, second_came)
        at = slice(k % (TS // 2), k % (TS // 2) + CH)
        re, im = [
            (part[ch, at, :].astype(f32) + came[ch, at, :].astype(f32)) * (1.0 / groups)
            for ch in range(2)
        ]
        over = 1.0 / jnp.maximum(jnp.sqrt(re * re + im * im), 1.0)
        re, im = re * over, im * over
        settled[0, rows, :] = re
        settled[1, rows, :] = im
        dual_new[0, rows, :] = combined[0, rows, :] - re
        dual_new[1, rows, :] = combined[1, rows, :] - im


V = pl.BlockSpec(memory_space=pltpu.VMEM)
S = pl.BlockSpec(memory_space=pltpu.SMEM)
H = pl.BlockSpec(memory_space=pltpu.HBM)


def pinned(value):
    return pltpu.with_memory_space_constraint(value, pltpu.VMEM)


def call(body, name, outs, scratch=(), scalars=0, far=0, copies=0, aliases=None, held=False, flops=0):
    def run(*operands):
        near = len(operands) - scalars - far
        spaces = [None] * (scalars + near) + [pltpu.HBM] * far
        operands = [
            v if space is None else pltpu.with_memory_space_constraint(v, space)
            for v, space in zip(operands, spaces)
        ]
        return pl.pallas_call(
            body,
            in_specs=[S] * scalars + [V] * near + [H] * far,
            out_specs=[V] * len(outs),
            out_shape=[
                pltpu.VMEM(shape, dtype) if held else jax.ShapeDtypeStruct(shape, dtype)
                for shape, dtype in outs
            ],
            scratch_shapes=[
                pltpu.SemaphoreType.DMA((copies,)) if one is None else pltpu.VMEM(*one)
                if isinstance(one, tuple) else one
                for one in scratch
            ],
            input_output_aliases=aliases or {},
            cost_estimate=pl.CostEstimate(
                flops=flops or sum(math.prod(shape) for shape, _ in outs),
                bytes_accessed=sum(v.size * v.dtype.itemsize for v in operands[scalars + near :]),
                transcendentals=0,
            ),
            compiler_params=pltpu.CompilerParams(vmem_limit_bytes=24 * 2**20),
            name=name,
        )(*operands)

    return run


PLANES = ((2, PS, PS), f32)
PASS = SLOTS * 4 * 8 * PS**3
WORK = [
    ((2, 2, PS, PS), f32),
    ((2, 2 * PS, PS), bf16),
    ((2, PS, 2 * PS), bf16),
    ((2, PS, 2 * PS), f32),
]
TABLE = ((2 * PS, 2 * PS), bf16)
WIDE = ((2, 3, SPAN, L), f32)
SUMS = ((3, PS, PS), f32)


def shards(consensus, duals, probes, amplitudes, offsets, counts):
    fwd, bwd = dft_tables()
    n = lax.axis_size("tile")
    index = lax.axis_index("tile")
    own = consensus[0]
    dual = duals[0, 0]
    probe = probes[0]
    amps = amplitudes[0, 0]
    measured = ((SLOTS, PS, PS), bf16)

    rounded = own.astype(bf16)
    below = [shifted(rounded[:, :OVER, j * L : (j + 1) * L], -1, 0) for j in range(2)]
    right = shifted(rounded[:, :, :OVER], 0, -1)
    below.append(shifted(below[0], 0, -1))

    height = n // TGW
    two = height == 2
    row, col = index // TGW, index % TGW
    flags = [col > 0, col < TGW - 1, row > 0, row < height - 1]
    flags = flags + [index % 2 == 1] + [col < 0] * 3
    flags = jnp.broadcast_to(jnp.stack(flags).astype(f32)[:, None], (8, L))
    meta = jnp.concatenate(
        [offsets[0, 0].reshape(COUNT), counts[0], jnp.zeros((META - COUNT - 1,), jnp.int32)]
    )
    _, meta = lax.optimization_barrier((rounded, meta))
    column = [meta, shifted(meta, 1, 0)] + ([] if two else [shifted(meta, -1, 0)])
    column = jnp.stack(column)
    metas = [column, shifted(column, 0, 1), shifted(column, 0, -1)]

    inputs = (own, dual, probe, amps, fwd, bwd)
    staged = call(
        stage, "stage", [WIDE, WIDE, PLANES], [None, PLANES, PLANES], 0, 3, 3, held=True
    )(own, dual, probe)
    staged = [pinned(v) for v in staged]
    rim = ((2, OVER, L), bf16)
    ext, acc, pnum, side, inner, *mids = call(
        functools.partial(first_pass, two), "first_pass",
        [WIDE, WIDE, SUMS, ((2, SPAN, L), bf16), ((2, SPAN, L), bf16)] + [rim] * (1 if two else 2),
        [TABLE, TABLE, measured, None] + WORK, 1, 6, 3, aliases={6: 0, 7: 1}, flops=PASS,
    )(meta, flags, right, *below, *staged, fwd, bwd, amps, *metas)
    side = swapped(side, "tile", 1)
    inner = inner_swapped(inner)

    def down_and_up(rims):
        down = shifted(rims[0], 1, 0)
        return down, down if two else shifted(rims[1], -1, 0)

    mid_above, mid_below = down_and_up(mids)
    rims = call(
        functools.partial(between, two), "between", [((2, 2, OVER, L), bf16)] * (1 if two else 2)
    )(flags, acc, side, inner, pnum, right, *below, mid_above, mid_below)
    from_above, from_below = down_and_up(rims)
    weight, *inputs = call(
        functools.partial(weigh, two), "weigh",
        [((3, SPAN, L), f32), PLANES, PLANES, PLANES, measured, TABLE, TABLE],
        [None, ((2, PS, L), f32), ((3, SPAN + 2 * OVER, L), f32), pltpu.SMEM((8, L), f32)],
        len(metas), 7, 7, held=True,
    )(*metas, rims[0], acc, side, inner, pnum, right, *below, mid_above, mid_below, flags, *inputs)
    weight, *inputs = [pinned(v) for v in (weight, *inputs)]

    base, shrink, to_right, rim, to_below, pnum, to_swap = call(
        second_pass, "second_pass",
        [PLANES, ((2, TS, L), f32), ((2, SPAN, L), bf16), ((2, OVER, L), f32), ((2, OVER, L), bf16),
         SUMS, ((3, PS // 2, PS), bf16)],
        [PLANES, WIDE, WIDE] + WORK, 1, flops=PASS,
    )(meta, flags, right, *below, acc, side, inner, mid_above, mid_below, from_above,
      from_below, weight, pnum, *inputs)
    from_left = shifted(to_right, 0, 1)
    above1 = shifted(to_below, 1, 0)
    (to_below,) = call(add_rim, "add_rim", [((2, OVER, L), bf16)])(flags, rim, from_left, base, shrink)
    above0 = shifted(to_below, 1, 0)

    eight = n == 8
    half = [((3, PS // 2, PS), bf16)]
    if eight:
        (sums,) = call(halve, "halve", half)(flags, pnum, swapped(to_swap, "tile", 1), base, shrink)
        came = swapped(sums, "tile", 2)
    combined, *parts = call(
        finish_estimate, "finish_estimate", [PLANES] + [((2, TS // 2, TS), bf16)] * 2
    )(flags, base, shrink, from_left, above0, above1, *([sums] if eight else []))
    if eight:
        (sums,) = call(add, "add", half)(sums, came, parts[0])
        came = swapped(sums, "tile", 4)
    pairs = scan_sums(parts)
    if eight:
        (change,) = call(update, "update", [((2, PS // 2, PS), bf16)])(sums, came, pairs[1])
    settled, dual_new = call(
        functools.partial(settle, lax.axis_size("scan")), "settle", [PLANES] * 2
    )(*pairs, combined)
    if eight:
        change = doubled(index, change, 1).astype(f32)
    else:
        total = lax.psum(pnum, "tile")
        change = probe_step * total[0:2] / jnp.sqrt(total[2] + 1.0)
    probe_new = probe + change
    return (settled[None], dual_new[None, None], probe_new[None])


def solution(mesh):
    placed = (
        P("tile", None, None, None),
        P("scan", "tile", None, None, None),
        P("scan", None, None, None),
        P("scan", "tile", None, None, None),
        P("scan", "tile", None, None),
        P("scan", "tile"),
    )
    return jax.shard_map(
        shards,
        mesh=mesh,
        in_specs=placed,
        out_specs=(
            P("tile", None, None, None),
            P("scan", "tile", None, None, None),
            P("scan", None, None, None),
        ),
        check_vma=False,
    )
```

```python
import functools
import math

import jax
import jax.numpy as jnp
import ml_dtypes
import numpy as np
from jax import lax
from jax.experimental import pallas as pl
from jax.experimental.pallas import tpu as pltpu
from jax.sharding import PartitionSpec as P

PS = 256
TS = 256
OVER = 128
TGW = 4
SLOTS = 4
SPAN = TS + OVER
L = 128
CH = 32
COUNT = 2 * SLOTS
CARD = 16
HAS_LEFT, HAS_RIGHT, HAS_ABOVE, HAS_BELOW, ODD = range(5)

penalty = 0.5
smoothing = 0.05
probe_step = 3.0

f32 = jnp.float32
bf16 = jnp.bfloat16


def dft_tables():
    indices = np.arange(PS, dtype=np.int32)
    phase_index = indices[:, None] * indices[None, :] % PS
    angles = phase_index.astype(np.float32) * np.float32(2.0 * math.pi / PS)
    scale = np.float32(1.0 / math.sqrt(PS))
    re = (np.cos(angles) * scale).astype(ml_dtypes.bfloat16)
    im = (-np.sin(angles) * scale).astype(ml_dtypes.bfloat16)
    fwd = np.block([[re, -im], [im, re]])
    bwd = np.block([[re, im], [-im, re]])
    return jnp.asarray(fwd), jnp.asarray(bwd)


def shifted(value, rows, cols):
    height = lax.axis_size("tile") // TGW
    pairs = []
    for i in range(height * TGW):
        r, c = divmod(i, TGW)
        pairs.append((i, (r + rows) % height * TGW + (c + cols) % TGW))
    return lax.ppermute(value, "tile", pairs)


def swapped(value, axis, bit):
    n = lax.axis_size(axis)
    return lax.ppermute(value, axis, [(i, i ^ bit) for i in range(n)])


def is_power(n):
    return n & (n - 1) == 0


def inner_swapped(value):
    n = lax.axis_size("tile")
    return lax.ppermute(value, "tile", [(i, i ^ 3 if i % TGW in (1, 2) else i) for i in range(n)])


def scan_sums(parts):
    n = lax.axis_size("scan")
    if not is_power(n):
        return [v for part in parts for v in (lax.psum(part, "scan"), jnp.zeros_like(part))]
    bits = [1 << k for k in range(n.bit_length() - 1)]
    for k in range(len(bits)):
        came = [swapped(parts[p], "scan", bits[(k + p) % len(bits)]) for p in range(2)]
        pairs = [parts[0], came[0], parts[1], came[1]]
        if k < len(bits) - 1:
            outs = [(parts[0].shape, bf16)] * 2
            parts = call(mix, f"mix{k}", outs)(*pairs)
    return pairs


def doubled(index, change, bit):
    other = swapped(change, "tile", bit)
    return jnp.where(
        (index // bit) % 2 == 1,
        jnp.concatenate([other, change], 1),
        jnp.concatenate([change, other], 1),
    )


def lane_pull(blocks, c):
    lane = lax.broadcasted_iota(jnp.int32, blocks[0].shape, 1)
    keep = lane < L - c
    r = [pltpu.roll(v, (L - c) % L, 1) for v in blocks]
    return jnp.concatenate([jnp.where(keep, r[0], r[1]), jnp.where(keep, r[1], r[2])], 1)


def lane_push(blocks, c):
    lane = lax.broadcasted_iota(jnp.int32, blocks[0].shape, 1)
    past = lane >= c
    r = [pltpu.roll(v, c % L, 1) for v in blocks]
    z = jnp.zeros_like(r[0])
    return [jnp.where(past, r[0], z), jnp.where(past, r[1], r[0]), jnp.where(past, z, r[1])]


def visit_pair(p, meta, ext, probe, amps, fwd, bwd, acc, pnum, win, X, Y, W):
    N = PS
    used = jnp.where(2 * p + 1 < meta[COUNT], 1.0, 0.0).astype(f32)
    corners = [(meta[4 * p + 2 * i], meta[4 * p + 2 * i + 1]) for i in range(2)]

    def leave(i):
        r, c = corners[i]
        for k in range(0, N, CH):
            rows = slice(k, k + CH)
            w = [
                lane_pull([ext[ch, j, pl.ds(r + k, CH), :] for j in range(3)], c) for ch in range(2)
            ]
            if i == 1:
                w = [v * used for v in w]
            pr, pi = probe[0, rows, :], probe[1, rows, :]
            win[i, 0, rows, :] = w[0]
            win[i, 1, rows, :] = w[1]
            X[i, rows, :] = (pr * w[0] - pi * w[1]).astype(bf16)
            X[i, N + k : N + k + CH, :] = (pr * w[1] + pi * w[0]).astype(bf16)
            pnum[2, rows, :] += w[0] * w[0] + w[1] * w[1]

    def columns(i, table):
        t = jnp.dot(table[...], X[i], preferred_element_type=f32)
        Y[i, :, :N] = t[:N].astype(bf16)
        Y[i, :, N:] = t[N:].astype(bf16)

    def rows_of(i, table):
        W[i] = jnp.dot(Y[i], table[...], preferred_element_type=f32)

    def compare(i):
        for k in range(0, N, CH):
            wr, wi = W[i, k : k + CH, :N], W[i, k : k + CH, N:]
            a = amps[2 * p + i, k : k + CH, :].astype(f32)
            f = a * lax.rsqrt(wr * wr + wi * wi + smoothing) - 1.0
            X[i, k : k + CH, :] = (wr * f).astype(bf16)
            X[i, N + k : N + k + CH, :] = (wi * f).astype(bf16)

    def gather(i):
        r, c = corners[i]
        for k in range(0, N, CH):
            rows = slice(k, k + CH)
            br, bi = W[i, rows, :N], W[i, rows, N:]
            pr, pi = probe[0, rows, :], probe[1, rows, :]
            wr, wi = win[i, 0, rows, :], win[i, 1, rows, :]
            pnum[0, rows, :] += wr * br + wi * bi
            pnum[1, rows, :] += wr * bi - wi * br
            for ch, v in enumerate((pr * br + pi * bi, pr * bi - pi * br)):
                for j, u in enumerate(lane_push([v[:, :L], v[:, L:]], c)):
                    acc[ch, j, pl.ds(r + k, CH), :] += u

    leave(0)
    columns(0, fwd)
    leave(1)
    rows_of(0, bwd)
    columns(1, fwd)
    compare(0)
    rows_of(1, bwd)
    columns(0, bwd)
    compare(1)
    rows_of(0, fwd)
    columns(1, bwd)
    gather(0)
    rows_of(1, fwd)
    gather(1)


def fetch(pairs, sems):
    copies = [pltpu.make_async_copy(src, dst, sems.at[i]) for i, (src, dst) in enumerate(pairs)]
    for copy in copies:
        copy.start()
    return copies


def stage(own_h, dual_h, probe_h, ext, acc, probe, sems, own, dual):
    copies = fetch([(own_h, own), (dual_h, dual), (probe_h, probe)], sems)
    acc[:, 2] = jnp.zeros((2, SPAN, L), f32)
    copies[0].wait()
    for j in range(2):
        cols = slice(j * L, (j + 1) * L)
        acc[:, j, TS:, :] = jnp.zeros((2, OVER, L), f32)
        ext[:, j, :TS, :] = own[:, :, cols].astype(bf16).astype(f32)
    copies[1].wait()
    for j in range(2):
        cols = slice(j * L, (j + 1) * L)
        acc[:, j, :TS, :] = -penalty * dual[:, :, cols]
    copies[2].wait()


def first_pass(
    two, meta, flags, right, below0, below1, diag, ext0, acc0, probe, *rest,
):
    *cards, fwd_h, bwd_h, amps_h = rest[: 4 if two else 5]
    ext, acc, pnum, side, inner, *mids, fwd, bwd, amps, sems, win, X, Y, W = rest[4 if two else 5 :]
    copies = fetch([(fwd_h, fwd), (bwd_h, bwd), (amps_h, amps)], sems)
    has_right = flags[HAS_RIGHT : HAS_RIGHT + 1, :]
    has_below = flags[HAS_BELOW : HAS_BELOW + 1, :]
    ext[:, 2, :TS, :] = right[...].astype(f32) * has_right
    for ch in range(2):
        ext[ch, 2, TS:, :] = diag[plane(ch, OVER), :].astype(f32) * (has_right * has_below)
    for j in range(2):
        for ch in range(2):
            ext[ch, j, TS:, :] = (below0, below1)[j][plane(ch, OVER), :].astype(f32) * has_below
    pnum[...] = jnp.zeros_like(pnum)
    for copy in copies:
        copy.wait()

    @pl.loop(0, (meta[COUNT] + 1) // 2)
    def _(p):
        visit_pair(p, meta, ext, probe, amps, fwd, bwd, acc, pnum, win, X, Y, W)

    odd = flags[ODD : ODD + 1, :] > 0.0
    column = [card[...] for card in cards] + [below1[2 * OVER :, :]]
    side[2 * SPAN :, :] = jnp.concatenate(column, 0)
    inner[2 * SPAN :, :] = jnp.concatenate(column, 0)
    for ch in range(2):
        side[plane(ch, SPAN), :] = jnp.where(odd, acc[ch, 0], acc[ch, 2]).astype(bf16)
        inner[plane(ch, SPAN), :] = jnp.where(odd, acc[ch, 2], acc[ch, 0]).astype(bf16)
        for rim, mid in zip(rims_of(two, flags, lambda rows: acc[ch, 1, rows, :]), mids):
            mid[ch] = rim.astype(bf16)


def plane(ch, rows, start=0, count=None):
    return slice(ch * rows + start, ch * rows + start + (rows if count is None else count))


def rims_of(two, flags, get):
    down, up = get(slice(TS, SPAN)), get(slice(0, OVER))
    return [jnp.where(flags[HAS_BELOW : HAS_BELOW + 1, :] > 0.0, down, up)] if two else [down, up]


def from_sides(flags, side, inner):
    odd = flags[ODD : ODD + 1, :] > 0.0
    valid = flags[HAS_LEFT : HAS_LEFT + 1, :] * flags[HAS_RIGHT : HAS_RIGHT + 1, :]
    side, inner = side.astype(f32), inner.astype(f32) * valid
    return jnp.where(odd, side, inner), jnp.where(odd, inner, side)


def between(two, flags, acc, side, inner, *rest):
    outs = rest[-1:] if two else rest[-2:]
    for ch in range(2):
        for at in range(2):

            def total(rows):
                where = plane(ch, SPAN, rows.start, OVER)
                came = from_sides(flags, side[where, :], inner[where, :])[at]
                return acc[ch, 2 * at, rows, :] + came

            for rim, out in zip(rims_of(two, flags, total), outs):
                out[ch, at] = rim.astype(bf16)


def weigh(two, *rest):
    *cards, flags, side, inner = rest[: 4 if two else 5]
    below1, *sources = rest[-19:-12]
    weight, *targets, sems, p2, buf, held, table = rest[-12:]
    copies = fetch(list(zip(sources, targets)), sems)
    probe = targets[2]
    last = 2 * OVER
    blocks = [card[...].astype(f32) for card in cards] + [below1[last:, :].astype(f32)]
    for k, block in enumerate(blocks):
        held[k : k + 1, :] = block[:1]
        at = 2 * SPAN + k * CARD
        odd = flags[ODD : ODD + 1, :] > 0.0
        by_side, by_inner = [v[at : at + CARD, :].astype(f32)[:1] for v in (side, inner)]
        held[4 + k : 5 + k, :] = jnp.where(odd, by_side, by_inner)
        held[8 + k : 9 + k, :] = jnp.where(odd, by_inner, by_side)
    held[16:24, :] = flags[...]
    moved = pltpu.make_async_copy(held, table, sems.at[6])
    moved.start()
    buf[...] = jnp.zeros_like(buf)
    copies[2].wait()
    for j in range(2):
        cols = slice(j * L, (j + 1) * L)
        p2[j] = probe[0, :, cols] * probe[0, :, cols] + probe[1, :, cols] * probe[1, :, cols]
    moved.wait()
    for dr in (-1, 0, 1):
        for dc in (-1, 0, 1):
            at_row = {0: 0, -1: 4, 1: 8}[dc] + {0: 0, -1: 1, 1: 1 if two else 2}[dr]
            first, rows = {-1: (OVER, OVER), 0: (0, PS), 1: (0, OVER)}[dr]
            base = {-1: 0, 0: OVER, 1: OVER + TS}[dr]
            count = table[at_row, COUNT].astype(jnp.int32)
            for flag, at, step in (
                (HAS_ABOVE, -1, dr), (HAS_BELOW, 1, dr), (HAS_LEFT, -1, dc), (HAS_RIGHT, 1, dc)
            ):
                if step == at:
                    count = jnp.where(table[16 + flag, 0] > 0.0, count, 0)

            @pl.loop(0, count)
            def _(s, at_row=at_row, dc=dc, first=first, rows=rows, base=base):
                r, c = [table[at_row, 2 * s + i].astype(jnp.int32) for i in range(2)]
                for k in range(0, rows, 64):
                    at = pl.ds(base + r + k, 64)
                    v = [p2[j, first + k : first + k + 64, :] for j in range(2)]
                    lane = lax.broadcasted_iota(jnp.int32, v[0].shape, 1)
                    if dc == 0:
                        for j, u in enumerate(lane_push(v, c)):
                            buf[j, at, :] += u
                    elif dc < 0:
                        buf[0, at, :] += jnp.where(lane < c, pltpu.roll(v[1], c % L, 1), 0.0)
                    else:
                        buf[2, at, :] += jnp.where(lane >= c, pltpu.roll(v[0], c % L, 1), 0.0)

    weight[...] = buf[:, OVER : OVER + SPAN, :]
    for k, copy in enumerate(copies):
        if k != 2:
            copy.wait()


def second_pass(
    meta, flags, right, below0, below1, diag, acc1, side, inner, mid_above, mid_below, from_above, from_below,
    weight, pnum1, own, dual, probe, amps, fwd, bwd,
    base, shrink, to_right, lower, to_below, pnum, to_swap,
    partial, ext, acc, win, X, Y, W,
):
    has_right = flags[HAS_RIGHT : HAS_RIGHT + 1, :]
    has_below = flags[HAS_BELOW : HAS_BELOW + 1, :]
    has_above = flags[HAS_ABOVE : HAS_ABOVE + 1, :]
    acc[...] = jnp.zeros_like(acc)
    pnum[...] = pnum1[...]
    for ch in range(2):
        for j in range(3):
            cols = slice(j * L, (j + 1) * L)
            for k in range(0, SPAN, 64):
                rows = slice(k, k + 64)
                total = acc1[ch, j, rows, :]
                if j != 1:
                    at = plane(ch, SPAN, k, 64)
                    total = total + from_sides(flags, side[at, :], inner[at, :])[j // 2]
                if k < OVER:
                    came = mid_above[ch, rows, :] if j == 1 else from_above[ch, j // 2, rows, :]
                    total = total + came.astype(f32) * has_above
                if k >= TS:
                    rim = slice(k - TS, k - TS + 64)
                    came = mid_below[ch, rim, :] if j == 1 else from_below[ch, j // 2, rim, :]
                    total = total + came.astype(f32)
                step = total / (weight[j, rows, :] + penalty)
                if j < 2 and k < TS:
                    est = own[ch, rows, cols] + step
                    partial[ch, rows, cols] = est
                else:
                    if k < TS:
                        est = right[ch, rows, :].astype(f32) + step
                    elif j < 2:
                        est = (below0, below1)[j][plane(ch, OVER, k - TS, 64), :].astype(f32) + step
                    else:
                        est = diag[plane(ch, OVER, k - TS, 64), :].astype(f32) + step
                    if j == 2:
                        est = est * has_right
                    if k >= TS:
                        est = est * has_below
                ext[ch, j, rows, :] = est.astype(bf16).astype(f32)

    @pl.loop(0, (meta[COUNT] + 1) // 2)
    def _(p):
        visit_pair(p, meta, ext, probe, amps, fwd, bwd, acc, pnum, win, X, Y, W)

    to_right[...] = acc[:, 2].astype(bf16)
    to_below[...] = acc[:, 1, TS:, :].astype(bf16)
    lower[...] = acc[:, 0, TS:, :]
    odd = flags[ODD : ODD + 1, :1] > 0.0
    for ch in range(3):
        lo, hi = pnum[ch, : PS // 2, :], pnum[ch, PS // 2 :, :]
        to_swap[ch] = jnp.where(odd, lo, hi).astype(bf16)
    for j in range(2):
        cols = slice(j * L, (j + 1) * L)
        for k in range(0, TS, 64):
            rows = slice(k, k + 64)
            over = 1.0 / (weight[j, rows, :] + penalty)
            shrink[j, rows, :] = over
            for ch in range(2):
                est = partial[ch, rows, cols]
                held = dual[ch, rows, cols]
                pull = penalty * (own[ch, rows, cols] - held - est)
                base[ch, rows, cols] = est + held + (acc[ch, j, rows, :] + pull) * over


def halve(flags, sums, came, *rest):
    odd = flags[ODD : ODD + 1, :1] > 0.0
    for ch in range(3):
        lo, hi = sums[ch, : PS // 2, :], sums[ch, PS // 2 :, :]
        rest[-1][ch] = (jnp.where(odd, hi, lo) + came[ch].astype(f32)).astype(bf16)


def add(held, came, *rest):
    for ch in range(3):
        rest[-1][ch] = (held[ch].astype(f32) + came[ch].astype(f32)).astype(bf16)


def add_rim(flags, rim, from_left, *rest):
    has_left = flags[HAS_LEFT : HAS_LEFT + 1, :]
    for ch in range(2):
        rest[-1][ch] = (rim[ch] + from_left[ch, TS:, :].astype(f32) * has_left).astype(bf16)


def finish_estimate(flags, base, shrink, from_left, above0, above1, *rest):
    combined, parts = rest[-3], rest[-2:]
    has_left = flags[HAS_LEFT : HAS_LEFT + 1, :]
    has_above = flags[HAS_ABOVE : HAS_ABOVE + 1, :]
    for ch in range(2):
        for j in range(2):
            cols = slice(j * L, (j + 1) * L)
            for k in range(0, TS, 64):
                rows = slice(k, k + 64)
                total = base[ch, rows, cols]
                came = None
                if j == 0:
                    came = from_left[ch, rows, :].astype(f32) * has_left
                if k < OVER:
                    above = (above0, above1)[j][ch, rows, :].astype(f32) * has_above
                    came = above if came is None else came + above
                if came is not None:
                    total = total + came * shrink[j, rows, :]
                combined[ch, rows, cols] = total
                part = slice(k % (TS // 2), k % (TS // 2) + 64)
                parts[k // (TS // 2)][ch, part, cols] = total.astype(bf16)


def mixed(first, first_came, second, second_came, outs):
    for out, part, came in ((outs[0], first, first_came), (outs[1], second, second_came)):
        for ch in range(2):
            out[ch] = (part[ch].astype(f32) + came[ch].astype(f32)).astype(bf16)


def mix(*refs):
    mixed(*refs[:4], refs[-2:])


def update(held, came, *rest):
    total = [held[ch].astype(f32) + came[ch].astype(f32) for ch in range(3)]
    over = probe_step * lax.rsqrt(total[2] + 1.0)
    for ch in range(2):
        rest[-1][ch] = (total[ch] * over).astype(bf16)


def settle(groups, first, first_came, second, second_came, combined, *rest):
    settled, dual_new = rest[-2:]
    for k in range(0, TS, CH):
        rows = slice(k, k + CH)
        part, came = (first, first_came) if k < TS // 2 else (second, second_came)
        at = slice(k % (TS // 2), k % (TS // 2) + CH)
        re, im = [
            (part[ch, at, :].astype(f32) + came[ch, at, :].astype(f32)) * (1.0 / groups)
            for ch in range(2)
        ]
        over = 1.0 / jnp.maximum(jnp.sqrt(re * re + im * im), 1.0)
        re, im = re * over, im * over
        settled[0, rows, :] = re
        settled[1, rows, :] = im
        dual_new[0, rows, :] = combined[0, rows, :] - re
        dual_new[1, rows, :] = combined[1, rows, :] - im


V = pl.BlockSpec(memory_space=pltpu.VMEM)
S = pl.BlockSpec(memory_space=pltpu.SMEM)
H = pl.BlockSpec(memory_space=pltpu.HBM)


def pinned(value):
    return pltpu.with_memory_space_constraint(value, pltpu.VMEM)


def call(body, name, outs, scratch=(), scalars=0, far=0, copies=0, aliases=None, held=False, flops=0):
    def run(*operands):
        near = len(operands) - scalars - far
        spaces = [None] * (scalars + near) + [pltpu.HBM] * far
        operands = [
            v if space is None else pltpu.with_memory_space_constraint(v, space)
            for v, space in zip(operands, spaces)
        ]
        return pl.pallas_call(
            body,
            in_specs=[S] * scalars + [V] * near + [H] * far,
            out_specs=[V] * len(outs),
            out_shape=[
                pltpu.VMEM(shape, dtype) if held else jax.ShapeDtypeStruct(shape, dtype)
                for shape, dtype in outs
            ],
            scratch_shapes=[
                pltpu.SemaphoreType.DMA((copies,)) if one is None else pltpu.VMEM(*one)
                if isinstance(one, tuple) else one
                for one in scratch
            ],
            input_output_aliases=aliases or {},
            cost_estimate=pl.CostEstimate(
                flops=flops or sum(math.prod(shape) for shape, _ in outs),
                bytes_accessed=sum(v.size * v.dtype.itemsize for v in operands[scalars + near :]),
                transcendentals=0,
            ),
            compiler_params=pltpu.CompilerParams(vmem_limit_bytes=24 * 2**20),
            name=name,
        )(*operands)

    return run


PLANES = ((2, PS, PS), f32)
PASS = SLOTS * 4 * 8 * PS**3
WORK = [
    ((2, 2, PS, PS), f32),
    ((2, 2 * PS, PS), bf16),
    ((2, PS, 2 * PS), bf16),
    ((2, PS, 2 * PS), f32),
]
TABLE = ((2 * PS, 2 * PS), bf16)
WIDE = ((2, 3, SPAN, L), f32)
SUMS = ((3, PS, PS), f32)


def shards(consensus, duals, probes, amplitudes, offsets, counts):
    fwd, bwd = dft_tables()
    n = lax.axis_size("tile")
    index = lax.axis_index("tile")
    own = consensus[0]
    dual = duals[0, 0]
    probe = probes[0]
    amps = amplitudes[0, 0]
    measured = ((SLOTS, PS, PS), bf16)

    rounded = own.astype(bf16)
    height = n // TGW
    two = height == 2
    row, col = index // TGW, index % TGW
    flags = [col > 0, col < TGW - 1, row > 0, row < height - 1]
    flags = flags + [index % 2 == 1] + [col < 0] * 3
    flags = jnp.broadcast_to(jnp.stack(flags).astype(f32)[:, None], (8, L))
    meta = jnp.concatenate([offsets[0, 0].reshape(COUNT), counts[0]])
    card = jnp.pad(meta.astype(bf16)[None], ((0, CARD - 1), (0, L - COUNT - 1)))

    sent = [rounded[:, :OVER, j * L : (j + 1) * L].reshape(2 * OVER, L) for j in range(2)]
    below = [shifted(sent[0], -1, 0), shifted(jnp.concatenate([sent[1], card]), -1, 0)]
    right = shifted(rounded[:, :, :OVER], 0, -1)
    below.append(shifted(below[0], 0, -1))
    cards = [card] if two else [card, shifted(card, 1, 0)]

    inputs = (own, dual, probe, amps, fwd, bwd)
    staged = call(
        stage, "stage", [WIDE, WIDE, PLANES], [None, PLANES, PLANES], 0, 3, 3, held=True
    )(own, dual, probe)
    staged = [pinned(v) for v in staged]
    rim = ((2, OVER, L), bf16)
    ext, acc, pnum, side, inner, *mids = call(
        functools.partial(first_pass, two), "first_pass",
        [WIDE, WIDE, SUMS] + [((2 * SPAN + (len(cards) + 1) * CARD, L), bf16)] * 2
        + [rim] * (1 if two else 2),
        [TABLE, TABLE, measured, None] + WORK, 1, 3, 3, aliases={6: 0, 7: 1}, flops=PASS,
    )(meta, flags, right, *below, *staged, *cards, fwd, bwd, amps)
    side = swapped(side, "tile", 1)
    inner = inner_swapped(inner)

    def down_and_up(rims):
        down = shifted(rims[0], 1, 0)
        return down, down if two else shifted(rims[1], -1, 0)

    mid_above, mid_below = down_and_up(mids)
    rims = call(
        functools.partial(between, two), "between", [((2, 2, OVER, L), bf16)] * (1 if two else 2)
    )(flags, acc, side, inner, pnum, right, *below, mid_above, mid_below)
    from_above, from_below = down_and_up(rims)
    weight, *inputs = call(
        functools.partial(weigh, two), "weigh",
        [((3, SPAN, L), f32), PLANES, PLANES, PLANES, measured, TABLE, TABLE],
        [None, ((2, PS, L), f32), ((3, SPAN + 2 * OVER, L), f32), ((24, L), f32),
         pltpu.SMEM((24, L), f32)],
        0, 6, 7, held=True,
    )(*cards, flags, side, inner, rims[0], acc, pnum, right, below[0], below[2], mid_above, mid_below,
      below[1], *inputs)
    weight, *inputs = [pinned(v) for v in (weight, *inputs)]

    base, shrink, to_right, rim, to_below, pnum, to_swap = call(
        second_pass, "second_pass",
        [PLANES, ((2, TS, L), f32), ((2, SPAN, L), bf16), ((2, OVER, L), f32), ((2, OVER, L), bf16),
         SUMS, ((3, PS // 2, PS), bf16)],
        [PLANES, WIDE, WIDE] + WORK, 1, flops=PASS,
    )(meta, flags, right, *below, acc, side, inner, mid_above, mid_below, from_above,
      from_below, weight, pnum, *inputs)
    from_left = shifted(to_right, 0, 1)
    above1 = shifted(to_below, 1, 0)
    (to_below,) = call(add_rim, "add_rim", [((2, OVER, L), bf16)])(flags, rim, from_left, base, shrink)
    above0 = shifted(to_below, 1, 0)

    eight = n == 8
    half = [((3, PS // 2, PS), bf16)]
    if eight:
        (sums,) = call(halve, "halve", half)(flags, pnum, swapped(to_swap, "tile", 1), base, shrink)
        came = swapped(sums, "tile", 2)
    combined, *parts = call(
        finish_estimate, "finish_estimate", [PLANES] + [((2, TS // 2, TS), bf16)] * 2
    )(flags, base, shrink, from_left, above0, above1, *([sums] if eight else []))
    if eight:
        (sums,) = call(add, "add", half)(sums, came, parts[0])
        came = swapped(sums, "tile", 6)
    pairs = scan_sums(parts)
    if eight:
        (change,) = call(update, "update", [((2, PS // 2, PS), bf16)])(sums, came, pairs[1])
    settled, dual_new = call(
        functools.partial(settle, lax.axis_size("scan")), "settle", [PLANES] * 2
    )(*pairs, combined)
    if eight:
        change = doubled(index, change, 1).astype(f32)
    else:
        total = lax.psum(pnum, "tile")
        change = probe_step * total[0:2] / jnp.sqrt(total[2] + 1.0)
    probe_new = probe + change
    return (settled[None], dual_new[None, None], probe_new[None])


def solution(mesh):
    placed = (
        P("tile", None, None, None),
        P("scan", "tile", None, None, None),
        P("scan", None, None, None),
        P("scan", "tile", None, None, None),
        P("scan", "tile", None, None),
        P("scan", "tile"),
    )
    return jax.shard_map(
        shards,
        mesh=mesh,
        in_specs=placed,
        out_specs=(
            P("tile", None, None, None),
            P("scan", "tile", None, None, None),
            P("scan", None, None, None),
        ),
        check_vma=False,
    )
```

```python
import functools
import math

import jax
import jax.numpy as jnp
import ml_dtypes
import numpy as np
from jax import lax
from jax.experimental import pallas as pl
from jax.experimental.pallas import tpu as pltpu
from jax.sharding import PartitionSpec as P

PS = 256
TS = 256
OVER = 128
TGW = 4
SLOTS = 4
SPAN = TS + OVER
L = 128
HALF = PS // 2
CH = 32
COUNT = 2 * SLOTS
CARD = 16
HAS_LEFT, HAS_RIGHT, HAS_ABOVE, HAS_BELOW, ODD = range(5)

penalty = 0.5
smoothing = 0.05
probe_step = 3.0

f32 = jnp.float32
bf16 = jnp.bfloat16


def dft_tables():
    indices = np.arange(PS, dtype=np.int32)
    phase_index = indices[:, None] * indices[None, :] % PS
    angles = phase_index.astype(np.float32) * np.float32(2.0 * math.pi / PS)
    scale = np.float32(1.0 / math.sqrt(PS))
    re = (np.cos(angles) * scale).astype(ml_dtypes.bfloat16)
    im = (-np.sin(angles) * scale).astype(ml_dtypes.bfloat16)
    half = np.concatenate([re[:HALF], re[HALF : HALF + 1], im[1:HALF]])
    order = np.concatenate([indices[: HALF + 1], indices[:HALF:-1]])
    return jnp.asarray(half), jnp.asarray(half.T), jnp.asarray(np.eye(PS, dtype=half.dtype)[order])


def shifted(value, rows, cols):
    height = lax.axis_size("tile") // TGW
    pairs = []
    for i in range(height * TGW):
        r, c = divmod(i, TGW)
        pairs.append((i, (r + rows) % height * TGW + (c + cols) % TGW))
    return lax.ppermute(value, "tile", pairs)


def swapped(value, axis, bit):
    n = lax.axis_size(axis)
    return lax.ppermute(value, axis, [(i, i ^ bit) for i in range(n)])


def is_power(n):
    return n & (n - 1) == 0


def inner_swapped(value):
    n = lax.axis_size("tile")
    return lax.ppermute(value, "tile", [(i, i ^ 3 if i % TGW in (1, 2) else i) for i in range(n)])


def scan_sums(parts):
    n = lax.axis_size("scan")
    if not is_power(n):
        return [v for part in parts for v in (lax.psum(part, "scan"), jnp.zeros_like(part))]
    bits = [1 << k for k in range(n.bit_length() - 1)]
    for k in range(len(bits)):
        came = [swapped(parts[p], "scan", bits[(k + p) % len(bits)]) for p in range(2)]
        pairs = [parts[0], came[0], parts[1], came[1]]
        if k < len(bits) - 1:
            outs = [(parts[0].shape, bf16)] * 2
            parts = call(mix, f"mix{k}", outs)(*pairs)
    return pairs


def doubled(index, change, bit):
    other = swapped(change, "tile", bit)
    return jnp.where(
        (index // bit) % 2 == 1,
        jnp.concatenate([other, change], 1),
        jnp.concatenate([change, other], 1),
    )


def lane_pull(blocks, c):
    lane = lax.broadcasted_iota(jnp.int32, blocks[0].shape, 1)
    keep = lane < L - c
    r = [pltpu.roll(v, (L - c) % L, 1) for v in blocks]
    return jnp.concatenate([jnp.where(keep, r[0], r[1]), jnp.where(keep, r[1], r[2])], 1)


def lane_push(blocks, c):
    lane = lax.broadcasted_iota(jnp.int32, blocks[0].shape, 1)
    past = lane >= c
    r = [pltpu.roll(v, c % L, 1) for v in blocks]
    z = jnp.zeros_like(r[0])
    return [jnp.where(past, r[0], z), jnp.where(past, r[1], r[0]), jnp.where(past, z, r[1])]


def split(pr, pi, qr, qi, first):
    planes = (pr - qi, pr + qi, pi + qr, pi - qr)
    if first is None:
        return planes
    return [jnp.where(first, v, w) for v, w in zip((pr, qr, pi, qi), planes)]


def joined(lr, hr, li, hi, first):
    planes = (lr + hr, li - hi, li + hi, hr - lr)
    if first is None:
        return planes
    return [jnp.where(first, v, w) for v, w in zip((lr, hr, li, hi), planes)]


def visit_pair(p, meta, ext, probe, amps, half, turned, acc, pnum, win, X, Y, W):
    N = PS
    used = jnp.where(2 * p + 1 < meta[COUNT], 1.0, 0.0).astype(f32)
    corners = [(meta[4 * p + 2 * i], meta[4 * p + 2 * i + 1]) for i in range(2)]

    def leave(i):
        r, c = corners[i]
        for k in range(0, N, CH):
            rows = slice(k, k + CH)
            w = [
                lane_pull([ext[ch, j, pl.ds(r + k, CH), :] for j in range(3)], c) for ch in range(2)
            ]
            if i == 1:
                w = [v * used for v in w]
            pr, pi = probe[0, rows, :], probe[1, rows, :]
            win[i, 0, rows, :] = w[0]
            win[i, 1, rows, :] = w[1]
            X[i, rows, :N] = (pr * w[0] - pi * w[1]).astype(bf16)
            X[i, rows, N:] = (pr * w[1] + pi * w[0]).astype(bf16)
            pnum[2, rows, :] += w[0] * w[0] + w[1] * w[1]

    def columns(i):
        t = jnp.dot(half[...], X[i], preferred_element_type=f32)
        for k in range(0, HALF, CH):
            p, q = t[k : k + CH], t[HALF + k : HALF + k + CH]
            first = lax.broadcasted_iota(jnp.int32, (CH, N), 0) == 0 if k == 0 else None
            planes = split(p[:, :N], p[:, N:], q[:, :N], q[:, N:], first)
            for j, v in enumerate(planes):
                Y[i, j * HALF + k : j * HALF + k + CH, :] = v.astype(bf16)

    def rows_of(i):
        W[i] = jnp.dot(Y[i], turned[...], preferred_element_type=f32)

    def compare(i):
        first = lax.broadcasted_iota(jnp.int32, (CH, L), 1) == 0
        top = lax.broadcasted_iota(jnp.int32, (CH, N), 0) == 0
        for k in range(0, HALF, CH):
            resid = []
            for h in range(2):
                rows = slice(h * HALF + k, h * HALF + k + CH)
                at = slice(N + h * HALF + k, N + h * HALF + k + CH)
                planes = split(W[i, rows, :L], W[i, at, :L], W[i, rows, L:], W[i, at, L:], first)
                a = amps[2 * p + i, rows, :].astype(f32)
                wr = jnp.concatenate([planes[0], planes[1]], 1)
                wi = jnp.concatenate([planes[2], planes[3]], 1)
                f = a * lax.rsqrt(wr * wr + wi * wi + smoothing) - 1.0
                resid.append((wr * f, wi * f))
            (lr, li), (hr, hi) = resid
            for j, v in enumerate(joined(lr, hr, li, hi, top if k == 0 else None)):
                X[i, j % 2 * HALF + k : j % 2 * HALF + k + CH, j // 2 * N : j // 2 * N + N] = v.astype(bf16)

    def columns_back(i):
        t = jnp.dot(turned[...], X[i], preferred_element_type=f32)
        first = lax.broadcasted_iota(jnp.int32, (CH, L), 1) == 0
        for k in range(0, N, CH):
            v = t[k : k + CH]
            planes = joined(v[:, :L], v[:, L:N], v[:, N : N + L], v[:, N + L :], first)
            for j, v in enumerate(planes):
                at = j // 2 * N + k
                Y[i, at : at + CH, j % 2 * L : j % 2 * L + L] = v.astype(bf16)

    def rows_back(i):
        W[i] = jnp.dot(Y[i], half[...], preferred_element_type=f32)

    def gather(i):
        r, c = corners[i]
        for k in range(0, N, CH):
            rows = slice(k, k + CH)
            br, bi = W[i, rows, :], W[i, N + k : N + k + CH, :]
            pr, pi = probe[0, rows, :], probe[1, rows, :]
            wr, wi = win[i, 0, rows, :], win[i, 1, rows, :]
            pnum[0, rows, :] += wr * br + wi * bi
            pnum[1, rows, :] += wr * bi - wi * br
            for ch, v in enumerate((pr * br + pi * bi, pr * bi - pi * br)):
                for j, u in enumerate(lane_push([v[:, :L], v[:, L:]], c)):
                    acc[ch, j, pl.ds(r + k, CH), :] += u

    leave(0)
    columns(0)
    leave(1)
    rows_of(0)
    columns(1)
    compare(0)
    rows_of(1)
    columns_back(0)
    compare(1)
    rows_back(0)
    columns_back(1)
    gather(0)
    rows_back(1)
    gather(1)


def fetch(pairs, sems):
    copies = [pltpu.make_async_copy(src, dst, sems.at[i]) for i, (src, dst) in enumerate(pairs)]
    for copy in copies:
        copy.start()
    return copies


def stage(
    below, own_h, dual_h, probe_h, amps_h, order_h, ext, acc, probe, ordered, sems, own, dual, amps, order
):
    copies = fetch(
        [(own_h, own), (dual_h, dual), (probe_h, probe), (amps_h, amps), (order_h, order)], sems
    )
    acc[:, 2] = jnp.zeros((2, SPAN, L), f32)
    copies[0].wait()
    for j in range(2):
        cols = slice(j * L, (j + 1) * L)
        acc[:, j, TS:, :] = jnp.zeros((2, OVER, L), f32)
        ext[:, j, :TS, :] = own[:, :, cols].astype(bf16).astype(f32)
    copies[1].wait()
    for j in range(2):
        cols = slice(j * L, (j + 1) * L)
        acc[:, j, :TS, :] = -penalty * dual[:, :, cols]
    for copy in copies[2:]:
        copy.wait()
    for k in range(SLOTS):
        rows = jnp.dot(order[...], amps[k], preferred_element_type=f32).astype(bf16)
        ordered[k] = jnp.dot(rows, order[...], preferred_element_type=f32).astype(bf16)


def first_pass(
    two, meta, flags, right, below0, below1, diag, ext0, acc0, probe, *rest,
):
    *cards, fwd_h, bwd_h, amps_h = rest[: 4 if two else 5]
    ext, acc, pnum, side, inner, *mids, fwd, bwd, amps, sems, win, X, Y, W = rest[4 if two else 5 :]
    copies = fetch([(fwd_h, fwd), (bwd_h, bwd), (amps_h, amps)], sems)
    has_right = flags[HAS_RIGHT : HAS_RIGHT + 1, :]
    has_below = flags[HAS_BELOW : HAS_BELOW + 1, :]
    ext[:, 2, :TS, :] = right[...].astype(f32) * has_right
    for ch in range(2):
        ext[ch, 2, TS:, :] = diag[plane(ch, OVER), :].astype(f32) * (has_right * has_below)
    for j in range(2):
        for ch in range(2):
            ext[ch, j, TS:, :] = (below0, below1)[j][plane(ch, OVER), :].astype(f32) * has_below
    pnum[...] = jnp.zeros_like(pnum)
    for copy in copies:
        copy.wait()

    @pl.loop(0, (meta[COUNT] + 1) // 2)
    def _(p):
        visit_pair(p, meta, ext, probe, amps, fwd, bwd, acc, pnum, win, X, Y, W)

    odd = flags[ODD : ODD + 1, :] > 0.0
    column = [card[...] for card in cards] + [below1[2 * OVER :, :]]
    side[2 * SPAN :, :] = jnp.concatenate(column, 0)
    inner[2 * SPAN :, :] = jnp.concatenate(column, 0)
    for ch in range(2):
        side[plane(ch, SPAN), :] = jnp.where(odd, acc[ch, 0], acc[ch, 2]).astype(bf16)
        inner[plane(ch, SPAN), :] = jnp.where(odd, acc[ch, 2], acc[ch, 0]).astype(bf16)
        for rim, mid in zip(rims_of(two, flags, lambda rows: acc[ch, 1, rows, :]), mids):
            mid[ch] = rim.astype(bf16)


def plane(ch, rows, start=0, count=None):
    return slice(ch * rows + start, ch * rows + start + (rows if count is None else count))


def rims_of(two, flags, get):
    down, up = get(slice(TS, SPAN)), get(slice(0, OVER))
    return [jnp.where(flags[HAS_BELOW : HAS_BELOW + 1, :] > 0.0, down, up)] if two else [down, up]


def from_sides(flags, side, inner):
    odd = flags[ODD : ODD + 1, :] > 0.0
    valid = flags[HAS_LEFT : HAS_LEFT + 1, :] * flags[HAS_RIGHT : HAS_RIGHT + 1, :]
    side, inner = side.astype(f32), inner.astype(f32) * valid
    return jnp.where(odd, side, inner), jnp.where(odd, inner, side)


def between(two, flags, acc, side, inner, *rest):
    outs = rest[-1:] if two else rest[-2:]
    for ch in range(2):
        for at in range(2):

            def total(rows):
                where = plane(ch, SPAN, rows.start, OVER)
                came = from_sides(flags, side[where, :], inner[where, :])[at]
                return acc[ch, 2 * at, rows, :] + came

            for rim, out in zip(rims_of(two, flags, total), outs):
                out[ch, at] = rim.astype(bf16)


def weigh(two, *rest):
    *cards, flags, side, inner = rest[: 4 if two else 5]
    below1, *sources = rest[-19:-12]
    weight, *targets, sems, p2, buf, held, table = rest[-12:]
    copies = fetch(list(zip(sources, targets)), sems)
    probe = targets[2]
    last = 2 * OVER
    blocks = [card[...].astype(f32) for card in cards] + [below1[last:, :].astype(f32)]
    for k, block in enumerate(blocks):
        held[k : k + 1, :] = block[:1]
        at = 2 * SPAN + k * CARD
        odd = flags[ODD : ODD + 1, :] > 0.0
        by_side, by_inner = [v[at : at + CARD, :].astype(f32)[:1] for v in (side, inner)]
        held[4 + k : 5 + k, :] = jnp.where(odd, by_side, by_inner)
        held[8 + k : 9 + k, :] = jnp.where(odd, by_inner, by_side)
    held[16:24, :] = flags[...]
    moved = pltpu.make_async_copy(held, table, sems.at[6])
    moved.start()
    buf[...] = jnp.zeros_like(buf)
    copies[2].wait()
    for j in range(2):
        cols = slice(j * L, (j + 1) * L)
        p2[j] = probe[0, :, cols] * probe[0, :, cols] + probe[1, :, cols] * probe[1, :, cols]
    moved.wait()
    for dr in (-1, 0, 1):
        for dc in (-1, 0, 1):
            at_row = {0: 0, -1: 4, 1: 8}[dc] + {0: 0, -1: 1, 1: 1 if two else 2}[dr]
            first, rows = {-1: (OVER, OVER), 0: (0, PS), 1: (0, OVER)}[dr]
            base = {-1: 0, 0: OVER, 1: OVER + TS}[dr]
            count = table[at_row, COUNT].astype(jnp.int32)
            for flag, at, step in (
                (HAS_ABOVE, -1, dr), (HAS_BELOW, 1, dr), (HAS_LEFT, -1, dc), (HAS_RIGHT, 1, dc)
            ):
                if step == at:
                    count = jnp.where(table[16 + flag, 0] > 0.0, count, 0)

            @pl.loop(0, count)
            def _(s, at_row=at_row, dc=dc, first=first, rows=rows, base=base):
                r, c = [table[at_row, 2 * s + i].astype(jnp.int32) for i in range(2)]
                for k in range(0, rows, 64):
                    at = pl.ds(base + r + k, 64)
                    v = [p2[j, first + k : first + k + 64, :] for j in range(2)]
                    lane = lax.broadcasted_iota(jnp.int32, v[0].shape, 1)
                    if dc == 0:
                        for j, u in enumerate(lane_push(v, c)):
                            buf[j, at, :] += u
                    elif dc < 0:
                        buf[0, at, :] += jnp.where(lane < c, pltpu.roll(v[1], c % L, 1), 0.0)
                    else:
                        buf[2, at, :] += jnp.where(lane >= c, pltpu.roll(v[0], c % L, 1), 0.0)

    weight[...] = buf[:, OVER : OVER + SPAN, :]
    for k, copy in enumerate(copies):
        if k != 2:
            copy.wait()


def second_pass(
    meta, flags, right, below0, below1, diag, acc1, side, inner, mid_above, mid_below, from_above, from_below,
    weight, pnum1, own, dual, probe, amps, fwd, bwd,
    base, shrink, to_right, lower, to_below, pnum, to_swap,
    partial, ext, acc, win, X, Y, W,
):
    has_right = flags[HAS_RIGHT : HAS_RIGHT + 1, :]
    has_below = flags[HAS_BELOW : HAS_BELOW + 1, :]
    has_above = flags[HAS_ABOVE : HAS_ABOVE + 1, :]
    acc[...] = jnp.zeros_like(acc)
    pnum[...] = pnum1[...]
    for ch in range(2):
        for j in range(3):
            cols = slice(j * L, (j + 1) * L)
            for k in range(0, SPAN, 64):
                rows = slice(k, k + 64)
                total = acc1[ch, j, rows, :]
                if j != 1:
                    at = plane(ch, SPAN, k, 64)
                    total = total + from_sides(flags, side[at, :], inner[at, :])[j // 2]
                if k < OVER:
                    came = mid_above[ch, rows, :] if j == 1 else from_above[ch, j // 2, rows, :]
                    total = total + came.astype(f32) * has_above
                if k >= TS:
                    rim = slice(k - TS, k - TS + 64)
                    came = mid_below[ch, rim, :] if j == 1 else from_below[ch, j // 2, rim, :]
                    total = total + came.astype(f32)
                step = total / (weight[j, rows, :] + penalty)
                if j < 2 and k < TS:
                    est = own[ch, rows, cols] + step
                    partial[ch, rows, cols] = est
                else:
                    if k < TS:
                        est = right[ch, rows, :].astype(f32) + step
                    elif j < 2:
                        est = (below0, below1)[j][plane(ch, OVER, k - TS, 64), :].astype(f32) + step
                    else:
                        est = diag[plane(ch, OVER, k - TS, 64), :].astype(f32) + step
                    if j == 2:
                        est = est * has_right
                    if k >= TS:
                        est = est * has_below
                ext[ch, j, rows, :] = est.astype(bf16).astype(f32)

    @pl.loop(0, (meta[COUNT] + 1) // 2)
    def _(p):
        visit_pair(p, meta, ext, probe, amps, fwd, bwd, acc, pnum, win, X, Y, W)

    to_right[...] = acc[:, 2].astype(bf16)
    to_below[...] = acc[:, 1, TS:, :].astype(bf16)
    lower[...] = acc[:, 0, TS:, :]
    odd = flags[ODD : ODD + 1, :1] > 0.0
    for ch in range(3):
        lo, hi = pnum[ch, : PS // 2, :], pnum[ch, PS // 2 :, :]
        to_swap[ch] = jnp.where(odd, lo, hi).astype(bf16)
    for j in range(2):
        cols = slice(j * L, (j + 1) * L)
        for k in range(0, TS, 64):
            rows = slice(k, k + 64)
            over = 1.0 / (weight[j, rows, :] + penalty)
            shrink[j, rows, :] = over
            for ch in range(2):
                est = partial[ch, rows, cols]
                held = dual[ch, rows, cols]
                pull = penalty * (own[ch, rows, cols] - held - est)
                base[ch, rows, cols] = est + held + (acc[ch, j, rows, :] + pull) * over


def halve(flags, sums, came, *rest):
    odd = flags[ODD : ODD + 1, :1] > 0.0
    for ch in range(3):
        lo, hi = sums[ch, : PS // 2, :], sums[ch, PS // 2 :, :]
        rest[-1][ch] = (jnp.where(odd, hi, lo) + came[ch].astype(f32)).astype(bf16)


def add(held, came, *rest):
    for ch in range(3):
        rest[-1][ch] = (held[ch].astype(f32) + came[ch].astype(f32)).astype(bf16)


def add_rim(flags, rim, from_left, *rest):
    has_left = flags[HAS_LEFT : HAS_LEFT + 1, :]
    for ch in range(2):
        rest[-1][ch] = (rim[ch] + from_left[ch, TS:, :].astype(f32) * has_left).astype(bf16)


def finish_estimate(flags, base, shrink, from_left, above0, above1, *rest):
    combined, parts = rest[-3], rest[-2:]
    has_left = flags[HAS_LEFT : HAS_LEFT + 1, :]
    has_above = flags[HAS_ABOVE : HAS_ABOVE + 1, :]
    for ch in range(2):
        for j in range(2):
            cols = slice(j * L, (j + 1) * L)
            for k in range(0, TS, 64):
                rows = slice(k, k + 64)
                total = base[ch, rows, cols]
                came = None
                if j == 0:
                    came = from_left[ch, rows, :].astype(f32) * has_left
                if k < OVER:
                    above = (above0, above1)[j][ch, rows, :].astype(f32) * has_above
                    came = above if came is None else came + above
                if came is not None:
                    total = total + came * shrink[j, rows, :]
                combined[ch, rows, cols] = total
                part = slice(k % (TS // 2), k % (TS // 2) + 64)
                parts[k // (TS // 2)][ch, part, cols] = total.astype(bf16)


def mixed(first, first_came, second, second_came, outs):
    for out, part, came in ((outs[0], first, first_came), (outs[1], second, second_came)):
        for ch in range(2):
            out[ch] = (part[ch].astype(f32) + came[ch].astype(f32)).astype(bf16)


def mix(*refs):
    mixed(*refs[:4], refs[-2:])


def update(held, came, *rest):
    total = [held[ch].astype(f32) + came[ch].astype(f32) for ch in range(3)]
    over = probe_step * lax.rsqrt(total[2] + 1.0)
    for ch in range(2):
        rest[-1][ch] = (total[ch] * over).astype(bf16)


def settle(groups, first, first_came, second, second_came, combined, *rest):
    settled, dual_new = rest[-2:]
    for k in range(0, TS, CH):
        rows = slice(k, k + CH)
        part, came = (first, first_came) if k < TS // 2 else (second, second_came)
        at = slice(k % (TS // 2), k % (TS // 2) + CH)
        re, im = [
            (part[ch, at, :].astype(f32) + came[ch, at, :].astype(f32)) * (1.0 / groups)
            for ch in range(2)
        ]
        over = 1.0 / jnp.maximum(jnp.sqrt(re * re + im * im), 1.0)
        re, im = re * over, im * over
        settled[0, rows, :] = re
        settled[1, rows, :] = im
        dual_new[0, rows, :] = combined[0, rows, :] - re
        dual_new[1, rows, :] = combined[1, rows, :] - im


V = pl.BlockSpec(memory_space=pltpu.VMEM)
S = pl.BlockSpec(memory_space=pltpu.SMEM)
H = pl.BlockSpec(memory_space=pltpu.HBM)


def pinned(value):
    return pltpu.with_memory_space_constraint(value, pltpu.VMEM)


def call(body, name, outs, scratch=(), scalars=0, far=0, copies=0, aliases=None, held=0, flops=0):
    def run(*operands):
        near = len(operands) - scalars - far
        spaces = [None] * (scalars + near) + [pltpu.HBM] * far
        operands = [
            v if space is None else pltpu.with_memory_space_constraint(v, space)
            for v, space in zip(operands, spaces)
        ]
        return pl.pallas_call(
            body,
            in_specs=[S] * scalars + [V] * near + [H] * far,
            out_specs=[V] * len(outs),
            out_shape=[
                pltpu.VMEM(shape, dtype) if k < held else jax.ShapeDtypeStruct(shape, dtype)
                for k, (shape, dtype) in enumerate(outs)
            ],
            scratch_shapes=[
                pltpu.SemaphoreType.DMA((copies,)) if one is None else pltpu.VMEM(*one)
                if isinstance(one, tuple) else one
                for one in scratch
            ],
            input_output_aliases=aliases or {},
            cost_estimate=pl.CostEstimate(
                flops=flops or sum(math.prod(shape) for shape, _ in outs),
                bytes_accessed=sum(v.size * v.dtype.itemsize for v in operands[scalars + near :]),
                transcendentals=0,
            ),
            compiler_params=pltpu.CompilerParams(vmem_limit_bytes=24 * 2**20),
            name=name,
        )(*operands)

    return run


PLANES = ((2, PS, PS), f32)
PASS = SLOTS * 4 * 4 * PS**3
WORK = [
    ((2, 2, PS, PS), f32),
    ((2, PS, 2 * PS), bf16),
    ((2, 2 * PS, PS), bf16),
    ((2, 2 * PS, PS), f32),
]
TABLE = ((PS, PS), bf16)
WIDE = ((2, 3, SPAN, L), f32)
SUMS = ((3, PS, PS), f32)


def shards(consensus, duals, probes, amplitudes, offsets, counts):
    fwd, bwd, order = dft_tables()
    n = lax.axis_size("tile")
    index = lax.axis_index("tile")
    own = consensus[0]
    dual = duals[0, 0]
    probe = probes[0]
    amps = amplitudes[0, 0]
    measured = ((SLOTS, PS, PS), bf16)

    rounded = own.astype(bf16)
    height = n // TGW
    two = height == 2
    row, col = index // TGW, index % TGW
    flags = [col > 0, col < TGW - 1, row > 0, row < height - 1]
    flags = flags + [index % 2 == 1] + [col < 0] * 3
    flags = jnp.broadcast_to(jnp.stack(flags).astype(f32)[:, None], (8, L))
    meta = jnp.concatenate([offsets[0, 0].reshape(COUNT), counts[0]])
    card = jnp.pad(meta.astype(bf16)[None], ((0, CARD - 1), (0, L - COUNT - 1)))

    sent = [rounded[:, :OVER, j * L : (j + 1) * L].reshape(2 * OVER, L) for j in range(2)]
    below = [shifted(sent[0], -1, 0), shifted(jnp.concatenate([sent[1], card]), -1, 0)]
    right = shifted(rounded[:, :, :OVER], 0, -1)
    below.append(shifted(below[0], 0, -1))
    cards = [card] if two else [card, shifted(card, 1, 0)]

    *staged, amps = call(
        stage, "stage", [WIDE, WIDE, PLANES, measured], [None, PLANES, PLANES, measured, TABLE], 0, 5, 5,
        held=3,
    )(below[0], own, dual, probe, amps, order)
    staged = [pinned(v) for v in staged]
    inputs = (own, dual, probe, amps, fwd, bwd)
    rim = ((2, OVER, L), bf16)
    ext, acc, pnum, side, inner, *mids = call(
        functools.partial(first_pass, two), "first_pass",
        [WIDE, WIDE, SUMS] + [((2 * SPAN + (len(cards) + 1) * CARD, L), bf16)] * 2
        + [rim] * (1 if two else 2),
        [TABLE, TABLE, measured, None] + WORK, 1, 3, 3, aliases={6: 0, 7: 1}, flops=PASS,
    )(meta, flags, right, *below, *staged, *cards, fwd, bwd, amps)
    side = swapped(side, "tile", 1)
    inner = inner_swapped(inner)

    def down_and_up(rims):
        down = shifted(rims[0], 1, 0)
        return down, down if two else shifted(rims[1], -1, 0)

    mid_above, mid_below = down_and_up(mids)
    rims = call(
        functools.partial(between, two), "between", [((2, 2, OVER, L), bf16)] * (1 if two else 2)
    )(flags, acc, side, inner, pnum, right, *below, mid_above, mid_below)
    from_above, from_below = down_and_up(rims)
    weight, *inputs = call(
        functools.partial(weigh, two), "weigh",
        [((3, SPAN, L), f32), PLANES, PLANES, PLANES, measured, TABLE, TABLE],
        [None, ((2, PS, L), f32), ((3, SPAN + 2 * OVER, L), f32), ((24, L), f32),
         pltpu.SMEM((24, L), f32)],
        0, 6, 7, held=7,
    )(*cards, flags, side, inner, rims[0], acc, pnum, right, below[0], below[2], mid_above, mid_below,
      below[1], *inputs)
    weight, *inputs = [pinned(v) for v in (weight, *inputs)]

    base, shrink, to_right, rim, to_below, pnum, to_swap = call(
        second_pass, "second_pass",
        [PLANES, ((2, TS, L), f32), ((2, SPAN, L), bf16), ((2, OVER, L), f32), ((2, OVER, L), bf16),
         SUMS, ((3, PS // 2, PS), bf16)],
        [PLANES, WIDE, WIDE] + WORK, 1, flops=PASS,
    )(meta, flags, right, *below, acc, side, inner, mid_above, mid_below, from_above,
      from_below, weight, pnum, *inputs)
    from_left = shifted(to_right, 0, 1)
    above1 = shifted(to_below, 1, 0)
    (to_below,) = call(add_rim, "add_rim", [((2, OVER, L), bf16)])(flags, rim, from_left, base, shrink)
    above0 = shifted(to_below, 1, 0)

    eight = n == 8
    half = [((3, PS // 2, PS), bf16)]
    if eight:
        (sums,) = call(halve, "halve", half)(flags, pnum, swapped(to_swap, "tile", 1), base, shrink)
        came = swapped(sums, "tile", 2)
    combined, *parts = call(
        finish_estimate, "finish_estimate", [PLANES] + [((2, TS // 2, TS), bf16)] * 2
    )(flags, base, shrink, from_left, above0, above1, *([sums] if eight else []))
    if eight:
        (sums,) = call(add, "add", half)(sums, came, parts[0])
        came = swapped(sums, "tile", 6)
    pairs = scan_sums(parts)
    if eight:
        (change,) = call(update, "update", [((2, PS // 2, PS), bf16)])(sums, came, pairs[1])
    settled, dual_new = call(
        functools.partial(settle, lax.axis_size("scan")), "settle", [PLANES] * 2
    )(*pairs, combined)
    if eight:
        change = doubled(index, change, 1).astype(f32)
    else:
        total = lax.psum(pnum, "tile")
        change = probe_step * total[0:2] / jnp.sqrt(total[2] + 1.0)
    probe_new = probe + change
    return (settled[None], dual_new[None, None], probe_new[None])


def solution(mesh):
    placed = (
        P("tile", None, None, None),
        P("scan", "tile", None, None, None),
        P("scan", None, None, None),
        P("scan", "tile", None, None, None),
        P("scan", "tile", None, None),
        P("scan", "tile"),
    )
    return jax.shard_map(
        shards,
        mesh=mesh,
        in_specs=placed,
        out_specs=(
            P("tile", None, None, None),
            P("scan", "tile", None, None, None),
            P("scan", None, None, None),
        ),
        check_vma=False,
    )
```

```python
import functools
import math

import jax
import jax.numpy as jnp
import ml_dtypes
import numpy as np
from jax import lax
from jax.experimental import pallas as pl
from jax.experimental.pallas import tpu as pltpu
from jax.sharding import PartitionSpec as P

PS = 256
TS = 256
OVER = 128
TGW = 4
SLOTS = 4
SPAN = TS + OVER
L = 128
HALF = PS // 2
CH = 32
COUNT = 2 * SLOTS
CARD = 16
HAS_LEFT, HAS_RIGHT, HAS_ABOVE, HAS_BELOW, ODD = range(5)

penalty = 0.5
smoothing = 0.05
probe_step = 3.0

f32 = jnp.float32
bf16 = jnp.bfloat16


def dft_tables():
    indices = np.arange(PS, dtype=np.int32)
    phase_index = indices[:, None] * indices[None, :] % PS
    angles = phase_index.astype(np.float32) * np.float32(2.0 * math.pi / PS)
    scale = np.float32(1.0 / math.sqrt(PS))
    re = (np.cos(angles) * scale).astype(ml_dtypes.bfloat16)
    im = (-np.sin(angles) * scale).astype(ml_dtypes.bfloat16)
    half = np.concatenate([re[:HALF], re[HALF : HALF + 1], im[1:HALF]])
    order = np.concatenate([indices[: HALF + 1], indices[:HALF:-1]])
    return jnp.asarray(half), jnp.asarray(half.T), jnp.asarray(np.eye(PS, dtype=half.dtype)[order])


def shifted(value, rows, cols):
    height = lax.axis_size("tile") // TGW
    pairs = []
    for i in range(height * TGW):
        r, c = divmod(i, TGW)
        pairs.append((i, (r + rows) % height * TGW + (c + cols) % TGW))
    return lax.ppermute(value, "tile", pairs)


def swapped(value, axis, bit):
    n = lax.axis_size(axis)
    return lax.ppermute(value, axis, [(i, i ^ bit) for i in range(n)])


def is_power(n):
    return n & (n - 1) == 0


def inner_swapped(value):
    n = lax.axis_size("tile")
    return lax.ppermute(value, "tile", [(i, i ^ 3 if i % TGW in (1, 2) else i) for i in range(n)])


def scan_sums(parts):
    n = lax.axis_size("scan")
    if not is_power(n):
        return [v for part in parts for v in (lax.psum(part, "scan"), jnp.zeros_like(part))]
    bits = [1 << k for k in range(n.bit_length() - 1)]
    for k in range(len(bits)):
        came = [swapped(parts[p], "scan", bits[(k + p) % len(bits)]) for p in range(2)]
        pairs = [parts[0], came[0], parts[1], came[1]]
        if k < len(bits) - 1:
            outs = [(parts[0].shape, bf16)] * 2
            parts = call(mix, f"mix{k}", outs)(*pairs)
    return pairs


def doubled(index, change, bit):
    other = swapped(change, "tile", bit)
    return jnp.where(
        (index // bit) % 2 == 1,
        jnp.concatenate([other, change], 1),
        jnp.concatenate([change, other], 1),
    )


def lane_pull(blocks, c):
    lane = lax.broadcasted_iota(jnp.int32, blocks[0].shape, 1)
    keep = lane < L - c
    r = [pltpu.roll(v, (L - c) % L, 1) for v in blocks]
    return jnp.concatenate([jnp.where(keep, r[0], r[1]), jnp.where(keep, r[1], r[2])], 1)


def lane_push(blocks, c):
    lane = lax.broadcasted_iota(jnp.int32, blocks[0].shape, 1)
    past = lane >= c
    r = [pltpu.roll(v, c % L, 1) for v in blocks]
    z = jnp.zeros_like(r[0])
    return [jnp.where(past, r[0], z), jnp.where(past, r[1], r[0]), jnp.where(past, z, r[1])]


def split(pr, pi, qr, qi, first):
    planes = (pr - qi, pr + qi, pi + qr, pi - qr)
    if first is None:
        return planes
    return [jnp.where(first, v, w) for v, w in zip((pr, qr, pi, qi), planes)]


def joined(lr, hr, li, hi, first):
    planes = (lr + hr, li - hi, li + hi, hr - lr)
    if first is None:
        return planes
    return [jnp.where(first, v, w) for v, w in zip((lr, hr, li, hi), planes)]


def visit_pair(p, meta, ext, probe, amps, half, turned, acc, pnum, win, X, Y, W):
    N = PS
    used = jnp.where(2 * p + 1 < meta[COUNT], 1.0, 0.0).astype(f32)
    corners = [(meta[4 * p + 2 * i], meta[4 * p + 2 * i + 1]) for i in range(2)]

    def leave(i):
        r, c = corners[i]
        for k in range(0, N, CH):
            rows = slice(k, k + CH)
            w = [
                lane_pull([ext[ch, j, pl.ds(r + k, CH), :] for j in range(3)], c) for ch in range(2)
            ]
            if i == 1:
                w = [v * used for v in w]
            pr, pi = probe[0, rows, :], probe[1, rows, :]
            win[i, 0, rows, :] = w[0]
            win[i, 1, rows, :] = w[1]
            X[i, rows, :N] = (pr * w[0] - pi * w[1]).astype(bf16)
            X[i, rows, N:] = (pr * w[1] + pi * w[0]).astype(bf16)
            pnum[2, rows, :] += w[0] * w[0] + w[1] * w[1]

    def columns(i):
        t = jnp.dot(half[...], X[i], preferred_element_type=f32)
        for k in range(0, HALF, CH):
            p, q = t[k : k + CH], t[HALF + k : HALF + k + CH]
            first = lax.broadcasted_iota(jnp.int32, (CH, N), 0) == 0 if k == 0 else None
            planes = split(p[:, :N], p[:, N:], q[:, :N], q[:, N:], first)
            for j, v in enumerate(planes):
                Y[i, j * HALF + k : j * HALF + k + CH, :] = v.astype(bf16)

    def rows_of(i):
        W[i] = jnp.dot(Y[i], turned[...], preferred_element_type=f32)

    def compare(i):
        first = lax.broadcasted_iota(jnp.int32, (CH, L), 1) == 0
        top = lax.broadcasted_iota(jnp.int32, (CH, N), 0) == 0
        for k in range(0, HALF, CH):
            resid = []
            for h in range(2):
                rows = slice(h * HALF + k, h * HALF + k + CH)
                at = slice(N + h * HALF + k, N + h * HALF + k + CH)
                planes = split(W[i, rows, :L], W[i, at, :L], W[i, rows, L:], W[i, at, L:], first)
                a = amps[2 * p + i, rows, :].astype(f32)
                wr = jnp.concatenate([planes[0], planes[1]], 1)
                wi = jnp.concatenate([planes[2], planes[3]], 1)
                f = a * lax.rsqrt(wr * wr + wi * wi + smoothing) - 1.0
                resid.append((wr * f, wi * f))
            (lr, li), (hr, hi) = resid
            for j, v in enumerate(joined(lr, hr, li, hi, top if k == 0 else None)):
                X[i, j % 2 * HALF + k : j % 2 * HALF + k + CH, j // 2 * N : j // 2 * N + N] = v.astype(bf16)

    def columns_back(i):
        t = jnp.dot(turned[...], X[i], preferred_element_type=f32)
        first = lax.broadcasted_iota(jnp.int32, (CH, L), 1) == 0
        for k in range(0, N, CH):
            v = t[k : k + CH]
            planes = joined(v[:, :L], v[:, L:N], v[:, N : N + L], v[:, N + L :], first)
            for j, v in enumerate(planes):
                at = j // 2 * N + k
                Y[i, at : at + CH, j % 2 * L : j % 2 * L + L] = v.astype(bf16)

    def rows_back(i):
        W[i] = jnp.dot(Y[i], half[...], preferred_element_type=f32)

    def gather(i):
        r, c = corners[i]
        for k in range(0, N, CH):
            rows = slice(k, k + CH)
            br, bi = W[i, rows, :], W[i, N + k : N + k + CH, :]
            pr, pi = probe[0, rows, :], probe[1, rows, :]
            wr, wi = win[i, 0, rows, :], win[i, 1, rows, :]
            pnum[0, rows, :] += wr * br + wi * bi
            pnum[1, rows, :] += wr * bi - wi * br
            for ch, v in enumerate((pr * br + pi * bi, pr * bi - pi * br)):
                for j, u in enumerate(lane_push([v[:, :L], v[:, L:]], c)):
                    acc[ch, j, pl.ds(r + k, CH), :] += u

    leave(0)
    columns(0)
    leave(1)
    rows_of(0)
    columns(1)
    compare(0)
    rows_of(1)
    columns_back(0)
    compare(1)
    rows_back(0)
    columns_back(1)
    gather(0)
    rows_back(1)
    gather(1)


def fetch(pairs, sems):
    copies = [pltpu.make_async_copy(src, dst, sems.at[i]) for i, (src, dst) in enumerate(pairs)]
    for copy in copies:
        copy.start()
    return copies


def stage(own_h, dual_h, probe_h, ext, acc, probe, sems, own, dual):
    copies = fetch([(own_h, own), (dual_h, dual), (probe_h, probe)], sems)
    acc[:, 2] = jnp.zeros((2, SPAN, L), f32)
    copies[0].wait()
    for j in range(2):
        cols = slice(j * L, (j + 1) * L)
        acc[:, j, TS:, :] = jnp.zeros((2, OVER, L), f32)
        ext[:, j, :TS, :] = own[:, :, cols].astype(bf16).astype(f32)
    copies[1].wait()
    for j in range(2):
        cols = slice(j * L, (j + 1) * L)
        acc[:, j, :TS, :] = -penalty * dual[:, :, cols]
    copies[2].wait()


def reorder(below, amps_h, order_h, ordered_h, sems, amps, order, ordered):
    copies = fetch([(order_h, order), (amps_h, amps)], sems)
    for copy in copies:
        copy.wait()
    for k in range(SLOTS):
        rows = jnp.dot(order[...], amps[k], preferred_element_type=f32).astype(bf16)
        ordered[k] = jnp.dot(rows, order[...], preferred_element_type=f32).astype(bf16)
    back = pltpu.make_async_copy(ordered, ordered_h, sems.at[2])
    back.start()
    back.wait()


def first_pass(
    two, meta, flags, right, below0, below1, diag, ext0, acc0, probe, *rest,
):
    *cards, fwd_h, bwd_h, amps_h = rest[: 4 if two else 5]
    ext, acc, pnum, side, *inner, fwd, bwd, amps, sems, win, X, Y, W = rest[4 if two else 5 :]
    copies = fetch([(fwd_h, fwd), (bwd_h, bwd), (amps_h, amps)], sems)
    has_right = flags[HAS_RIGHT : HAS_RIGHT + 1, :]
    has_below = flags[HAS_BELOW : HAS_BELOW + 1, :]
    ext[:, 2, :TS, :] = right[...].astype(f32) * has_right
    for ch in range(2):
        ext[ch, 2, TS:, :] = diag[plane(ch, OVER), :].astype(f32) * (has_right * has_below)
    for j in range(2):
        for ch in range(2):
            ext[ch, j, TS:, :] = (below0, below1)[j][plane(ch, OVER), :].astype(f32) * has_below
    pnum[...] = jnp.zeros_like(pnum)
    for copy in copies:
        copy.wait()

    @pl.loop(0, (meta[COUNT] + 1) // 2)
    def _(p):
        visit_pair(p, meta, ext, probe, amps, fwd, bwd, acc, pnum, win, X, Y, W)

    odd = flags[ODD : ODD + 1, :] > 0.0
    column = [card[...] for card in cards] + [below1[2 * OVER :, :]]
    side[2 * SPAN :, :] = jnp.concatenate(column, 0)
    inner[0][2 * (OVER if two else SPAN) :, :] = jnp.concatenate(column, 0)
    for ch in range(2):
        side[plane(ch, SPAN), :] = jnp.where(odd, acc[ch, 0], acc[ch, 2]).astype(bf16)
        other = [jnp.where(odd, acc[ch, 2, rows, :], acc[ch, 0, rows, :]) for rows in BANDS]
        for part, values in zip(inner, parted(two, flags, other)):
            rows = values.shape[0]
            part[plane(ch, rows), :] = values.astype(bf16)


def plane(ch, rows, start=0, count=None):
    return slice(ch * rows + start, ch * rows + start + (rows if count is None else count))


def parted(two, flags, bands):
    if not two:
        return [jnp.concatenate(bands, 0)]
    lower = flags[HAS_BELOW : HAS_BELOW + 1, :] > 0.0
    rest = [jnp.where(lower, bands[k], bands[k + 1]) for k in range(2)]
    return [jnp.where(lower, bands[2], bands[0]), jnp.concatenate(rest, 0)]


def from_inner(two, flags, inner, ch, start, count):
    if not two:
        return inner[0][plane(ch, SPAN, start, count), :]
    band, at = divmod(start, OVER)
    lower = flags[HAS_BELOW : HAS_BELOW + 1, :] > 0.0
    rim = inner[0][plane(ch, OVER, at, count), :]
    first, second = [inner[1][plane(ch, TS, k * OVER + at, count), :] for k in range(2)]
    on_top = (first, second, rim)[band].astype(f32)
    return jnp.where(lower, on_top, (rim, first, second)[band].astype(f32))


def rims_of(two, flags, get):
    down, up = get(slice(TS, SPAN)), get(slice(0, OVER))
    return [jnp.where(flags[HAS_BELOW : HAS_BELOW + 1, :] > 0.0, down, up)] if two else [down, up]


def from_sides(flags, side, inner):
    odd = flags[ODD : ODD + 1, :] > 0.0
    valid = flags[HAS_LEFT : HAS_LEFT + 1, :] * flags[HAS_RIGHT : HAS_RIGHT + 1, :]
    side, inner = side.astype(f32), inner.astype(f32) * valid
    return jnp.where(odd, side, inner), jnp.where(odd, inner, side)


def between(two, flags, acc, side, inner, *rest):
    outs = rest[-3:] if two else rest[-6:]
    for ch in range(2):
        for j in range(3):
            rims = rims_of(two, flags, lambda rows: acc[ch, j, rows, :])
            if j != 1:
                sides = rims_of(
                    two, flags, lambda rows: side[plane(ch, SPAN, rows.start, OVER), :].astype(f32)
                )
                size = OVER if two else SPAN
                starts = [0] if two else [TS, 0]
                for k, start in enumerate(starts):
                    other = inner[plane(ch, size, start, OVER), :]
                    rims[k] = rims[k] + from_sides(flags, sides[k], other)[j // 2]
            for k, rim in enumerate(rims):
                outs[3 * k + j][ch] = rim.astype(bf16)


def weigh(two, *rest):
    *cards, flags, side, inner = rest[: 4 if two else 5]
    below1, *sources = rest[-19:-12]
    weight, *targets, sems, p2, buf, held, table = rest[-12:]
    copies = fetch(list(zip(sources, targets)), sems)
    probe = targets[2]
    last = 2 * OVER
    blocks = [card[...].astype(f32) for card in cards] + [below1[last:, :].astype(f32)]
    for k, block in enumerate(blocks):
        held[k : k + 1, :] = block[:1]
        ends = [2 * SPAN + k * CARD, 2 * (OVER if two else SPAN) + k * CARD]
        odd = flags[ODD : ODD + 1, :] > 0.0
        by_side, by_inner = [
            v[at : at + CARD, :].astype(f32)[:1] for v, at in zip((side, inner), ends)
        ]
        held[4 + k : 5 + k, :] = jnp.where(odd, by_side, by_inner)
        held[8 + k : 9 + k, :] = jnp.where(odd, by_inner, by_side)
    held[16:24, :] = flags[...]
    moved = pltpu.make_async_copy(held, table, sems.at[6])
    moved.start()
    buf[...] = jnp.zeros_like(buf)
    copies[2].wait()
    for j in range(2):
        cols = slice(j * L, (j + 1) * L)
        p2[j] = probe[0, :, cols] * probe[0, :, cols] + probe[1, :, cols] * probe[1, :, cols]
    moved.wait()
    for dr in (-1, 0, 1):
        for dc in (-1, 0, 1):
            at_row = {0: 0, -1: 4, 1: 8}[dc] + {0: 0, -1: 1, 1: 1 if two else 2}[dr]
            first, rows = {-1: (OVER, OVER), 0: (0, PS), 1: (0, OVER)}[dr]
            base = {-1: 0, 0: OVER, 1: OVER + TS}[dr]
            count = table[at_row, COUNT].astype(jnp.int32)
            for flag, at, step in (
                (HAS_ABOVE, -1, dr), (HAS_BELOW, 1, dr), (HAS_LEFT, -1, dc), (HAS_RIGHT, 1, dc)
            ):
                if step == at:
                    count = jnp.where(table[16 + flag, 0] > 0.0, count, 0)

            @pl.loop(0, count)
            def _(s, at_row=at_row, dc=dc, first=first, rows=rows, base=base):
                r, c = [table[at_row, 2 * s + i].astype(jnp.int32) for i in range(2)]
                for k in range(0, rows, 64):
                    at = pl.ds(base + r + k, 64)
                    v = [p2[j, first + k : first + k + 64, :] for j in range(2)]
                    lane = lax.broadcasted_iota(jnp.int32, v[0].shape, 1)
                    if dc == 0:
                        for j, u in enumerate(lane_push(v, c)):
                            buf[j, at, :] += u
                    elif dc < 0:
                        buf[0, at, :] += jnp.where(lane < c, pltpu.roll(v[1], c % L, 1), 0.0)
                    else:
                        buf[2, at, :] += jnp.where(lane >= c, pltpu.roll(v[0], c % L, 1), 0.0)

    weight[...] = buf[:, OVER : OVER + SPAN, :]
    for k, copy in enumerate(copies):
        if k != 2:
            copy.wait()


def second_pass(
    two, meta, flags, right, below0, below1, diag, acc1, side, *rest,
):
    inner, rest = rest[: 2 if two else 1], rest[2 if two else 1 :]
    from_above, from_below, rest = rest[:3], rest[3:6], rest[6:]
    weight, pnum1, own, dual, probe, amps, fwd, bwd = rest[:8]
    base, shrink, to_right, to_corner, lower, to_below, pnum, to_swap = rest[8:16]
    partial, ext, acc, win, X, Y, W = rest[16:]
    has_right = flags[HAS_RIGHT : HAS_RIGHT + 1, :]
    has_below = flags[HAS_BELOW : HAS_BELOW + 1, :]
    has_above = flags[HAS_ABOVE : HAS_ABOVE + 1, :]
    acc[...] = jnp.zeros_like(acc)
    pnum[...] = pnum1[...]
    for ch in range(2):
        for j in range(3):
            cols = slice(j * L, (j + 1) * L)
            for k in range(0, SPAN, 64):
                rows = slice(k, k + 64)
                total = acc1[ch, j, rows, :]
                if j != 1:
                    at = plane(ch, SPAN, k, 64)
                    total = total + from_sides(
                        flags, side[at, :], from_inner(two, flags, inner, ch, k, 64)
                    )[j // 2]
                if k < OVER:
                    came = from_above[j][ch, rows, :]
                    total = total + came.astype(f32) * has_above
                if k >= TS:
                    rim = slice(k - TS, k - TS + 64)
                    came = from_below[j][ch, rim, :]
                    total = total + came.astype(f32)
                step = total / (weight[j, rows, :] + penalty)
                if j < 2 and k < TS:
                    est = own[ch, rows, cols] + step
                    partial[ch, rows, cols] = est
                else:
                    if k < TS:
                        est = right[ch, rows, :].astype(f32) + step
                    elif j < 2:
                        est = (below0, below1)[j][plane(ch, OVER, k - TS, 64), :].astype(f32) + step
                    else:
                        est = diag[plane(ch, OVER, k - TS, 64), :].astype(f32) + step
                    if j == 2:
                        est = est * has_right
                    if k >= TS:
                        est = est * has_below
                ext[ch, j, rows, :] = est.astype(bf16).astype(f32)

    @pl.loop(0, (meta[COUNT] + 1) // 2)
    def _(p):
        visit_pair(p, meta, ext, probe, amps, fwd, bwd, acc, pnum, win, X, Y, W)

    to_corner[...] = acc[:, 2, TS:, :].astype(bf16)
    to_right[...] = acc[:, 2, :TS, :].astype(bf16)
    to_below[...] = acc[:, 1, TS:, :].astype(bf16)
    lower[...] = acc[:, 0, TS:, :]
    odd = flags[ODD : ODD + 1, :1] > 0.0
    for ch in range(3):
        lo, hi = pnum[ch, : PS // 2, :], pnum[ch, PS // 2 :, :]
        to_swap[ch] = jnp.where(odd, lo, hi).astype(bf16)
    for j in range(2):
        cols = slice(j * L, (j + 1) * L)
        for k in range(0, TS, 64):
            rows = slice(k, k + 64)
            over = 1.0 / (weight[j, rows, :] + penalty)
            shrink[j, rows, :] = over
            for ch in range(2):
                est = partial[ch, rows, cols]
                held = dual[ch, rows, cols]
                pull = penalty * (own[ch, rows, cols] - held - est)
                base[ch, rows, cols] = est + held + (acc[ch, j, rows, :] + pull) * over


def halve(flags, sums, came, *rest):
    odd = flags[ODD : ODD + 1, :1] > 0.0
    for ch in range(3):
        lo, hi = sums[ch, : PS // 2, :], sums[ch, PS // 2 :, :]
        rest[-1][ch] = (jnp.where(odd, hi, lo) + came[ch].astype(f32)).astype(bf16)


def add(held, came, *rest):
    for ch in range(3):
        rest[-1][ch] = (held[ch].astype(f32) + came[ch].astype(f32)).astype(bf16)


def add_rim(flags, rim, from_left, *rest):
    has_left = flags[HAS_LEFT : HAS_LEFT + 1, :]
    for ch in range(2):
        rest[-1][ch] = (rim[ch] + from_left[ch].astype(f32) * has_left).astype(bf16)


def finish_estimate(flags, base, shrink, from_left, above0, above1, *rest):
    combined, parts = rest[-3], rest[-2:]
    has_left = flags[HAS_LEFT : HAS_LEFT + 1, :]
    has_above = flags[HAS_ABOVE : HAS_ABOVE + 1, :]
    for ch in range(2):
        for j in range(2):
            cols = slice(j * L, (j + 1) * L)
            for k in range(0, TS, 64):
                rows = slice(k, k + 64)
                total = base[ch, rows, cols]
                came = None
                if j == 0:
                    came = from_left[ch, rows, :].astype(f32) * has_left
                if k < OVER:
                    above = (above0, above1)[j][ch, rows, :].astype(f32) * has_above
                    came = above if came is None else came + above
                if came is not None:
                    total = total + came * shrink[j, rows, :]
                combined[ch, rows, cols] = total
                part = slice(k % (TS // 2), k % (TS // 2) + 64)
                parts[k // (TS // 2)][ch, part, cols] = total.astype(bf16)


def mixed(first, first_came, second, second_came, outs):
    for out, part, came in ((outs[0], first, first_came), (outs[1], second, second_came)):
        for ch in range(2):
            out[ch] = (part[ch].astype(f32) + came[ch].astype(f32)).astype(bf16)


def mix(*refs):
    mixed(*refs[:4], refs[-2:])


def update(held, came, *rest):
    total = [held[ch].astype(f32) + came[ch].astype(f32) for ch in range(3)]
    over = probe_step * lax.rsqrt(total[2] + 1.0)
    for ch in range(2):
        rest[-1][ch] = (total[ch] * over).astype(bf16)


def settle(groups, first, first_came, second, second_came, combined, *rest):
    settled, dual_new = rest[-2:]
    for k in range(0, TS, CH):
        rows = slice(k, k + CH)
        part, came = (first, first_came) if k < TS // 2 else (second, second_came)
        at = slice(k % (TS // 2), k % (TS // 2) + CH)
        re, im = [
            (part[ch, at, :].astype(f32) + came[ch, at, :].astype(f32)) * (1.0 / groups)
            for ch in range(2)
        ]
        over = 1.0 / jnp.maximum(jnp.sqrt(re * re + im * im), 1.0)
        re, im = re * over, im * over
        settled[0, rows, :] = re
        settled[1, rows, :] = im
        dual_new[0, rows, :] = combined[0, rows, :] - re
        dual_new[1, rows, :] = combined[1, rows, :] - im


BANDS = [slice(k, k + OVER) for k in range(0, SPAN, OVER)]
V = pl.BlockSpec(memory_space=pltpu.VMEM)
S = pl.BlockSpec(memory_space=pltpu.SMEM)
H = pl.BlockSpec(memory_space=pltpu.HBM)


def pinned(value):
    return pltpu.with_memory_space_constraint(value, pltpu.VMEM)


def call(body, name, outs, scratch=(), scalars=0, far=0, copies=0, aliases=None, held=0, flops=0):
    def run(*operands):
        near = len(operands) - scalars - far
        place = pltpu.HBM if held < 0 else pltpu.VMEM
        spaces = [None] * (scalars + near) + [pltpu.HBM] * far
        operands = [
            v if space is None else pltpu.with_memory_space_constraint(v, space)
            for v, space in zip(operands, spaces)
        ]
        return pl.pallas_call(
            body,
            in_specs=[S] * scalars + [V] * near + [H] * far,
            out_specs=[H if held < 0 else V] * len(outs),
            out_shape=[
                place(shape, dtype) if k < abs(held) else jax.ShapeDtypeStruct(shape, dtype)
                for k, (shape, dtype) in enumerate(outs)
            ],
            scratch_shapes=[
                pltpu.SemaphoreType.DMA((copies,)) if one is None else pltpu.VMEM(*one)
                if isinstance(one, tuple) else one
                for one in scratch
            ],
            input_output_aliases=aliases or {},
            cost_estimate=pl.CostEstimate(
                flops=flops or sum(math.prod(shape) for shape, _ in outs),
                bytes_accessed=sum(v.size * v.dtype.itemsize for v in operands[scalars + near :]),
                transcendentals=0,
            ),
            compiler_params=pltpu.CompilerParams(vmem_limit_bytes=24 * 2**20),
            name=name,
        )(*operands)

    return run


PLANES = ((2, PS, PS), f32)
PASS = SLOTS * 4 * 4 * PS**3
WORK = [
    ((2, 2, PS, PS), f32),
    ((2, PS, 2 * PS), bf16),
    ((2, 2 * PS, PS), bf16),
    ((2, 2 * PS, PS), f32),
]
TABLE = ((PS, PS), bf16)
WIDE = ((2, 3, SPAN, L), f32)
SUMS = ((3, PS, PS), f32)


def shards(consensus, duals, probes, amplitudes, offsets, counts):
    fwd, bwd, order = dft_tables()
    n = lax.axis_size("tile")
    index = lax.axis_index("tile")
    own = consensus[0]
    dual = duals[0, 0]
    probe = probes[0]
    amps = amplitudes[0, 0]
    measured = ((SLOTS, PS, PS), bf16)

    rounded = own.astype(bf16)
    height = n // TGW
    two = height == 2
    row, col = index // TGW, index % TGW
    flags = [col > 0, col < TGW - 1, row > 0, row < height - 1]
    flags = flags + [index % 2 == 1] + [col < 0] * 3
    flags = jnp.broadcast_to(jnp.stack(flags).astype(f32)[:, None], (8, L))
    meta = jnp.concatenate([offsets[0, 0].reshape(COUNT), counts[0]])
    card = jnp.pad(meta.astype(bf16)[None], ((0, CARD - 1), (0, L - COUNT - 1)))

    sent = [rounded[:, :OVER, j * L : (j + 1) * L].reshape(2 * OVER, L) for j in range(2)]
    below = [shifted(sent[0], -1, 0), shifted(jnp.concatenate([sent[1], card]), -1, 0)]
    right = shifted(rounded[:, :, :OVER], 0, -1)
    below.append(shifted(below[0], 0, -1))
    cards = [card] if two else [card, shifted(card, 1, 0)]

    staged = call(
        stage, "stage", [WIDE, WIDE, PLANES], [None, PLANES, PLANES], 0, 3, 3, held=3
    )(own, dual, probe)
    staged = [pinned(v) for v in staged]
    (amps,) = call(
        reorder, "reorder", [measured], [None, measured, TABLE, measured], 0, 2, 3, held=-1
    )(below[0], amps, order)
    inputs = (own, dual, probe, amps, fwd, bwd)
    more = (len(cards) + 1) * CARD
    sent = [(SPAN, more)] + ([(OVER, more), (TS, 0)] if two else [(SPAN, more)])
    ext, acc, pnum, side, *inner = call(
        functools.partial(first_pass, two), "first_pass",
        [WIDE, WIDE, SUMS] + [((2 * rows + more, L), bf16) for rows, more in sent],
        [TABLE, TABLE, measured, None] + WORK, 1, 3, 3, aliases={6: 0, 7: 1}, flops=PASS,
    )(meta, flags, right, *below, *staged, *cards, fwd, bwd, amps)
    side = swapped(side, "tile", 1)
    inner = [inner_swapped(part) for part in inner]

    rims = call(
        functools.partial(between, two), "between", [((2, OVER, L), bf16)] * (3 if two else 6)
    )(flags, acc, side, inner[0], pnum, right, *below)
    from_above = [shifted(rim, 1, 0) for rim in rims[:3]]
    from_below = from_above if two else [shifted(rim, -1, 0) for rim in rims[3:]]
    weight, *inputs = call(
        functools.partial(weigh, two), "weigh",
        [((3, SPAN, L), f32), PLANES, PLANES, PLANES, measured, TABLE, TABLE],
        [None, ((2, PS, L), f32), ((3, SPAN + 2 * OVER, L), f32), ((24, L), f32),
         pltpu.SMEM((24, L), f32)],
        0, 6, 7, held=7,
    )(*cards, flags, side, inner[0], rims[0], acc, pnum, right, below[0], below[2],
      below[1], *inputs)
    weight, *inputs = [pinned(v) for v in (weight, *inputs)]

    base, shrink, to_right, to_corner, rim, to_below, pnum, to_swap = call(
        functools.partial(second_pass, two), "second_pass",
        [PLANES, ((2, TS, L), f32), ((2, TS, L), bf16), ((2, OVER, L), bf16), ((2, OVER, L), f32),
         ((2, OVER, L), bf16),
         SUMS, ((3, PS // 2, PS), bf16)],
        [PLANES, WIDE, WIDE] + WORK, 1, flops=PASS,
    )(meta, flags, right, *below, acc, side, *inner, *from_above,
      *from_below, weight, pnum, *inputs)
    corner = shifted(to_corner, 0, 1)
    from_left = shifted(to_right, 0, 1)
    above1 = shifted(to_below, 1, 0)
    (to_below,) = call(add_rim, "add_rim", [((2, OVER, L), bf16)])(flags, rim, corner, base, shrink)
    above0 = shifted(to_below, 1, 0)

    eight = n == 8
    half = [((3, PS // 2, PS), bf16)]
    if eight:
        (sums,) = call(halve, "halve", half)(flags, pnum, swapped(to_swap, "tile", 1), base, shrink)
        came = swapped(sums, "tile", 2)
    combined, *parts = call(
        finish_estimate, "finish_estimate", [PLANES] + [((2, TS // 2, TS), bf16)] * 2
    )(flags, base, shrink, from_left, above0, above1, *([sums] if eight else []))
    if eight:
        (sums,) = call(add, "add", half)(sums, came, parts[0])
        came = swapped(sums, "tile", 6)
    pairs = scan_sums(parts)
    if eight:
        (change,) = call(update, "update", [((2, PS // 2, PS), bf16)])(sums, came, pairs[1])
    settled, dual_new = call(
        functools.partial(settle, lax.axis_size("scan")), "settle", [PLANES] * 2
    )(*pairs, combined)
    if eight:
        change = doubled(index, change, 1).astype(f32)
    else:
        total = lax.psum(pnum, "tile")
        change = probe_step * total[0:2] / jnp.sqrt(total[2] + 1.0)
    probe_new = probe + change
    return (settled[None], dual_new[None, None], probe_new[None])


def solution(mesh):
    placed = (
        P("tile", None, None, None),
        P("scan", "tile", None, None, None),
        P("scan", None, None, None),
        P("scan", "tile", None, None, None),
        P("scan", "tile", None, None),
        P("scan", "tile"),
    )
    return jax.shard_map(
        shards,
        mesh=mesh,
        in_specs=placed,
        out_specs=(
            P("tile", None, None, None),
            P("scan", "tile", None, None, None),
            P("scan", None, None, None),
        ),
        check_vma=False,
    )
```

```python
import functools
import math

import jax
import jax.numpy as jnp
import ml_dtypes
import numpy as np
from jax import lax
from jax.experimental import pallas as pl
from jax.experimental.pallas import tpu as pltpu
from jax.sharding import PartitionSpec as P

PS = 256
TS = 256
OVER = 128
TGW = 4
SLOTS = 4
SPAN = TS + OVER
L = 128
HALF = PS // 2
CH = 32
COUNT = 2 * SLOTS
CARD = 16
HAS_LEFT, HAS_RIGHT, HAS_ABOVE, HAS_BELOW, ODD = range(5)

penalty = 0.5
smoothing = 0.05
probe_step = 3.0

f32 = jnp.float32
bf16 = jnp.bfloat16


def dft_tables():
    indices = np.arange(PS, dtype=np.int32)
    phase_index = indices[:, None] * indices[None, :] % PS
    angles = phase_index.astype(np.float32) * np.float32(2.0 * math.pi / PS)
    scale = np.float32(1.0 / math.sqrt(PS))
    re = (np.cos(angles) * scale).astype(ml_dtypes.bfloat16)
    im = (-np.sin(angles) * scale).astype(ml_dtypes.bfloat16)
    half = np.concatenate([re[:HALF], re[HALF : HALF + 1], im[1:HALF]])
    order = np.concatenate([indices[: HALF + 1], indices[:HALF:-1]])
    return jnp.asarray(half), jnp.asarray(half.T), jnp.asarray(np.eye(PS, dtype=half.dtype)[order])


def shifted(value, rows, cols):
    height = lax.axis_size("tile") // TGW
    pairs = []
    for i in range(height * TGW):
        r, c = divmod(i, TGW)
        pairs.append((i, (r + rows) % height * TGW + (c + cols) % TGW))
    return lax.ppermute(value, "tile", pairs)


def swapped(value, axis, bit):
    n = lax.axis_size(axis)
    return lax.ppermute(value, axis, [(i, i ^ bit) for i in range(n)])


def is_power(n):
    return n & (n - 1) == 0


def inner_swapped(value):
    n = lax.axis_size("tile")
    return lax.ppermute(value, "tile", [(i, i ^ 3 if i % TGW in (1, 2) else i) for i in range(n)])


def scan_sums(parts):
    n = lax.axis_size("scan")
    if not is_power(n):
        return [v for part in parts for v in (lax.psum(part, "scan"), jnp.zeros_like(part))]
    bits = [1 << k for k in range(n.bit_length() - 1)]
    for k in range(len(bits)):
        came = [swapped(parts[p], "scan", bits[(k + p) % len(bits)]) for p in range(2)]
        pairs = [parts[0], came[0], parts[1], came[1]]
        if k < len(bits) - 1:
            outs = [(parts[0].shape, bf16)] * 2
            parts = call(mix, f"mix{k}", outs)(*pairs)
    return pairs


def doubled(index, change, bit):
    other = swapped(change, "tile", bit)
    return jnp.where(
        (index // bit) % 2 == 1,
        jnp.concatenate([other, change], 1),
        jnp.concatenate([change, other], 1),
    )


def lane_pull(blocks, c):
    lane = lax.broadcasted_iota(jnp.int32, blocks[0].shape, 1)
    keep = lane < L - c
    r = [pltpu.roll(v, (L - c) % L, 1) for v in blocks]
    return jnp.concatenate([jnp.where(keep, r[0], r[1]), jnp.where(keep, r[1], r[2])], 1)


def lane_push(blocks, c):
    lane = lax.broadcasted_iota(jnp.int32, blocks[0].shape, 1)
    past = lane >= c
    r = [pltpu.roll(v, c % L, 1) for v in blocks]
    z = jnp.zeros_like(r[0])
    return [jnp.where(past, r[0], z), jnp.where(past, r[1], r[0]), jnp.where(past, z, r[1])]


def split(pr, pi, qr, qi, first):
    planes = (pr - qi, pr + qi, pi + qr, pi - qr)
    if first is None:
        return planes
    return [jnp.where(first, v, w) for v, w in zip((pr, qr, pi, qi), planes)]


def joined(lr, hr, li, hi, first):
    planes = (lr + hr, li - hi, li + hi, hr - lr)
    if first is None:
        return planes
    return [jnp.where(first, v, w) for v, w in zip((lr, hr, li, hi), planes)]


def visit_pair(p, meta, ext, probe, amps, half, turned, acc, pnum, win, X, Y, W):
    N = PS
    used = jnp.where(2 * p + 1 < meta[COUNT], 1.0, 0.0).astype(f32)
    corners = [(meta[4 * p + 2 * i], meta[4 * p + 2 * i + 1]) for i in range(2)]

    def leave(i):
        r, c = corners[i]
        for k in range(0, N, CH):
            rows = slice(k, k + CH)
            w = [
                lane_pull([ext[ch, j, pl.ds(r + k, CH), :] for j in range(3)], c) for ch in range(2)
            ]
            if i == 1:
                w = [v * used for v in w]
            pr, pi = probe[0, rows, :], probe[1, rows, :]
            win[i, 0, rows, :] = w[0]
            win[i, 1, rows, :] = w[1]
            X[i, rows, :N] = (pr * w[0] - pi * w[1]).astype(bf16)
            X[i, rows, N:] = (pr * w[1] + pi * w[0]).astype(bf16)
            pnum[2, rows, :] += w[0] * w[0] + w[1] * w[1]

    def columns(i):
        t = jnp.dot(half[...], X[i], preferred_element_type=f32)
        for k in range(0, HALF, CH):
            p, q = t[k : k + CH], t[HALF + k : HALF + k + CH]
            first = lax.broadcasted_iota(jnp.int32, (CH, N), 0) == 0 if k == 0 else None
            planes = split(p[:, :N], p[:, N:], q[:, :N], q[:, N:], first)
            for j, v in enumerate(planes):
                Y[i, j * HALF + k : j * HALF + k + CH, :] = v.astype(bf16)

    def rows_of(i):
        W[i] = jnp.dot(Y[i], turned[...], preferred_element_type=f32)

    def compare(i):
        first = lax.broadcasted_iota(jnp.int32, (CH, L), 1) == 0
        top = lax.broadcasted_iota(jnp.int32, (CH, N), 0) == 0
        for k in range(0, HALF, CH):
            resid = []
            for h in range(2):
                rows = slice(h * HALF + k, h * HALF + k + CH)
                at = slice(N + h * HALF + k, N + h * HALF + k + CH)
                planes = split(W[i, rows, :L], W[i, at, :L], W[i, rows, L:], W[i, at, L:], first)
                a = amps[2 * p + i, rows, :].astype(f32)
                wr = jnp.concatenate([planes[0], planes[1]], 1)
                wi = jnp.concatenate([planes[2], planes[3]], 1)
                f = a * lax.rsqrt(wr * wr + wi * wi + smoothing) - 1.0
                resid.append((wr * f, wi * f))
            (lr, li), (hr, hi) = resid
            for j, v in enumerate(joined(lr, hr, li, hi, top if k == 0 else None)):
                X[i, j % 2 * HALF + k : j % 2 * HALF + k + CH, j // 2 * N : j // 2 * N + N] = v.astype(bf16)

    def columns_back(i):
        t = jnp.dot(turned[...], X[i], preferred_element_type=f32)
        first = lax.broadcasted_iota(jnp.int32, (CH, L), 1) == 0
        for k in range(0, N, CH):
            v = t[k : k + CH]
            planes = joined(v[:, :L], v[:, L:N], v[:, N : N + L], v[:, N + L :], first)
            for j, v in enumerate(planes):
                at = j // 2 * N + k
                Y[i, at : at + CH, j % 2 * L : j % 2 * L + L] = v.astype(bf16)

    def rows_back(i):
        W[i] = jnp.dot(Y[i], half[...], preferred_element_type=f32)

    def gather(i):
        r, c = corners[i]
        for k in range(0, N, CH):
            rows = slice(k, k + CH)
            br, bi = W[i, rows, :], W[i, N + k : N + k + CH, :]
            pr, pi = probe[0, rows, :], probe[1, rows, :]
            wr, wi = win[i, 0, rows, :], win[i, 1, rows, :]
            pnum[0, rows, :] += wr * br + wi * bi
            pnum[1, rows, :] += wr * bi - wi * br
            for ch, v in enumerate((pr * br + pi * bi, pr * bi - pi * br)):
                for j, u in enumerate(lane_push([v[:, :L], v[:, L:]], c)):
                    acc[ch, j, pl.ds(r + k, CH), :] += u

    leave(0)
    columns(0)
    leave(1)
    rows_of(0)
    columns(1)
    compare(0)
    rows_of(1)
    columns_back(0)
    compare(1)
    rows_back(0)
    columns_back(1)
    gather(0)
    rows_back(1)
    gather(1)


def fetch(pairs, sems):
    copies = [pltpu.make_async_copy(src, dst, sems.at[i]) for i, (src, dst) in enumerate(pairs)]
    for copy in copies:
        copy.start()
    return copies


def stage(own_h, dual_h, probe_h, ext, acc, probe, sems, own, dual):
    copies = fetch([(own_h, own), (dual_h, dual), (probe_h, probe)], sems)
    acc[:, 2] = jnp.zeros((2, SPAN, L), f32)
    copies[0].wait()
    for j in range(2):
        cols = slice(j * L, (j + 1) * L)
        acc[:, j, TS:, :] = jnp.zeros((2, OVER, L), f32)
        ext[:, j, :TS, :] = own[:, :, cols].astype(bf16).astype(f32)
    copies[1].wait()
    for j in range(2):
        cols = slice(j * L, (j + 1) * L)
        acc[:, j, :TS, :] = -penalty * dual[:, :, cols]
    copies[2].wait()


def reorder(below, amps_h, order_h, ordered_h, sems, amps, order, ordered):
    copies = fetch([(order_h, order), (amps_h, amps)], sems)
    for copy in copies:
        copy.wait()
    for k in range(SLOTS):
        rows = jnp.dot(order[...], amps[k], preferred_element_type=f32).astype(bf16)
        ordered[k] = jnp.dot(rows, order[...], preferred_element_type=f32).astype(bf16)
    back = pltpu.make_async_copy(ordered, ordered_h, sems.at[2])
    back.start()
    back.wait()


def first_pass(
    two, meta, flags, right, below0, below1, diag, ext0, acc0, probe, *rest,
):
    *cards, fwd_h, bwd_h, amps_h = rest[: 4 if two else 5]
    ext, acc, pnum, side, *inner, fwd, bwd, amps, sems, win, X, Y, W = rest[4 if two else 5 :]
    copies = fetch([(fwd_h, fwd), (bwd_h, bwd), (amps_h, amps)], sems)
    has_right = flags[HAS_RIGHT : HAS_RIGHT + 1, :]
    has_below = flags[HAS_BELOW : HAS_BELOW + 1, :]
    ext[:, 2, :TS, :] = right[...].astype(f32) * has_right
    for ch in range(2):
        ext[ch, 2, TS:, :] = diag[plane(ch, OVER), :].astype(f32) * (has_right * has_below)
    for j in range(2):
        for ch in range(2):
            ext[ch, j, TS:, :] = (below0, below1)[j][plane(ch, OVER), :].astype(f32) * has_below
    pnum[...] = jnp.zeros_like(pnum)
    for copy in copies:
        copy.wait()

    @pl.loop(0, (meta[COUNT] + 1) // 2)
    def _(p):
        visit_pair(p, meta, ext, probe, amps, fwd, bwd, acc, pnum, win, X, Y, W)

    odd = flags[ODD : ODD + 1, :] > 0.0
    column = [card[...] for card in cards] + [below1[2 * OVER :, :]]
    side[2 * SPAN :, :] = jnp.concatenate(column, 0)
    inner[0][2 * (OVER if two else SPAN) :, :] = jnp.concatenate(column, 0)
    if two:
        inner[1][2 * TS :, :] = cards[0][...]
    for ch in range(2):
        side[plane(ch, SPAN), :] = jnp.where(odd, acc[ch, 0], acc[ch, 2]).astype(bf16)
        other = [jnp.where(odd, acc[ch, 2, rows, :], acc[ch, 0, rows, :]) for rows in BANDS]
        for part, values in zip(inner, parted(two, flags, other)):
            rows = values.shape[0]
            part[plane(ch, rows), :] = values.astype(bf16)


def plane(ch, rows, start=0, count=None):
    return slice(ch * rows + start, ch * rows + start + (rows if count is None else count))


def parted(two, flags, bands):
    if not two:
        return [jnp.concatenate(bands, 0)]
    lower = flags[HAS_BELOW : HAS_BELOW + 1, :] > 0.0
    rest = [jnp.where(lower, bands[k], bands[k + 1]) for k in range(2)]
    return [jnp.where(lower, bands[2], bands[0]), jnp.concatenate(rest, 0)]


def from_inner(two, flags, inner, ch, start, count):
    if not two:
        return inner[0][plane(ch, SPAN, start, count), :]
    band, at = divmod(start, OVER)
    lower = flags[HAS_BELOW : HAS_BELOW + 1, :] > 0.0
    rim = inner[0][plane(ch, OVER, at, count), :]
    first, second = [inner[1][plane(ch, TS, k * OVER + at, count), :] for k in range(2)]
    on_top = (first, second, rim)[band].astype(f32)
    return jnp.where(lower, on_top, (rim, first, second)[band].astype(f32))


def rims_of(two, flags, get):
    down, up = get(slice(TS, SPAN)), get(slice(0, OVER))
    return [jnp.where(flags[HAS_BELOW : HAS_BELOW + 1, :] > 0.0, down, up)] if two else [down, up]


def from_sides(flags, side, inner):
    odd = flags[ODD : ODD + 1, :] > 0.0
    valid = flags[HAS_LEFT : HAS_LEFT + 1, :] * flags[HAS_RIGHT : HAS_RIGHT + 1, :]
    side, inner = side.astype(f32), inner.astype(f32) * valid
    return jnp.where(odd, side, inner), jnp.where(odd, inner, side)


def between(two, flags, acc, side, inner, *rest):
    outs = rest[-2:] if two else rest[-4:]
    for ch in range(2):
        for j in range(3):
            rims = rims_of(two, flags, lambda rows: acc[ch, j, rows, :])
            if j != 1:
                sides = rims_of(
                    two, flags, lambda rows: side[plane(ch, SPAN, rows.start, OVER), :].astype(f32)
                )
                size = OVER if two else SPAN
                starts = [0] if two else [TS, 0]
                for k, start in enumerate(starts):
                    other = inner[plane(ch, size, start, OVER), :]
                    rims[k] = rims[k] + from_sides(flags, sides[k], other)[j // 2]
            for k, rim in enumerate(rims):
                if j < 2:
                    outs[2 * k][ch, j] = rim.astype(bf16)
                else:
                    outs[2 * k + 1][ch] = rim.astype(bf16)


def weigh(two, *rest):
    *cards, flags, side, inner = rest[: 4 if two else 5]
    below1, *sources = rest[-19:-12]
    weight, *targets, sems, p2, buf, held, table = rest[-12:]
    copies = fetch(list(zip(sources, targets)), sems)
    probe = targets[2]
    last = 2 * OVER
    blocks = [card[...].astype(f32) for card in cards] + [below1[last:, :].astype(f32)]
    for k, block in enumerate(blocks):
        held[k : k + 1, :] = block[:1]
        ends = [2 * SPAN + k * CARD, 2 * (OVER if two else SPAN) + k * CARD]
        odd = flags[ODD : ODD + 1, :] > 0.0
        by_side, by_inner = [
            v[at : at + CARD, :].astype(f32)[:1] for v, at in zip((side, inner), ends)
        ]
        held[4 + k : 5 + k, :] = jnp.where(odd, by_side, by_inner)
        held[8 + k : 9 + k, :] = jnp.where(odd, by_inner, by_side)
    held[16:24, :] = flags[...]
    moved = pltpu.make_async_copy(held, table, sems.at[6])
    moved.start()
    buf[...] = jnp.zeros_like(buf)
    copies[2].wait()
    for j in range(2):
        cols = slice(j * L, (j + 1) * L)
        p2[j] = probe[0, :, cols] * probe[0, :, cols] + probe[1, :, cols] * probe[1, :, cols]
    moved.wait()
    for dr in (-1, 0, 1):
        for dc in (-1, 0, 1):
            at_row = {0: 0, -1: 4, 1: 8}[dc] + {0: 0, -1: 1, 1: 1 if two else 2}[dr]
            first, rows = {-1: (OVER, OVER), 0: (0, PS), 1: (0, OVER)}[dr]
            base = {-1: 0, 0: OVER, 1: OVER + TS}[dr]
            count = table[at_row, COUNT].astype(jnp.int32)
            for flag, at, step in (
                (HAS_ABOVE, -1, dr), (HAS_BELOW, 1, dr), (HAS_LEFT, -1, dc), (HAS_RIGHT, 1, dc)
            ):
                if step == at:
                    count = jnp.where(table[16 + flag, 0] > 0.0, count, 0)

            @pl.loop(0, count)
            def _(s, at_row=at_row, dc=dc, first=first, rows=rows, base=base):
                r, c = [table[at_row, 2 * s + i].astype(jnp.int32) for i in range(2)]
                for k in range(0, rows, 64):
                    at = pl.ds(base + r + k, 64)
                    v = [p2[j, first + k : first + k + 64, :] for j in range(2)]
                    lane = lax.broadcasted_iota(jnp.int32, v[0].shape, 1)
                    if dc == 0:
                        for j, u in enumerate(lane_push(v, c)):
                            buf[j, at, :] += u
                    elif dc < 0:
                        buf[0, at, :] += jnp.where(lane < c, pltpu.roll(v[1], c % L, 1), 0.0)
                    else:
                        buf[2, at, :] += jnp.where(lane >= c, pltpu.roll(v[0], c % L, 1), 0.0)

    weight[...] = buf[:, OVER : OVER + SPAN, :]
    for k, copy in enumerate(copies):
        if k != 2:
            copy.wait()


def second_pass(
    two, meta, flags, right, below0, below1, diag, acc1, side, *rest,
):
    inner, rest = rest[: 2 if two else 1], rest[2 if two else 1 :]
    from_above, from_below, rest = rest[:2], rest[2:4], rest[4:]
    weight, pnum1, own, dual, probe, amps, fwd, bwd = rest[:8]
    base, shrink, to_right, to_corner, lower, to_below, pnum, to_swap = rest[8:16]
    partial, ext, acc, win, X, Y, W = rest[16:]
    has_right = flags[HAS_RIGHT : HAS_RIGHT + 1, :]
    has_below = flags[HAS_BELOW : HAS_BELOW + 1, :]
    has_above = flags[HAS_ABOVE : HAS_ABOVE + 1, :]
    acc[...] = jnp.zeros_like(acc)
    pnum[...] = pnum1[...]
    for ch in range(2):
        for j in range(3):
            cols = slice(j * L, (j + 1) * L)
            for k in range(0, SPAN, 64):
                rows = slice(k, k + 64)
                total = acc1[ch, j, rows, :]
                if j != 1:
                    at = plane(ch, SPAN, k, 64)
                    total = total + from_sides(
                        flags, side[at, :], from_inner(two, flags, inner, ch, k, 64)
                    )[j // 2]
                if k < OVER:
                    came = from_above[0][ch, j, rows, :] if j < 2 else from_above[1][ch, rows, :]
                    total = total + came.astype(f32) * has_above
                if k >= TS:
                    rim = slice(k - TS, k - TS + 64)
                    came = from_below[0][ch, j, rim, :] if j < 2 else from_below[1][ch, rim, :]
                    total = total + came.astype(f32)
                step = total / (weight[j, rows, :] + penalty)
                if j < 2 and k < TS:
                    est = own[ch, rows, cols] + step
                    partial[ch, rows, cols] = est
                else:
                    if k < TS:
                        est = right[ch, rows, :].astype(f32) + step
                    elif j < 2:
                        est = (below0, below1)[j][plane(ch, OVER, k - TS, 64), :].astype(f32) + step
                    else:
                        est = diag[plane(ch, OVER, k - TS, 64), :].astype(f32) + step
                    if j == 2:
                        est = est * has_right
                    if k >= TS:
                        est = est * has_below
                ext[ch, j, rows, :] = est.astype(bf16).astype(f32)

    @pl.loop(0, (meta[COUNT] + 1) // 2)
    def _(p):
        visit_pair(p, meta, ext, probe, amps, fwd, bwd, acc, pnum, win, X, Y, W)

    to_corner[...] = acc[:, 2, TS:, :].astype(bf16)
    to_right[...] = acc[:, 2, :TS, :].astype(bf16)
    to_below[...] = acc[:, 1, TS:, :].astype(bf16)
    lower[...] = acc[:, 0, TS:, :]
    odd = flags[ODD : ODD + 1, :1] > 0.0
    for ch in range(3):
        lo, hi = pnum[ch, : PS // 2, :], pnum[ch, PS // 2 :, :]
        to_swap[ch] = jnp.where(odd, lo, hi).astype(bf16)
    for j in range(2):
        cols = slice(j * L, (j + 1) * L)
        for k in range(0, TS, 64):
            rows = slice(k, k + 64)
            over = 1.0 / (weight[j, rows, :] + penalty)
            shrink[j, rows, :] = over
            for ch in range(2):
                est = partial[ch, rows, cols]
                held = dual[ch, rows, cols]
                pull = penalty * (own[ch, rows, cols] - held - est)
                base[ch, rows, cols] = est + held + (acc[ch, j, rows, :] + pull) * over


def halve(flags, sums, came, *rest):
    odd = flags[ODD : ODD + 1, :1] > 0.0
    for ch in range(3):
        lo, hi = sums[ch, : PS // 2, :], sums[ch, PS // 2 :, :]
        rest[-1][ch] = (jnp.where(odd, hi, lo) + came[ch].astype(f32)).astype(bf16)


def add(held, came, *rest):
    for ch in range(3):
        rest[-1][ch] = (held[ch].astype(f32) + came[ch].astype(f32)).astype(bf16)


def add_rim(flags, rim, from_left, *rest):
    has_left = flags[HAS_LEFT : HAS_LEFT + 1, :]
    for ch in range(2):
        rest[-1][ch] = (rim[ch] + from_left[ch].astype(f32) * has_left).astype(bf16)


def finish_estimate(flags, base, shrink, from_left, above0, above1, *rest):
    combined, parts = rest[-3], rest[-2:]
    has_left = flags[HAS_LEFT : HAS_LEFT + 1, :]
    has_above = flags[HAS_ABOVE : HAS_ABOVE + 1, :]
    for ch in range(2):
        for j in range(2):
            cols = slice(j * L, (j + 1) * L)
            for k in range(0, TS, 64):
                rows = slice(k, k + 64)
                total = base[ch, rows, cols]
                came = None
                if j == 0:
                    came = from_left[ch, rows, :].astype(f32) * has_left
                if k < OVER:
                    above = (above0, above1)[j][ch, rows, :].astype(f32) * has_above
                    came = above if came is None else came + above
                if came is not None:
                    total = total + came * shrink[j, rows, :]
                combined[ch, rows, cols] = total
                part = slice(k % (TS // 2), k % (TS // 2) + 64)
                parts[k // (TS // 2)][ch, part, cols] = total.astype(bf16)


def mixed(first, first_came, second, second_came, outs):
    for out, part, came in ((outs[0], first, first_came), (outs[1], second, second_came)):
        for ch in range(2):
            out[ch] = (part[ch].astype(f32) + came[ch].astype(f32)).astype(bf16)


def mix(*refs):
    mixed(*refs[:4], refs[-2:])


def update(held, came, *rest):
    total = [held[ch].astype(f32) + came[ch].astype(f32) for ch in range(3)]
    over = probe_step * lax.rsqrt(total[2] + 1.0)
    for ch in range(2):
        rest[-1][ch] = (total[ch] * over).astype(bf16)


def settle(groups, first, first_came, second, second_came, combined, *rest):
    settled, dual_new = rest[-2:]
    for k in range(0, TS, CH):
        rows = slice(k, k + CH)
        part, came = (first, first_came) if k < TS // 2 else (second, second_came)
        at = slice(k % (TS // 2), k % (TS // 2) + CH)
        re, im = [
            (part[ch, at, :].astype(f32) + came[ch, at, :].astype(f32)) * (1.0 / groups)
            for ch in range(2)
        ]
        over = 1.0 / jnp.maximum(jnp.sqrt(re * re + im * im), 1.0)
        re, im = re * over, im * over
        settled[0, rows, :] = re
        settled[1, rows, :] = im
        dual_new[0, rows, :] = combined[0, rows, :] - re
        dual_new[1, rows, :] = combined[1, rows, :] - im


BANDS = [slice(k, k + OVER) for k in range(0, SPAN, OVER)]
V = pl.BlockSpec(memory_space=pltpu.VMEM)
S = pl.BlockSpec(memory_space=pltpu.SMEM)
H = pl.BlockSpec(memory_space=pltpu.HBM)


def pinned(value):
    return pltpu.with_memory_space_constraint(value, pltpu.VMEM)


def call(body, name, outs, scratch=(), scalars=0, far=0, copies=0, aliases=None, held=0, flops=0):
    def run(*operands):
        near = len(operands) - scalars - far
        place = pltpu.HBM if held < 0 else pltpu.VMEM
        spaces = [None] * (scalars + near) + [pltpu.HBM] * far
        operands = [
            v if space is None else pltpu.with_memory_space_constraint(v, space)
            for v, space in zip(operands, spaces)
        ]
        return pl.pallas_call(
            body,
            in_specs=[S] * scalars + [V] * near + [H] * far,
            out_specs=[H if held < 0 else V] * len(outs),
            out_shape=[
                place(shape, dtype) if k < abs(held) else jax.ShapeDtypeStruct(shape, dtype)
                for k, (shape, dtype) in enumerate(outs)
            ],
            scratch_shapes=[
                pltpu.SemaphoreType.DMA((copies,)) if one is None else pltpu.VMEM(*one)
                if isinstance(one, tuple) else one
                for one in scratch
            ],
            input_output_aliases=aliases or {},
            cost_estimate=pl.CostEstimate(
                flops=flops or sum(math.prod(shape) for shape, _ in outs),
                bytes_accessed=sum(v.size * v.dtype.itemsize for v in operands[scalars + near :]),
                transcendentals=0,
            ),
            compiler_params=pltpu.CompilerParams(vmem_limit_bytes=24 * 2**20),
            name=name,
        )(*operands)

    return run


PLANES = ((2, PS, PS), f32)
PASS = SLOTS * 4 * 4 * PS**3
WORK = [
    ((2, 2, PS, PS), f32),
    ((2, PS, 2 * PS), bf16),
    ((2, 2 * PS, PS), bf16),
    ((2, 2 * PS, PS), f32),
]
TABLE = ((PS, PS), bf16)
WIDE = ((2, 3, SPAN, L), f32)
SUMS = ((3, PS, PS), f32)


def shards(consensus, duals, probes, amplitudes, offsets, counts):
    fwd, bwd, order = dft_tables()
    n = lax.axis_size("tile")
    index = lax.axis_index("tile")
    own = consensus[0]
    dual = duals[0, 0]
    probe = probes[0]
    amps = amplitudes[0, 0]
    measured = ((SLOTS, PS, PS), bf16)

    rounded = own.astype(bf16)
    height = n // TGW
    two = height == 2
    row, col = index // TGW, index % TGW
    flags = [col > 0, col < TGW - 1, row > 0, row < height - 1]
    flags = flags + [index % 2 == 1] + [col < 0] * 3
    flags = jnp.broadcast_to(jnp.stack(flags).astype(f32)[:, None], (8, L))
    meta = jnp.concatenate([offsets[0, 0].reshape(COUNT), counts[0]])
    card = jnp.pad(meta.astype(bf16)[None], ((0, CARD - 1), (0, L - COUNT - 1)))

    sent = [rounded[:, :OVER, j * L : (j + 1) * L].reshape(2 * OVER, L) for j in range(2)]
    below = [shifted(sent[0], -1, 0), shifted(jnp.concatenate([sent[1], card]), -1, 0)]
    right = shifted(rounded[:, :, :OVER], 0, -1)
    below.append(shifted(below[0], 0, -1))
    cards = [card] if two else [card, shifted(card, 1, 0)]

    staged = call(
        stage, "stage", [WIDE, WIDE, PLANES], [None, PLANES, PLANES], 0, 3, 3, held=3
    )(own, dual, probe)
    staged = [pinned(v) for v in staged]
    (amps,) = call(
        reorder, "reorder", [measured], [None, measured, TABLE, measured], 0, 2, 3, held=-1
    )(below[0], amps, order)
    inputs = (own, dual, probe, amps, fwd, bwd)
    more = (len(cards) + 1) * CARD
    sent = [(SPAN, more)] + ([(OVER, more), (TS, CARD)] if two else [(SPAN, more)])
    ext, acc, pnum, side, *inner = call(
        functools.partial(first_pass, two), "first_pass",
        [WIDE, WIDE, SUMS] + [((2 * rows + more, L), bf16) for rows, more in sent],
        [TABLE, TABLE, measured, None] + WORK, 1, 3, 3, aliases={6: 0, 7: 1}, flops=PASS,
    )(meta, flags, right, *below, *staged, *cards, fwd, bwd, amps)
    side = swapped(side, "tile", 1)
    inner = [inner_swapped(part) for part in inner]

    rims = call(
        functools.partial(between, two), "between", [((2, 2, OVER, L), bf16), ((2, OVER, L), bf16)] * (1 if two else 2)
    )(flags, acc, side, inner[0], pnum, right, *below)
    from_above = [shifted(rim, 1, 0) for rim in rims[:2]]
    from_below = from_above if two else [shifted(rim, -1, 0) for rim in rims[2:]]
    weight, *inputs = call(
        functools.partial(weigh, two), "weigh",
        [((3, SPAN, L), f32), PLANES, PLANES, PLANES, measured, TABLE, TABLE],
        [None, ((2, PS, L), f32), ((3, SPAN + 2 * OVER, L), f32), ((24, L), f32),
         pltpu.SMEM((24, L), f32)],
        0, 6, 7, held=7,
    )(*cards, flags, side, inner[0], rims[0], acc, pnum, right, below[0], below[2],
      below[1], *inputs)
    weight, *inputs = [pinned(v) for v in (weight, *inputs)]

    base, shrink, to_right, to_corner, rim, to_below, pnum, to_swap = call(
        functools.partial(second_pass, two), "second_pass",
        [PLANES, ((2, TS, L), f32), ((2, TS, L), bf16), ((2, OVER, L), bf16), ((2, OVER, L), f32),
         ((2, OVER, L), bf16),
         SUMS, ((3, PS // 2, PS), bf16)],
        [PLANES, WIDE, WIDE] + WORK, 1, flops=PASS,
    )(meta, flags, right, *below, acc, side, *inner, *from_above,
      *from_below, weight, pnum, *inputs)
    corner = shifted(to_corner, 0, 1)
    from_left = shifted(to_right, 0, 1)
    above1 = shifted(to_below, 1, 0)
    (to_below,) = call(add_rim, "add_rim", [((2, OVER, L), bf16)])(flags, rim, corner, base, shrink)
    above0 = shifted(to_below, 1, 0)

    eight = n == 8
    half = [((3, PS // 2, PS), bf16)]
    if eight:
        (sums,) = call(halve, "halve", half)(flags, pnum, swapped(to_swap, "tile", 1), base, shrink)
        came = swapped(sums, "tile", 2)
    combined, *parts = call(
        finish_estimate, "finish_estimate", [PLANES] + [((2, TS // 2, TS), bf16)] * 2
    )(flags, base, shrink, from_left, above0, above1, *([sums] if eight else []))
    if eight:
        (sums,) = call(add, "add", half)(sums, came, parts[0])
        came = swapped(sums, "tile", 6)
    pairs = scan_sums(parts)
    if eight:
        (change,) = call(update, "update", [((2, PS // 2, PS), bf16)])(sums, came, pairs[1])
    settled, dual_new = call(
        functools.partial(settle, lax.axis_size("scan")), "settle", [PLANES] * 2
    )(*pairs, combined)
    if eight:
        change = doubled(index, change, 1).astype(f32)
    else:
        total = lax.psum(pnum, "tile")
        change = probe_step * total[0:2] / jnp.sqrt(total[2] + 1.0)
    probe_new = probe + change
    return (settled[None], dual_new[None, None], probe_new[None])


def solution(mesh):
    placed = (
        P("tile", None, None, None),
        P("scan", "tile", None, None, None),
        P("scan", None, None, None),
        P("scan", "tile", None, None, None),
        P("scan", "tile", None, None),
        P("scan", "tile"),
    )
    return jax.shard_map(
        shards,
        mesh=mesh,
        in_specs=placed,
        out_specs=(
            P("tile", None, None, None),
            P("scan", "tile", None, None, None),
            P("scan", None, None, None),
        ),
        check_vma=False,
    )
```
